128 devices in a mesh: rows: 8 (over y_hi, z), cols: 16 (over x, y_lo, core).
Axes of the slice: x: 4, y: 4 (y_hi: 2, y_lo: 2; y = y_hi * 2 + y_lo), z: 4, core: 2. Of those that a mesh axis runs over, the one named last changes fastest.
Arguments:
- tokens: bfloat16 [128, 256, 768], P('rows', 'cols'), may hold values from -6 to 6
- cotangent: bfloat16 [128, 256, 768], P('rows', 'cols'), may hold values from -6 to 6
- gain_attn: float32 [768], replicated, may hold values from 0.1 to 1.9
- gain_mlp: float32 [768], replicated, may hold values from 0.1 to 1.9
- weight_qkv: bfloat16 [768, 2304], replicated, may hold values from -0.21875 to 0.21875
- weight_out: bfloat16 [768, 768], replicated, may hold values from -0.21875 to 0.21875
- weight_up: bfloat16 [768, 3072], replicated, may hold values from -0.21875 to 0.21875
- weight_down: bfloat16 [3072, 768], replicated, may hold values from -0.109375 to 0.109375
- left_qkv: float32 [128, 96, 96], P(('rows', 'cols')), may hold values from -0.3125 to 0.3125
- right_qkv: float32 [128, 144, 144], P(('rows', 'cols')), may hold values from -0.3125 to 0.3125
- left_up: float32 [128, 96, 96], P(('rows', 'cols')), may hold values from -0.3125 to 0.3125
- right_up: float32 [128, 192, 192], P(('rows', 'cols')), may hold values from -0.3125 to 0.3125
- left_down: float32 [128, 192, 192], P(('rows', 'cols')), may hold values from -0.3125 to 0.3125
- right_down: float32 [128, 96, 96], P(('rows', 'cols')), may hold values from -0.3125 to 0.3125
Outputs:
- mixed: bfloat16 [128, 256, 768], P('rows', 'cols')
- d_tokens: bfloat16 [128, 256, 768], P('rows', 'cols')
- new_left_qkv: float32 [128, 96, 96], P(('rows', 'cols'))
- new_right_qkv: float32 [128, 144, 144], P(('rows', 'cols'))
- new_left_up: float32 [128, 96, 96], P(('rows', 'cols'))
- new_right_up: float32 [128, 192, 192], P(('rows', 'cols'))
- new_left_down: float32 [128, 192, 192], P(('rows', 'cols'))
- new_right_down: float32 [128, 96, 96], P(('rows', 'cols'))
The draws below stay inside these ranges and needn't reach their ends.
All inputs are finite; a program needn't handle non-finite values.
Results may differ from the reference program's by a relative error of at most 0.018.
Values may be sent and summed in bfloat16 or wider, within the bound.
A program may use at most 192 MiB of HBM per device.

```python
import jax
import jax.numpy as jnp
from jax import lax

D = 768
HEADS = 12
FF = 3072
TH = 16
TW = 16
NBLK = 128
BR = 96
BQ = 144
BM = 192
HT = 128
WT = 256
N_ROWS = 8
N_COLS = 16


def levels(key, extent, pieces, least, high):
    level, own = 1.0, jax.random.fold_in(key, 6)
    for axis_at, parts in pieces:
        heights = jnp.exp(jax.random.uniform(jax.random.fold_in(own, axis_at), (parts,), jnp.float32, least / len(pieces), high / len(pieces)))
        level = level * jnp.repeat(heights, extent[axis_at] // parts).reshape([-1 if axis == axis_at else 1 for axis in range(len(extent))])
    return level


def normal_values(key, shape, deviation, most, split=(), kind=jnp.bfloat16):
    factor_of = levels(key, shape, split, -0.22, 0.18) if split else 1.0
    drawn = jax.random.normal(key, shape, jnp.float32) * deviation * factor_of
    return jnp.minimum(jnp.maximum(drawn, -most), most).astype(kind)


def setup_inputs(seed: int = 0) -> dict:
    key_of = jax.random.split(jax.random.key(seed), 15)
    return {
        "tokens": normal_values(key_of[0], (HT, WT, D), 1.0, 6.0, ((0, 8), (1, 16))),
        "cotangent": normal_values(key_of[1], (HT, WT, D), 1.0, 6.0, ((0, 8), (1, 16))),
        "gain_attn": jnp.clip(1.0 + 0.18 * jax.random.normal(key_of[2], (D,), jnp.float32), 0.1, 1.9),
        "gain_mlp": jnp.clip(1.0 + 0.18 * jax.random.normal(key_of[3], (D,), jnp.float32), 0.1, 1.9),
        "weight_qkv": normal_values(key_of[4], (D, 3 * D), D ** -0.5, 0.21875),
        "weight_out": normal_values(key_of[5], (D, D), D ** -0.5, 0.21875),
        "weight_up": normal_values(key_of[6], (D, FF), D ** -0.5, 0.21875),
        "weight_down": normal_values(key_of[7], (FF, D), FF ** -0.5, 0.109375),
        "left_qkv": normal_values(key_of[8], (NBLK, BR, BR), 0.02, 0.3125, ((0, 128),), jnp.float32),
        "right_qkv": normal_values(key_of[9], (NBLK, BQ, BQ), 0.02, 0.3125, ((0, 128),), jnp.float32),
        "left_up": normal_values(key_of[10], (NBLK, BR, BR), 0.02, 0.3125, ((0, 128),), jnp.float32),
        "right_up": normal_values(key_of[11], (NBLK, BM, BM), 0.02, 0.3125, ((0, 128),), jnp.float32),
        "left_down": normal_values(key_of[12], (NBLK, BM, BM), 0.02, 0.3125, ((0, 128),), jnp.float32),
        "right_down": normal_values(key_of[13], (NBLK, BR, BR), 0.02, 0.3125, ((0, 128),), jnp.float32),
    }


epsilon = 1e-06
window_half = 6
window_span = 13
group_rows = 8

def normed(inputs, gain):
    return inputs * lax.rsqrt(lax.optimization_barrier(jnp.mean(inputs * inputs, axis=-1, keepdims=True)) + epsilon) * gain

def norm_grad(inputs, gain, upstream):
    return jax.vjp(lambda column: normed(column, gain), inputs)[1](upstream)[0]

def gelu_tanh(inputs):
    return jax.nn.gelu(inputs, approximate=True)

def product(formula, left_side, right_side):
    return jnp.einsum(formula, left_side.astype(jnp.float32), right_side.astype(jnp.float32))

def window_mask(query_rows, query_cols, key_rows, key_cols, image_rows, image_cols):
    row_first = jnp.clip(query_rows - window_half, 0, image_rows - window_span)
    row_valid = (query_rows >= 0) & (query_rows < image_rows)
    row_valid = row_valid[:, :, None] & (key_rows[:, None, :] >= row_first[:, :, None]) & (key_rows[:, None, :] < row_first[:, :, None] + window_span)
    col_first = jnp.clip(query_cols - window_half, 0, image_cols - window_span)
    col_valid = (query_cols >= 0) & (query_cols < image_cols)
    col_valid = col_valid[:, None] & (key_cols[None, :] >= col_first[:, None]) & (key_cols[None, :] < col_first[:, None] + window_span)
    joined = row_valid[:, :, None, :, None] & col_valid[None, None, :, None, :]
    shape_now = joined.shape
    return joined.reshape(shape_now[0], shape_now[1] * shape_now[2], shape_now[3] * shape_now[4])

def query_side_mask(row_start, col_start, tile_rows, tile_cols, image_rows, image_cols):
    groups = tile_rows // group_rows
    group_base = jnp.arange(groups, dtype=jnp.int32)[:, None] * group_rows
    query_rows = row_start + group_base + jnp.arange(group_rows, dtype=jnp.int32)[None, :]
    query_cols = col_start + jnp.arange(tile_cols, dtype=jnp.int32)
    key_rows = row_start - window_half + group_base + jnp.arange(group_rows + 2 * window_half, dtype=jnp.int32)[None, :]
    key_cols = col_start - window_half + jnp.arange(tile_cols + 2 * window_half, dtype=jnp.int32)
    return window_mask(query_rows, query_cols, key_rows, key_cols, image_rows, image_cols)

def key_side_mask(row_start, col_start, tile_rows, tile_cols, image_rows, image_cols):
    groups = tile_rows // group_rows
    group_base = jnp.arange(groups, dtype=jnp.int32)[:, None] * group_rows
    key_rows = row_start + group_base + jnp.arange(group_rows, dtype=jnp.int32)[None, :]
    key_cols = col_start + jnp.arange(tile_cols, dtype=jnp.int32)
    query_rows = row_start - 2 * window_half + group_base + jnp.arange(group_rows + 4 * window_half, dtype=jnp.int32)[None, :]
    query_cols = col_start - window_half + jnp.arange(tile_cols + 2 * window_half, dtype=jnp.int32)
    return window_mask(query_rows, query_cols, key_rows, key_cols, image_rows, image_cols)

def row_bands(slab, groups, depth):
    return jnp.stack([slab[member * group_rows:member * group_rows + depth] for member in range(groups)])

def attend_tile(query_tile, kv_slab, row_start, col_start, image_rows, image_cols):
    tile_rows, tile_cols, model_dim = query_tile.shape
    head_dim = model_dim // HEADS
    scaling = head_dim ** (-0.5)
    groups = tile_rows // group_rows
    key_band = row_bands(kv_slab, groups, group_rows + 2 * window_half).reshape(groups, -1, 2, HEADS, head_dim)
    queries = query_tile.reshape(groups, group_rows * tile_cols, HEADS, head_dim)
    visible = query_side_mask(row_start, col_start, tile_rows, tile_cols, image_rows, image_cols)[:, None]
    scores = jnp.where(visible, product('gqhe,gkhe->ghqk', queries, key_band[:, :, 0]) * scaling, -jnp.inf)
    row_max = lax.optimization_barrier(jnp.max(scores, axis=-1, keepdims=True))
    log_total = row_max + jnp.log(lax.optimization_barrier(jnp.sum(jnp.exp(scores - row_max), axis=-1, keepdims=True)))
    weights = jnp.exp(scores - log_total).astype(jnp.bfloat16)
    attended = product('ghqk,gkhe->gqhe', weights, key_band[:, :, 1]).astype(jnp.bfloat16)
    log_tile = log_total[..., 0].transpose(0, 2, 1).reshape(tile_rows, tile_cols, HEADS)
    return (attended.reshape(tile_rows, tile_cols, model_dim), log_tile)

def query_grad_tile(query_tile, kv_slab, grad_tile, log_tile, delta_tile, row_start, col_start, image_rows, image_cols):
    tile_rows, tile_cols, model_dim = query_tile.shape
    head_dim = model_dim // HEADS
    scaling = head_dim ** (-0.5)
    groups = tile_rows // group_rows
    key_band = row_bands(kv_slab, groups, group_rows + 2 * window_half).reshape(groups, -1, 2, HEADS, head_dim)
    queries = query_tile.reshape(groups, group_rows * tile_cols, HEADS, head_dim)
    grads = grad_tile.reshape(groups, group_rows * tile_cols, HEADS, head_dim)
    log_group = log_tile.reshape(groups, group_rows * tile_cols, HEADS).transpose(0, 2, 1)[..., None]
    delta_group = delta_tile.reshape(groups, group_rows * tile_cols, HEADS).transpose(0, 2, 1)[..., None]
    visible = query_side_mask(row_start, col_start, tile_rows, tile_cols, image_rows, image_cols)[:, None]
    scores = product('gqhe,gkhe->ghqk', queries, key_band[:, :, 0]) * scaling
    chances = jnp.exp(jnp.where(visible, scores - log_group, -jnp.inf))
    d_prob = product('gqhe,gkhe->ghqk', grads, key_band[:, :, 1])
    d_score = (chances * (d_prob - delta_group)).astype(jnp.bfloat16)
    d_query = (product('ghqk,gkhe->gqhe', d_score, key_band[:, :, 0]) * scaling).astype(jnp.bfloat16)
    return d_query.reshape(tile_rows, tile_cols, model_dim)

def key_grad_tile(kv_tile, pair_slab, stat_slab, row_start, col_start, image_rows, image_cols):
    tile_rows, tile_cols, double_dim = kv_tile.shape
    head_dim = double_dim // (2 * HEADS)
    scaling = head_dim ** (-0.5)
    groups = tile_rows // group_rows
    depth = group_rows + 4 * window_half
    query_band = row_bands(pair_slab, groups, depth).reshape(groups, -1, 2, HEADS, head_dim)
    stat_band = row_bands(stat_slab, groups, depth).reshape(groups, -1, 2, HEADS).transpose(0, 2, 3, 1)
    own_keys = kv_tile.reshape(groups, group_rows * tile_cols, 2, HEADS, head_dim)
    visible = key_side_mask(row_start, col_start, tile_rows, tile_cols, image_rows, image_cols)[:, None]
    scores = product('gqhe,gkhe->ghqk', query_band[:, :, 0], own_keys[:, :, 0]) * scaling
    chances = jnp.exp(jnp.where(visible, scores - stat_band[:, 0, :, :, None], -jnp.inf))
    d_value = product('ghqk,gqhe->gkhe', chances.astype(jnp.bfloat16), query_band[:, :, 1]).astype(jnp.bfloat16)
    d_prob = product('gqhe,gkhe->ghqk', query_band[:, :, 1], own_keys[:, :, 1])
    d_score = (chances * (d_prob - stat_band[:, 1, :, :, None])).astype(jnp.bfloat16)
    d_key = (product('ghqk,gqhe->gkhe', d_score, query_band[:, :, 0]) * scaling).astype(jnp.bfloat16)
    return jnp.stack([d_key, d_value], axis=2).reshape(tile_rows, tile_cols, double_dim)

def blocks(left_side, right_side, left_parts, right_parts):
    token_total = left_side.shape[0]
    left_view = left_side.reshape(token_total, left_parts, -1)
    right_view = right_side.reshape(token_total, right_parts, -1)
    summed = product('tar,tbc->abrc', left_view, right_view)
    return summed.reshape(left_parts * right_parts, left_view.shape[2], right_view.shape[2])

def accumulate(left_stat, right_stat, gradient, scaling):
    scaled = gradient * scaling
    new_left = left_stat + jnp.einsum('brc,bsc->brs', scaled, scaled, precision=lax.Precision.HIGHEST) / scaled.shape[2]
    new_right = right_stat + jnp.einsum('brc,brs->bcs', scaled, scaled, precision=lax.Precision.HIGHEST) / scaled.shape[1]
    return (new_left, new_right)

def tiles_to_image(stacked):
    channels = stacked.shape[-1]
    return stacked.reshape(N_ROWS, N_COLS, TH, TW, channels).transpose(0, 2, 1, 3, 4).reshape(N_ROWS * TH, N_COLS * TW, channels)

def reference(tokens, cotangent, gain_attn, gain_mlp, weight_qkv, weight_out, weight_up, weight_down, left_qkv, right_qkv, left_up, right_up, left_down, right_down):
    image_rows, image_cols, model_dim = tokens.shape
    token_total = image_rows * image_cols
    flat_tokens = tokens.reshape(token_total, model_dim).astype(jnp.float32)
    normed_attn = normed(flat_tokens, gain_attn).astype(jnp.bfloat16)
    qkv_image = jnp.dot(normed_attn, weight_qkv, preferred_element_type=jnp.float32).astype(jnp.bfloat16).reshape(image_rows, image_cols, 3 * model_dim)
    query_image = qkv_image[:, :, :model_dim]
    kv_image = qkv_image[:, :, model_dim:]
    kv_padded = jnp.pad(kv_image, ((window_half, window_half), (window_half, window_half), (0, 0)))
    tile_ids = jnp.arange(N_ROWS * N_COLS, dtype=jnp.int32)
    zero_index = jnp.zeros((), jnp.int32)

    def corner(tile_index):
        return (tile_index // N_COLS * TH, tile_index % N_COLS * TW)

    def forward_one(tile_index):
        row_start, col_start = corner(tile_index)
        query_tile = lax.dynamic_slice(query_image, (row_start, col_start, zero_index), (TH, TW, model_dim))
        kv_slab = lax.dynamic_slice(kv_padded, (row_start, col_start, zero_index), (TH + 2 * window_half, TW + 2 * window_half, 2 * model_dim))
        return attend_tile(query_tile, kv_slab, row_start, col_start, image_rows, image_cols)
    attended_tiles, log_tiles = lax.map(forward_one, tile_ids)
    attended = tiles_to_image(attended_tiles)
    log_total = tiles_to_image(log_tiles)
    attended_flat = attended.reshape(token_total, model_dim)
    residual = (flat_tokens + jnp.dot(attended_flat, weight_out, preferred_element_type=jnp.float32)).astype(jnp.bfloat16)
    residual_wide = residual.astype(jnp.float32)
    normed_mlp = normed(residual_wide, gain_mlp).astype(jnp.bfloat16)
    up_proj = jnp.dot(normed_mlp, weight_up, preferred_element_type=jnp.float32)
    activated = gelu_tanh(up_proj).astype(jnp.bfloat16)
    mixed = (residual_wide + jnp.dot(activated, weight_down, preferred_element_type=jnp.float32)).astype(jnp.bfloat16)
    grad_output = cotangent.reshape(token_total, model_dim)
    d_act = jnp.dot(grad_output, weight_down.T, preferred_element_type=jnp.float32)
    d_up = jax.vjp(gelu_tanh, up_proj)[1](d_act)[0].astype(jnp.bfloat16)
    d_normed = jnp.dot(d_up, weight_up.T, preferred_element_type=jnp.float32)
    d_residual = (grad_output.astype(jnp.float32) + norm_grad(residual_wide, gain_mlp, d_normed)).astype(jnp.bfloat16)
    d_attended = jnp.dot(d_residual, weight_out.T, preferred_element_type=jnp.float32).astype(jnp.bfloat16)
    delta_sum = lax.optimization_barrier(jnp.sum((attended_flat.astype(jnp.float32) * d_attended.astype(jnp.float32)).reshape(token_total, HEADS, -1), axis=-1)).reshape(image_rows, image_cols, HEADS)
    d_attended_image = d_attended.reshape(image_rows, image_cols, model_dim)

    def query_back(tile_index):
        row_start, col_start = corner(tile_index)
        query_tile = lax.dynamic_slice(query_image, (row_start, col_start, zero_index), (TH, TW, model_dim))
        kv_slab = lax.dynamic_slice(kv_padded, (row_start, col_start, zero_index), (TH + 2 * window_half, TW + 2 * window_half, 2 * model_dim))
        grad_tile = lax.dynamic_slice(d_attended_image, (row_start, col_start, zero_index), (TH, TW, model_dim))
        log_tile = lax.dynamic_slice(log_total, (row_start, col_start, zero_index), (TH, TW, HEADS))
        delta_tile = lax.dynamic_slice(delta_sum, (row_start, col_start, zero_index), (TH, TW, HEADS))
        return query_grad_tile(query_tile, kv_slab, grad_tile, log_tile, delta_tile, row_start, col_start, image_rows, image_cols)
    d_query = tiles_to_image(lax.map(query_back, tile_ids))
    pad_rule = ((2 * window_half, 2 * window_half), (window_half, window_half), (0, 0))
    pair_padded = jnp.pad(jnp.concatenate([query_image, d_attended_image], axis=-1), pad_rule)
    stat_padded = jnp.pad(jnp.concatenate([log_total, delta_sum], axis=-1), pad_rule)

    def key_back(tile_index):
        row_start, col_start = corner(tile_index)
        kv_tile = lax.dynamic_slice(kv_image, (row_start, col_start, zero_index), (TH, TW, 2 * model_dim))
        pair_slab = lax.dynamic_slice(pair_padded, (row_start, col_start, zero_index), (TH + 4 * window_half, TW + 2 * window_half, 2 * model_dim))
        stat_slab = lax.dynamic_slice(stat_padded, (row_start, col_start, zero_index), (TH + 4 * window_half, TW + 2 * window_half, 2 * HEADS))
        return key_grad_tile(kv_tile, pair_slab, stat_slab, row_start, col_start, image_rows, image_cols)
    d_kv = tiles_to_image(lax.map(key_back, tile_ids))
    d_qkv = jnp.concatenate([d_query, d_kv], axis=-1).reshape(token_total, 3 * model_dim)
    d_normed_attn = jnp.dot(d_qkv, weight_qkv.T, preferred_element_type=jnp.float32)
    d_tokens = (d_residual.astype(jnp.float32) + norm_grad(flat_tokens, gain_attn, d_normed_attn)).astype(jnp.bfloat16)
    scaling = float(token_total) ** (-0.5)
    new_left_qkv, new_right_qkv = accumulate(left_qkv, right_qkv, blocks(normed_attn, d_qkv, 8, 16), scaling)
    new_left_up, new_right_up = accumulate(left_up, right_up, blocks(normed_mlp, d_up, 8, 16), scaling)
    new_left_down, new_right_down = accumulate(left_down, right_down, blocks(activated, grad_output, 16, 8), scaling)
    return (mixed.reshape(image_rows, image_cols, model_dim), d_tokens.reshape(image_rows, image_cols, model_dim), new_left_qkv, new_right_qkv, new_left_up, new_right_up, new_left_down, new_right_down)
```

```python
import jax
import jax.numpy as jnp
from jax import lax
from jax.experimental import pallas as pl
from jax.experimental.pallas import tpu as pltpu
from jax.sharding import PartitionSpec as P

HEADS = 12


epsilon = 1e-06
window_half = 6
window_span = 13
group_rows = 8


def with_halo(x, sides, width):
    for axis, dim in sides:
        size, length = (lax.axis_size(axis), x.shape[dim])
        up = [(i, (i + 1) % size) for i in range(size - 1)]
        down = [(j, i) for i, j in up]
        last = lax.slice_in_dim(x, length - width, length, axis=dim)
        initial = lax.slice_in_dim(x, 0, width, axis=dim)
        before = lax.ppermute(last, axis, up)
        after = lax.ppermute(initial, axis, down)
        x = jnp.concatenate([before, x, after], axis=dim)
    return x


def normed(inputs, gain):
    return inputs * lax.rsqrt(jnp.mean(inputs * inputs, axis=-1, keepdims=True) + epsilon) * gain


def norm_grad(inputs, gain, upstream):
    return jax.vjp(lambda column: normed(column, gain), inputs)[1](upstream)[0]


def gelu_tanh(inputs):
    return jax.nn.gelu(inputs, approximate=True)


def product(formula, left_side, right_side):
    return jnp.einsum(formula, left_side, right_side, preferred_element_type=jnp.float32)


def window_mask(query_rows, query_cols, key_rows, key_cols, image_rows, image_cols):
    row_first = jnp.clip(query_rows - window_half, 0, image_rows - window_span)
    row_valid = (query_rows >= 0) & (query_rows < image_rows)
    row_valid = (
        row_valid[:, :, None]
        & (key_rows[:, None, :] >= row_first[:, :, None])
        & (key_rows[:, None, :] < row_first[:, :, None] + window_span)
    )
    col_first = jnp.clip(query_cols - window_half, 0, image_cols - window_span)
    col_valid = (query_cols >= 0) & (query_cols < image_cols)
    col_valid = (
        col_valid[:, None]
        & (key_cols[None, :] >= col_first[:, None])
        & (key_cols[None, :] < col_first[:, None] + window_span)
    )
    joined = row_valid[:, :, None, :, None] & col_valid[None, None, :, None, :]
    shape_now = joined.shape
    return joined.reshape(shape_now[0], shape_now[1] * shape_now[2], shape_now[3] * shape_now[4])


def query_side_mask(row_start, col_start, tile_rows, tile_cols, image_rows, image_cols):
    groups = tile_rows // group_rows
    group_base = jnp.arange(groups, dtype=jnp.int32)[:, None] * group_rows
    query_rows = row_start + group_base + jnp.arange(group_rows, dtype=jnp.int32)[None, :]
    query_cols = col_start + jnp.arange(tile_cols, dtype=jnp.int32)
    key_rows = (
        row_start
        - window_half
        + group_base
        + jnp.arange(group_rows + 2 * window_half, dtype=jnp.int32)[None, :]
    )
    key_cols = col_start - window_half + jnp.arange(tile_cols + 2 * window_half, dtype=jnp.int32)
    return window_mask(query_rows, query_cols, key_rows, key_cols, image_rows, image_cols)


def key_side_mask(row_start, col_start, tile_rows, tile_cols, image_rows, image_cols):
    groups = tile_rows // group_rows
    group_base = jnp.arange(groups, dtype=jnp.int32)[:, None] * group_rows
    key_rows = row_start + group_base + jnp.arange(group_rows, dtype=jnp.int32)[None, :]
    key_cols = col_start + jnp.arange(tile_cols, dtype=jnp.int32)
    query_rows = (
        row_start
        - 2 * window_half
        + group_base
        + jnp.arange(group_rows + 4 * window_half, dtype=jnp.int32)[None, :]
    )
    query_cols = col_start - window_half + jnp.arange(tile_cols + 2 * window_half, dtype=jnp.int32)
    return window_mask(query_rows, query_cols, key_rows, key_cols, image_rows, image_cols)


def row_bands(slab, groups, depth):
    return jnp.stack(
        [slab[member * group_rows : member * group_rows + depth] for member in range(groups)]
    )


def attend_tile(query_tile, kv_slab, row_start, col_start, image_rows, image_cols):
    tile_rows, tile_cols, model_dim = query_tile.shape
    head_dim = model_dim // HEADS
    scaling = head_dim ** (-0.5)
    groups = tile_rows // group_rows
    key_band = row_bands(kv_slab, groups, group_rows + 2 * window_half).reshape(
        groups, -1, 2, HEADS, head_dim
    )
    queries = query_tile.reshape(groups, group_rows * tile_cols, HEADS, head_dim)
    visible = query_side_mask(row_start, col_start, tile_rows, tile_cols, image_rows, image_cols)[
        :, None
    ]
    scores = jnp.where(
        visible, product("gqhe,gkhe->ghqk", queries, key_band[:, :, 0]) * scaling, -jnp.inf
    )
    row_max = jnp.max(scores, axis=-1, keepdims=True)
    log_total = row_max + jnp.log(jnp.sum(jnp.exp(scores - row_max), axis=-1, keepdims=True))
    weights = jnp.exp(scores - log_total).astype(jnp.bfloat16)
    attended = product("ghqk,gkhe->gqhe", weights, key_band[:, :, 1]).astype(jnp.bfloat16)
    log_tile = log_total[..., 0].transpose(0, 2, 1).reshape(tile_rows, tile_cols, HEADS)
    return (attended.reshape(tile_rows, tile_cols, model_dim), log_tile)


def query_grad_tile(
    query_tile,
    kv_slab,
    grad_tile,
    log_tile,
    delta_tile,
    row_start,
    col_start,
    image_rows,
    image_cols,
):
    tile_rows, tile_cols, model_dim = query_tile.shape
    head_dim = model_dim // HEADS
    scaling = head_dim ** (-0.5)
    groups = tile_rows // group_rows
    key_band = row_bands(kv_slab, groups, group_rows + 2 * window_half).reshape(
        groups, -1, 2, HEADS, head_dim
    )
    queries = query_tile.reshape(groups, group_rows * tile_cols, HEADS, head_dim)
    grads = grad_tile.reshape(groups, group_rows * tile_cols, HEADS, head_dim)
    log_group = log_tile.reshape(groups, group_rows * tile_cols, HEADS).transpose(0, 2, 1)[
        ..., None
    ]
    delta_group = delta_tile.reshape(groups, group_rows * tile_cols, HEADS).transpose(0, 2, 1)[
        ..., None
    ]
    visible = query_side_mask(row_start, col_start, tile_rows, tile_cols, image_rows, image_cols)[
        :, None
    ]
    scores = product("gqhe,gkhe->ghqk", queries, key_band[:, :, 0]) * scaling
    chances = jnp.exp(jnp.where(visible, scores - log_group, -jnp.inf))
    d_prob = product("gqhe,gkhe->ghqk", grads, key_band[:, :, 1])
    d_score = (chances * (d_prob - delta_group)).astype(jnp.bfloat16)
    d_query = (product("ghqk,gkhe->gqhe", d_score, key_band[:, :, 0]) * scaling).astype(
        jnp.bfloat16
    )
    return d_query.reshape(tile_rows, tile_cols, model_dim)


def key_grad_tile(kv_tile, pair_slab, stat_slab, row_start, col_start, image_rows, image_cols):
    tile_rows, tile_cols, double_dim = kv_tile.shape
    head_dim = double_dim // (2 * HEADS)
    scaling = head_dim ** (-0.5)
    groups = tile_rows // group_rows
    depth = group_rows + 4 * window_half
    query_band = row_bands(pair_slab, groups, depth).reshape(groups, -1, 2, HEADS, head_dim)
    stat_band = (
        row_bands(stat_slab, groups, depth).reshape(groups, -1, 2, HEADS).transpose(0, 2, 3, 1)
    )
    own_keys = kv_tile.reshape(groups, group_rows * tile_cols, 2, HEADS, head_dim)
    visible = key_side_mask(row_start, col_start, tile_rows, tile_cols, image_rows, image_cols)[
        :, None
    ]
    scores = product("gqhe,gkhe->ghqk", query_band[:, :, 0], own_keys[:, :, 0]) * scaling
    chances = jnp.exp(jnp.where(visible, scores - stat_band[:, 0, :, :, None], -jnp.inf))
    d_value = product("ghqk,gqhe->gkhe", chances.astype(jnp.bfloat16), query_band[:, :, 1]).astype(
        jnp.bfloat16
    )
    d_prob = product("gqhe,gkhe->ghqk", query_band[:, :, 1], own_keys[:, :, 1])
    d_score = (chances * (d_prob - stat_band[:, 1, :, :, None])).astype(jnp.bfloat16)
    d_key = (product("ghqk,gqhe->gkhe", d_score, query_band[:, :, 0]) * scaling).astype(
        jnp.bfloat16
    )
    return jnp.stack([d_key, d_value], axis=2).reshape(tile_rows, tile_cols, double_dim)


MESH = pl.DeviceIdType.MESH
FLOWS = 6
CHIPS = 64


def gray_bits(position):
    high = position // 2
    return (high, (high + position % 2) % 2)


def my_place():
    row = lax.axis_index("rows")
    col = lax.axis_index("cols")
    core = col % 2
    x = col // 4
    y = (row // 4) * 2 + (col // 2) % 2
    z = row % 4
    return x, y, z, core


def device_at(x, y, z, core):
    return ((y // 2) * 4 + z, x * 4 + (y % 2) * 2 + core)


def link_bits(x, y, z):
    gx, gy, gz = gray_bits(x), gray_bits(y), gray_bits(z)
    return (gx[1], gy[1], gz[1], gx[0], gy[0], gz[0])


def link_partners(x, y, z, core):
    return (
        device_at(x + 1 - 2 * (x % 2), y, z, core),
        device_at(x, y + 1 - 2 * (y % 2), z, core),
        device_at(x, y, z + 1 - 2 * (z % 2), core),
        device_at(3 - x, y, z, core),
        device_at(x, 3 - y, z, core),
        device_at(x, y, 3 - z, core),
    )


def flow_slots(mine, theirs):
    differs = [(m + t) % 2 for m, t in zip(mine, theirs)]
    slots = []
    for flow in range(FLOWS):
        slot = 0
        for step in range(6):
            slot = slot * 2 + differs[(flow + step) % 6]
        slots.append(slot)
    return slots


class Channel:
    def __init__(self, own, core_in, mesh_in, sems, index, flow, total_at):
        self.own, self.core_in, self.mesh_in = own, core_in, mesh_in
        self.core_send, self.core_recv, self.mesh_send, self.mesh_recv = sems
        self.index, self.flow, self.total_at = index, flow, total_at

    def core_copy(self, sibling):
        return pltpu.make_async_remote_copy(
            src_ref=self.own.at[1, self.index],
            dst_ref=self.core_in.at[self.index],
            send_sem=self.core_send.at[self.index],
            recv_sem=self.core_recv.at[self.index],
            device_id=sibling,
            device_id_type=MESH,
        )

    def mesh_copy(self, step, partners):
        count = 32 >> step
        return pltpu.make_async_remote_copy(
            src_ref=self.own.at[0, self.index, pl.ds(count, count)],
            dst_ref=self.mesh_in.at[self.index, pl.ds(count, count)],
            send_sem=self.mesh_send.at[self.index, step],
            recv_sem=self.mesh_recv.at[self.index, step],
            device_id=partners[(self.flow + step) % 6],
            device_id_type=MESH,
        )

    def add(self, source, source_first, first, count):
        own, index = self.own, self.index
        rows, lanes = own.shape[3], own.shape[4]
        chunk = min(count, max(1, 128 // rows))

        def body(turn, carry):
            at = first + turn * chunk
            own[0, index, pl.ds(at, chunk)] = (
                own[0, index, pl.ds(at, chunk)]
                + source[index, pl.ds(source_first + turn * chunk, chunk)]
            )
            return carry

        lax.fori_loop(0, count // chunk, body, 0)

    def after_core(self, partners, sibling):
        self.core_copy(sibling).wait_recv()
        self.add(self.core_in, 32, 32, 32)
        self.mesh_copy(0, partners).start()
        self.add(self.core_in, 0, 0, 32)

    def after_mesh(self, step, partners, total):
        self.mesh_copy(step, partners).wait_recv()
        count = 32 >> step
        if step < 5:
            half = count // 2
            self.add(self.mesh_in, count + half, half, half)
            self.mesh_copy(step + 1, partners).start()
            self.add(self.mesh_in, count, 0, half)
        else:
            rows = self.own.shape[3]
            total[pl.ds(self.total_at, rows)] = self.own[0, self.index, 0].astype(
                jnp.float32
            ) + self.mesh_in[self.index, 1].astype(jnp.float32)

    def finish(self, partners, sibling):
        self.core_copy(sibling).wait_send()
        for step in range(6):
            self.mesh_copy(step, partners).wait_send()


def up_payload(group, mine, core, a2t, b2, a3t, b3, ubuf):
    z = group % 4
    y_hi = group // 4
    left = a2t[pl.ds(pl.multiple_of(96 * group, 32), 96), :]
    lane = lax.broadcasted_iota(jnp.int32, (96, 128), 1)
    for c in range(8):
        x, y = c // 2, y_hi * 2 + c % 2
        slots = flow_slots(mine, link_bits(x, y, z))
        up = jnp.dot(
            left, b2[:, 384 * c : 384 * c + 384], preferred_element_type=jnp.float32
        )
        q, odd = c % 4, c // 4
        tile = 3 * group
        down_left = a3t[192 * q : 192 * q + 192, :]
        main_at = pl.multiple_of((tile + 2 * odd) * 128, 128)
        half_at = pl.multiple_of((tile + 1) * 128, 128)
        main = jnp.dot(
            down_left, b3[:, pl.ds(main_at, 128)], preferred_element_type=jnp.float32
        )
        half = jnp.dot(
            down_left, b3[:, pl.ds(half_at, 128)], preferred_element_type=jnp.float32
        )
        first, second = half[:96], half[96:]
        if odd:
            packed = jnp.where(lane < 64, pltpu.roll(first, 64, 1), second)
        else:
            packed = jnp.where(lane < 64, first, pltpu.roll(second, 64, 1))
        pieces = [
            up[:, :128],
            up[:, 128:256],
            up[:, 256:],
            main[:96],
            main[96:],
            packed,
        ]
        for flow, piece in enumerate(pieces):
            piece = piece.astype(jnp.bfloat16)
            for half_at in range(2):
                ubuf[(core + half_at) % 2, flow, slots[flow]] = piece[
                    48 * half_at : 48 * half_at + 48
                ]


def qkv_payload(group, mine, core, a1t, a1p, b1m, b1rt, qbuf, rbuf):
    z = group % 4
    y_hi = group // 4
    left = a1t[pl.ds(pl.multiple_of(96 * group, 32), 96), :]
    rest = jnp.dot(
        b1rt[...],
        a1p[:, pl.ds(pl.multiple_of(128 * group, 128), 128)],
        preferred_element_type=jnp.float32,
    ).astype(jnp.bfloat16)
    for c in range(8):
        x, y = c // 2, y_hi * 2 + c % 2
        slots = flow_slots(mine, link_bits(x, y, z))
        main = jnp.dot(
            left, b1m[:, 256 * c : 256 * c + 256], preferred_element_type=jnp.float32
        ).astype(jnp.bfloat16)
        for half in range(2):
            for flow in range(FLOWS):
                qbuf[(core + half) % 2, flow, slots[flow]] = main[
                    16 * flow : 16 * flow + 16, 128 * half : 128 * half + 128
                ]
            rbuf[(core + half) % 2, 0, slots[0]] = rest[
                32 * c + 16 * half : 32 * c + 16 * half + 16
            ]


def grads_kernel(
    a2t,
    b2,
    a3t,
    b3,
    a1t,
    a1p,
    b1m,
    b1rt,
    out,
    ubuf,
    ucore,
    umesh,
    qbuf,
    qcore,
    qmesh,
    rbuf,
    rcore,
    rmesh,
    total,
    other,
    *sems,
):
    x, y, z, core = my_place()
    sibling = device_at(x, y, z, 1 - core)
    partners = link_partners(x, y, z, core)
    mine = link_bits(x, y, z)
    barrier = pltpu.get_barrier_semaphore()
    for partner in (sibling,) + partners:
        pl.semaphore_signal(barrier, inc=1, device_id=partner, device_id_type=MESH)
    pl.semaphore_wait(barrier, 7)

    up = [
        Channel(ubuf, ucore, umesh, sems[0:4], flow, flow, 48 * flow)
        for flow in range(FLOWS)
    ]
    qkv = [
        Channel(qbuf, qcore, qmesh, sems[4:8], flow, flow, 288 + 16 * flow)
        for flow in range(FLOWS)
    ]
    qkv.append(Channel(rbuf, rcore, rmesh, sems[8:12], 0, 0, 384))
    channels = up + qkv

    def up_body(group, carry):
        up_payload(group, mine, core, a2t, b2, a3t, b3, ubuf)
        return carry

    lax.fori_loop(0, 8, up_body, 0)
    for channel in up:
        channel.core_copy(sibling).start()

    def qkv_body(group, carry):
        qkv_payload(group, mine, core, a1t, a1p, b1m, b1rt, qbuf, rbuf)
        return carry

    lax.fori_loop(0, 8, qkv_body, 0)
    for channel in qkv:
        channel.core_copy(sibling).start()
    for channel in channels:
        channel.after_core(partners, sibling)
    for step in range(6):
        for channel in channels:
            channel.after_mesh(step, partners, total)
    last = pltpu.make_async_remote_copy(
        src_ref=total,
        dst_ref=other,
        send_sem=sems[12],
        recv_sem=sems[13],
        device_id=sibling,
        device_id_type=MESH,
    )
    last.start()
    last.wait_recv()
    own_first = core == 0
    out[0] = jnp.where(own_first, total[...], other[...])
    out[1] = jnp.where(own_first, other[...], total[...])
    for channel in channels:
        channel.finish(partners, sibling)
    last.wait_send()


def summed_grads(a2t, b2, a3t, b3, a1t, a1p, b1m, b1rt):
    def set_of(count, rows):
        return [
            pltpu.VMEM((2, count, CHIPS, rows, 128), jnp.bfloat16),
            pltpu.VMEM((count, CHIPS, rows, 128), jnp.bfloat16),
            pltpu.VMEM((count, CHIPS, rows, 128), jnp.bfloat16),
        ]

    def sems_of(count):
        return [
            pltpu.SemaphoreType.DMA((count,)),
            pltpu.SemaphoreType.DMA((count,)),
            pltpu.SemaphoreType.DMA((count, 6)),
            pltpu.SemaphoreType.DMA((count, 6)),
        ]

    return pl.pallas_call(
        grads_kernel,
        out_shape=jax.ShapeDtypeStruct((2, 400, 128), jnp.float32),
        in_specs=[pl.BlockSpec(memory_space=pltpu.VMEM)] * 8,
        out_specs=pl.BlockSpec(memory_space=pltpu.VMEM),
        scratch_shapes=set_of(6, 48)
        + set_of(6, 16)
        + set_of(1, 16)
        + [pltpu.VMEM((400, 128), jnp.float32)] * 2
        + sems_of(6)
        + sems_of(6)
        + sems_of(1)
        + [pltpu.SemaphoreType.DMA, pltpu.SemaphoreType.DMA],
        compiler_params=pltpu.CompilerParams(
            collective_id=0, has_side_effects=True, vmem_limit_bytes=56 * 2**20
        ),
    )(a2t, b2, a3t, b3, a1t, a1p, b1m, b1rt)


def owned_blocks(summed, core, part_odd):
    def rows_of(first):
        return jnp.concatenate(
            [summed[0, first : first + 48], summed[1, first : first + 48]], axis=0
        )

    left, middle, right = rows_of(0), rows_of(48), rows_of(96)
    up = jnp.where(
        core == 0,
        jnp.concatenate([left, middle[:, :64]], axis=1),
        jnp.concatenate([middle[:, 64:], right], axis=1),
    )
    main = jnp.where(core == 0, rows_of(144), rows_of(192))
    packed = rows_of(240)
    half = jnp.where(core == 0, packed[:, :64], packed[:, 64:])
    down = jnp.where(
        part_odd == 1,
        jnp.concatenate([half, main], axis=1),
        jnp.concatenate([main, half], axis=1),
    )
    first, second = summed[0, 288:384], summed[1, 288:384]
    rest = jnp.concatenate([summed[0, 384:400], summed[1, 384:400]], axis=0).T[:96]
    qkv = jnp.where(
        core == 0,
        jnp.concatenate([first, second[:, :16]], axis=1),
        jnp.concatenate([second[:, 16:], rest], axis=1),
    )
    return up, down, qkv


def accumulate(left_stat, right_stat, gradient, scaling):
    scaled = gradient * scaling
    new_left = (
        left_stat
        + jnp.einsum("brc,bsc->brs", scaled, scaled, precision=lax.Precision.HIGHEST)
        / scaled.shape[2]
    )
    new_right = (
        right_stat
        + jnp.einsum("brc,brs->bcs", scaled, scaled, precision=lax.Precision.HIGHEST)
        / scaled.shape[1]
    )
    return (new_left, new_right)


def surround_keys(kv_tile):
    return with_halo(kv_tile, (("rows", 0), ("cols", 1)), 6)


def on_device(
    tokens,
    cotangent,
    gain_attn,
    gain_mlp,
    weight_qkv,
    weight_out,
    weight_up,
    weight_down,
    left_qkv,
    right_qkv,
    left_up,
    right_up,
    left_down,
    right_down,
):
    tile_rows, tile_cols, model_dim = tokens.shape
    row_count = lax.axis_size("rows")
    col_count = lax.axis_size("cols")
    image_rows = tile_rows * row_count
    image_cols = tile_cols * col_count
    row_start = lax.axis_index("rows") * tile_rows
    col_start = lax.axis_index("cols") * tile_cols
    token_count = tile_rows * tile_cols
    scaling = float(image_rows * image_cols) ** (-0.5)
    flat_tokens = tokens.reshape(token_count, model_dim).astype(jnp.float32)
    normed_attn = normed(flat_tokens, gain_attn).astype(jnp.bfloat16)
    qkv_tile = (
        jnp.dot(normed_attn, weight_qkv, preferred_element_type=jnp.float32)
        .astype(jnp.bfloat16)
        .reshape(tile_rows, tile_cols, 3 * model_dim)
    )
    query_tile = qkv_tile[:, :, :model_dim]
    kv_tile = qkv_tile[:, :, model_dim:]
    kv_slab = surround_keys(kv_tile)
    attended, log_tile = attend_tile(
        query_tile, kv_slab, row_start, col_start, image_rows, image_cols
    )
    attended_flat = attended.reshape(token_count, model_dim)
    residual = (
        flat_tokens + jnp.dot(attended_flat, weight_out, preferred_element_type=jnp.float32)
    ).astype(jnp.bfloat16)
    residual_wide = residual.astype(jnp.float32)
    normed_mlp = normed(residual_wide, gain_mlp).astype(jnp.bfloat16)
    up_proj = jnp.dot(normed_mlp, weight_up, preferred_element_type=jnp.float32)
    activated = gelu_tanh(up_proj).astype(jnp.bfloat16)
    mixed = (
        residual_wide + jnp.dot(activated, weight_down, preferred_element_type=jnp.float32)
    ).astype(jnp.bfloat16)
    grad_output = cotangent.reshape(token_count, model_dim)
    d_act = jnp.dot(grad_output, weight_down.T, preferred_element_type=jnp.float32)
    d_up = jax.vjp(gelu_tanh, up_proj)[1](d_act)[0].astype(jnp.bfloat16)
    d_normed = jnp.dot(d_up, weight_up.T, preferred_element_type=jnp.float32)
    d_residual = (
        grad_output.astype(jnp.float32) + norm_grad(residual_wide, gain_mlp, d_normed)
    ).astype(jnp.bfloat16)
    d_attended = jnp.dot(d_residual, weight_out.T, preferred_element_type=jnp.float32).astype(
        jnp.bfloat16
    )
    delta_sum = jnp.sum(
        (attended_flat.astype(jnp.float32) * d_attended.astype(jnp.float32)).reshape(
            token_count, HEADS, -1
        ),
        axis=-1,
    ).reshape(tile_rows, tile_cols, HEADS)
    d_attended_tile = d_attended.reshape(tile_rows, tile_cols, model_dim)
    pair_ext = with_halo(
        jnp.concatenate([query_tile, d_attended_tile], axis=-1), (("rows", 0), ("cols", 1)), 6
    )
    stat_ext = with_halo(
        jnp.concatenate([log_tile, delta_sum], axis=-1), (("rows", 0), ("cols", 1)), 6
    )
    d_query = query_grad_tile(
        query_tile,
        kv_slab,
        d_attended_tile,
        log_tile,
        delta_sum,
        row_start,
        col_start,
        image_rows,
        image_cols,
    )
    pad_rule = ((window_half, window_half), (0, 0), (0, 0))
    d_kv = key_grad_tile(
        kv_tile,
        jnp.pad(pair_ext, pad_rule),
        jnp.pad(stat_ext, pad_rule),
        row_start,
        col_start,
        image_rows,
        image_cols,
    )
    d_qkv = jnp.concatenate([d_query, d_kv], axis=-1).reshape(token_count, 3 * model_dim)
    d_normed_attn = jnp.dot(d_qkv, weight_qkv.T, preferred_element_type=jnp.float32)
    d_tokens = (
        d_residual.astype(jnp.float32) + norm_grad(flat_tokens, gain_attn, d_normed_attn)
    ).astype(jnp.bfloat16)
    d_qkv_pairs = d_qkv.reshape(token_count, 8, 288)
    summed = summed_grads(
        normed_mlp.T,
        d_up,
        grad_output.T,
        activated,
        normed_attn.T,
        jnp.pad(normed_attn.reshape(token_count, 8, 96), ((0, 0), (0, 0), (0, 32))).reshape(
            token_count, 1024
        ),
        d_qkv_pairs[:, :, :256].reshape(token_count, 2048),
        d_qkv_pairs[:, :, 256:].reshape(token_count, 256).T,
    )
    col = lax.axis_index("cols")
    up_owned, down_owned, qkv_owned = owned_blocks(summed, col % 2, (col // 8) % 2)
    up_owned, qkv_owned = up_owned[None], qkv_owned[None]
    down_owned = down_owned.T[None]
    new_left_qkv, new_right_qkv = accumulate(left_qkv, right_qkv, qkv_owned, scaling)
    new_left_up, new_right_up = accumulate(left_up, right_up, up_owned, scaling)
    new_left_down, new_right_down = accumulate(left_down, right_down, down_owned, scaling)
    return (
        mixed.reshape(tile_rows, tile_cols, model_dim),
        d_tokens.reshape(tile_rows, tile_cols, model_dim),
        new_left_qkv,
        new_right_qkv,
        new_left_up,
        new_right_up,
        new_left_down,
        new_right_down,
    )


def solution(mesh):
    in_specs = (
        P("rows", "cols", None),
        P("rows", "cols", None),
        P(),
        P(),
        P(),
        P(),
        P(),
        P(),
        P(("rows", "cols"), None, None),
        P(("rows", "cols"), None, None),
        P(("rows", "cols"), None, None),
        P(("rows", "cols"), None, None),
        P(("rows", "cols"), None, None),
        P(("rows", "cols"), None, None),
    )
    out_specs = (
        P("rows", "cols", None),
        P("rows", "cols", None),
        P(("rows", "cols"), None, None),
        P(("rows", "cols"), None, None),
        P(("rows", "cols"), None, None),
        P(("rows", "cols"), None, None),
        P(("rows", "cols"), None, None),
        P(("rows", "cols"), None, None),
    )
    return jax.shard_map(
        on_device, mesh=mesh, in_specs=in_specs, out_specs=out_specs, check_vma=False
    )
```

```python
import jax
import jax.numpy as jnp
import numpy as np
from jax import lax
from jax.experimental import pallas as pl
from jax.experimental.pallas import tpu as pltpu
from jax.sharding import PartitionSpec as P

HEADS = 12


epsilon = 1e-06
window_half = 6
window_span = 13


MODEL = 768
HIDDEN = 3072
TILE = 16
TOKENS = TILE * TILE
PIECES = (
    (-1, 0, 0, 96),
    (1, 0, 96, 96),
    (0, -1, 192, 96),
    (0, 1, 288, 96),
    (-1, -1, 384, 64),
    (-1, 1, 448, 64),
    (1, -1, 512, 64),
    (1, 1, 576, 64),
)
OPPOSITE = (1, 0, 3, 2, 7, 6, 5, 4)
KEYS = TOKENS + 640


def piece_tokens(down, right):
    near = {-1: range(window_half), 0: range(TILE), 1: range(TILE - window_half, TILE)}
    return [(r, c) for r in near[down] for c in near[right]]


def halo_tables():
    key_place = np.full((KEYS, 2), -1000, np.int32)
    key_place[:TOKENS] = [(r, c) for r in range(TILE) for c in range(TILE)]
    picks = np.zeros((448, TOKENS), np.float32)
    for down, right, first, _ in PIECES:
        for at, (r, c) in enumerate(piece_tokens(-down, -right)):
            key_place[TOKENS + first + at] = (r + TILE * down, c + TILE * right)
        if first >= 192:
            for at, (r, c) in enumerate(piece_tokens(down, right)):
                picks[first - 192 + at, r * TILE + c] = 1
    return key_place, picks


def dot(left, right):
    return jnp.dot(left, right, preferred_element_type=jnp.float32)


def dot_nt(left, right):
    return lax.dot_general(
        left, right, (((1,), (1,)), ((), ())), preferred_element_type=jnp.float32
    )


def inverse_rms(wide):
    return lax.rsqrt(jnp.mean(wide * wide, axis=-1, keepdims=True) + epsilon)


def norm_back(wide, scale, gain, upstream):
    scaled = upstream * gain
    return scale * scaled - wide * (
        scale * scale * scale * jnp.mean(wide * scaled, axis=-1, keepdims=True)
    )


def head_rows(pair_rows, second):
    blank = jnp.zeros((64, pair_rows.shape[1]), pair_rows.dtype)
    if second:
        return jnp.concatenate([blank, pair_rows[64:]], axis=0)
    return jnp.concatenate([pair_rows[:64], blank], axis=0)


def lane_masks():
    lane = lax.broadcasted_iota(jnp.int32, (1, 128), 1)
    low = jnp.where(lane < 64, 1.0, 0.0)
    return low.astype(jnp.bfloat16), (1.0 - low).astype(jnp.bfloat16)


MESH = pl.DeviceIdType.MESH


class Halo:
    def __init__(self, row, col, rows, cols):
        self.places = [
            ((row + down + rows) % rows, (col + right + cols) % cols)
            for down, right, _, _ in PIECES
        ]

    def copies(self, sources, target, base, send_sems, recv_sems):
        made = []
        for piece, (_, _, _, count) in enumerate(PIECES):
            lands = PIECES[OPPOSITE[piece]]
            made.append(
                pltpu.make_async_remote_copy(
                    src_ref=sources[piece],
                    dst_ref=target.at[pl.ds(base + lands[2], count)],
                    send_sem=send_sems.at[piece],
                    recv_sem=recv_sems.at[OPPOSITE[piece]],
                    device_id=self.places[piece],
                    device_id_type=MESH,
                )
            )
        return made


def block_kernel(
    tokens,
    cotangent,
    gain_attn,
    gain_mlp,
    key_place,
    picks,
    picks_t,
    weight_qkv,
    weight_out,
    weight_up,
    weight_down,
    mixed,
    d_tokens,
    a1t,
    a2t,
    a3t,
    d_up,
    activated,
    d_qkv_t,
    w_qkv,
    w_out,
    w_up,
    w_down,
    kv,
    packed,
    kv_t,
    query,
    query_t,
    chances,
    hidden,
    attended_t,
    d_act,
    d_query_t,
    d_attended,
    d_attended_t,
    d_kv_own,
    d_kv_far,
    d_kv_in,
    weight_sems,
    kv_send,
    kv_recv,
    back_send,
    back_recv,
):
    row, col = lax.axis_index("rows"), lax.axis_index("cols")
    rows, cols = lax.axis_size("rows"), lax.axis_size("cols")
    halo = Halo(row, col, rows, cols)
    loads = [
        pltpu.make_async_copy(source, place, weight_sems.at[at])
        for at, (source, place) in enumerate(
            ((weight_qkv, w_qkv), (weight_down, w_down), (weight_out, w_out), (weight_up, w_up))
        )
    ]
    for load in loads:
        load.start()
    barrier = pltpu.get_barrier_semaphore()
    for place in halo.places:
        pl.semaphore_signal(barrier, inc=1, device_id=place, device_id_type=MESH)

    wide = tokens[...].astype(jnp.float32)
    normed_attn = (wide * inverse_rms(wide) * gain_attn[...]).astype(jnp.bfloat16)
    loads[0].wait()
    kv[:TOKENS] = dot(normed_attn, w_qkv[:, MODEL:]).astype(jnp.bfloat16)
    packed[...] = dot(picks[...], kv[:TOKENS]).astype(jnp.bfloat16)
    pl.semaphore_wait(barrier, 8)
    sources = [kv.at[pl.ds(0, 96)], kv.at[pl.ds(TOKENS - 96, 96)]] + [
        packed.at[pl.ds(first - 192, count)] for _, _, first, count in PIECES[2:]
    ]
    sends = halo.copies(sources, kv, TOKENS, kv_send, kv_recv)
    for send in sends:
        send.start()

    own_query = dot(normed_attn, w_qkv[:, :MODEL]).astype(jnp.bfloat16)
    own_query = (own_query.astype(jnp.float32) * 0.125).astype(jnp.bfloat16)
    query[...] = own_query
    query_t[...] = own_query.T
    a1t[...] = normed_attn.T
    a3t[...] = cotangent[...].T

    at = lax.broadcasted_iota(jnp.int32, (1, TOKENS), 1)
    row_first = jnp.clip(row * TILE + at // TILE - window_half, 0, rows * TILE - window_span)
    col_first = jnp.clip(col * TILE + at % TILE - window_half, 0, cols * TILE - window_span)
    key_row = row * TILE + key_place[:, 0:1]
    key_col = col * TILE + key_place[:, 1:2]
    visible = (
        (key_row >= row_first)
        & (key_row < row_first + window_span)
        & (key_col >= col_first)
        & (key_col < col_first + window_span)
    )
    hidden[...] = jnp.where(visible, 0.0, -1e30)

    loads[1].wait()
    for part in range(4):
        d_act[:, MODEL * part : MODEL * part + MODEL] = dot_nt(
            cotangent[...], w_down[MODEL * part : MODEL * part + MODEL]
        )

    for send in sends:
        send.wait_recv()
    kv_t[...] = kv[...].T

    def attend(pair, carry):
        lanes = pl.ds(pl.multiple_of(pair * 128, 128), 128)
        keys = kv[:, lanes]
        queries = query_t[lanes, :]
        for second in range(2):
            scores = dot(keys, head_rows(queries, second)) + hidden[...]
            most = jnp.max(scores, axis=0, keepdims=True)
            powers = jnp.exp(scores - most)
            total = jnp.sum(powers, axis=0, keepdims=True)
            weights = (powers * (1.0 / total)).astype(jnp.bfloat16)
            chances[pair * 2 + second] = weights
            head = pl.multiple_of(pair * 128 + 64 * second, 64)
            values_t = kv_t[pl.ds(MODEL + head, 64), :]
            attended_t[pl.ds(head, 64), :] = dot(values_t, weights).astype(jnp.bfloat16)
        return carry

    lax.fori_loop(0, HEADS // 2, attend, 0)

    loads[2].wait()
    residual = (wide + dot(attended_t[...].T, w_out[...])).astype(jnp.bfloat16)
    residual_wide = residual.astype(jnp.float32)
    scale_mlp = inverse_rms(residual_wide)
    normed_mlp = (residual_wide * scale_mlp * gain_mlp[...]).astype(jnp.bfloat16)
    a2t[...] = normed_mlp.T
    loads[3].wait()
    mix = residual_wide
    d_normed = jnp.zeros((TOKENS, MODEL), jnp.float32)
    slope = float(np.sqrt(2 / np.pi))
    for part in range(4):
        units = slice(MODEL * part, MODEL * part + MODEL)
        up = dot(normed_mlp, w_up[:, units])
        square = up * up
        tanh = jnp.tanh(slope * up * (1.0 + 0.044715 * square))
        grown = 0.5 * (1.0 + tanh)
        active = (up * grown).astype(jnp.bfloat16)
        activated[:, units] = active
        mix = mix + dot(active, w_down[units])
        steep = grown + 0.5 * up * (1.0 - tanh * tanh) * (
            slope * (1.0 + 3 * 0.044715 * square)
        )
        d_up_part = (d_act[:, units] * steep).astype(jnp.bfloat16)
        d_up[:, units] = d_up_part
        d_normed = d_normed + dot_nt(d_up_part, w_up[:, units])
    mixed[...] = mix.astype(jnp.bfloat16)
    d_residual = (
        cotangent[...].astype(jnp.float32)
        + norm_back(residual_wide, scale_mlp, gain_mlp[...], d_normed)
    ).astype(jnp.bfloat16)
    d_att = dot_nt(d_residual, w_out[...]).astype(jnp.bfloat16)
    d_attended[...] = d_att
    d_attended_t[...] = d_att.T

    masks = lane_masks()

    def attend_back(pair, carry):
        lanes = pl.ds(pl.multiple_of(pair * 128, 128), 128)
        value_lanes = pl.ds(pl.multiple_of(MODEL + pair * 128, 128), 128)
        values = kv[:, value_lanes]
        upstream_t = d_attended_t[lanes, :]
        products = upstream_t.astype(jnp.float32) * attended_t[lanes, :].astype(jnp.float32)
        d_keys = d_values = 0.0
        for second in range(2):
            delta = jnp.sum(products[64 * second : 64 * second + 64], axis=0, keepdims=True)
            weights = chances[pair * 2 + second]
            d_prob = dot(values, head_rows(upstream_t, second))
            d_score = (weights.astype(jnp.float32) * (d_prob - delta)).astype(jnp.bfloat16)
            head = pl.multiple_of(pair * 128 + 64 * second, 64)
            d_query_t[pl.ds(head, 64), :] = (
                dot(kv_t[pl.ds(head, 64), :], d_score) * 0.125
            ).astype(jnp.bfloat16)
            d_keys = d_keys + dot(d_score, query[:, lanes] * masks[second])
            d_values = d_values + dot(weights, d_attended[:, lanes] * masks[second])
        d_kv_own[:, lanes] = d_keys[:TOKENS]
        d_kv_own[:, value_lanes] = d_values[:TOKENS]
        d_kv_far[:, lanes] = d_keys[TOKENS:].astype(jnp.bfloat16)
        d_kv_far[:, value_lanes] = d_values[TOKENS:].astype(jnp.bfloat16)
        return carry

    lax.fori_loop(0, HEADS // 2, attend_back, 0)

    sources = [d_kv_far.at[pl.ds(first, count)] for _, _, first, count in PIECES]
    back = halo.copies(sources, d_kv_in, 0, back_send, back_recv)
    for send in back:
        send.start()
    for send in back:
        send.wait_recv()
    for part in range(2):
        lanes = slice(MODEL * part, MODEL * part + MODEL)
        summed = d_kv_own[:, lanes] + dot(picks_t[...], d_kv_in[192:, lanes])
        top = d_kv_in[0:96, lanes].astype(jnp.float32)
        bottom = d_kv_in[96:192, lanes].astype(jnp.float32)
        summed = jnp.concatenate(
            [summed[:96] + top, summed[96:160], summed[160:] + bottom], axis=0
        )
        d_kv_own[:, lanes] = summed
    d_keys_values = d_kv_own[...].astype(jnp.bfloat16)
    d_query = d_query_t[...].T
    d_qkv_t[:MODEL] = d_query_t[...]
    d_qkv_t[MODEL:] = d_keys_values.T
    d_normed = dot_nt(d_query, w_qkv[:, :MODEL]) + dot_nt(d_keys_values, w_qkv[:, MODEL:])
    wide = tokens[...].astype(jnp.float32)
    d_tokens[...] = (
        d_residual.astype(jnp.float32)
        + norm_back(wide, inverse_rms(wide), gain_attn[...], d_normed)
    ).astype(jnp.bfloat16)
    for send in sends + back:
        send.wait_send()


def block(tokens, cotangent, gain_attn, gain_mlp, weights):
    key_place, picks = halo_tables()
    bf16, f32 = jnp.bfloat16, jnp.float32

    def out(*shape):
        return jax.ShapeDtypeStruct(shape, bf16)

    def vmem(kind, *shape):
        return pltpu.VMEM(shape, kind)

    in_vmem = pl.BlockSpec(memory_space=pltpu.VMEM)
    return pl.pallas_call(
        block_kernel,
        out_shape=[
            out(TOKENS, MODEL),
            out(TOKENS, MODEL),
            out(MODEL, TOKENS),
            out(MODEL, TOKENS),
            out(MODEL, TOKENS),
            out(TOKENS, HIDDEN),
            out(TOKENS, HIDDEN),
            out(3 * MODEL, TOKENS),
        ],
        in_specs=[in_vmem] * 7 + [pl.BlockSpec(memory_space=pl.ANY)] * 4,
        out_specs=[in_vmem] * 8,
        scratch_shapes=[
            vmem(bf16, MODEL, 3 * MODEL),
            vmem(bf16, MODEL, MODEL),
            vmem(bf16, MODEL, HIDDEN),
            vmem(bf16, HIDDEN, MODEL),
            vmem(bf16, KEYS, 2 * MODEL),
            vmem(bf16, 448, 2 * MODEL),
            vmem(bf16, 2 * MODEL, KEYS),
            vmem(bf16, TOKENS, MODEL),
            vmem(bf16, MODEL, TOKENS),
            vmem(bf16, HEADS, KEYS, TOKENS),
            vmem(f32, KEYS, TOKENS),
            vmem(bf16, MODEL, TOKENS),
            vmem(f32, TOKENS, HIDDEN),
            vmem(bf16, MODEL, TOKENS),
            vmem(bf16, TOKENS, MODEL),
            vmem(bf16, MODEL, TOKENS),
            vmem(f32, TOKENS, 2 * MODEL),
            vmem(bf16, 640, 2 * MODEL),
            vmem(bf16, 640, 2 * MODEL),
            pltpu.SemaphoreType.DMA((4,)),
            pltpu.SemaphoreType.DMA((8,)),
            pltpu.SemaphoreType.DMA((8,)),
            pltpu.SemaphoreType.DMA((8,)),
            pltpu.SemaphoreType.DMA((8,)),
        ],
        compiler_params=pltpu.CompilerParams(
            collective_id=1, has_side_effects=True, vmem_limit_bytes=56 * 2**20
        ),
    )(
        tokens,
        cotangent,
        gain_attn,
        gain_mlp,
        jnp.asarray(key_place),
        jnp.asarray(picks, bf16),
        jnp.asarray(picks.T, bf16),
        *weights,
    )


FLOWS = 6
CHIPS = 64


def gray_bits(position):
    high = position // 2
    return (high, (high + position % 2) % 2)


def my_place():
    row = lax.axis_index("rows")
    col = lax.axis_index("cols")
    core = col % 2
    x = col // 4
    y = (row // 4) * 2 + (col // 2) % 2
    z = row % 4
    return x, y, z, core


def device_at(x, y, z, core):
    return ((y // 2) * 4 + z, x * 4 + (y % 2) * 2 + core)


def link_bits(x, y, z):
    gx, gy, gz = gray_bits(x), gray_bits(y), gray_bits(z)
    return (gx[1], gy[1], gz[1], gx[0], gy[0], gz[0])


def link_partners(x, y, z, core):
    return (
        device_at(x + 1 - 2 * (x % 2), y, z, core),
        device_at(x, y + 1 - 2 * (y % 2), z, core),
        device_at(x, y, z + 1 - 2 * (z % 2), core),
        device_at(3 - x, y, z, core),
        device_at(x, 3 - y, z, core),
        device_at(x, y, 3 - z, core),
    )


def flow_slots(mine, theirs):
    differs = [(m + t) % 2 for m, t in zip(mine, theirs)]
    slots = []
    for flow in range(FLOWS):
        slot = 0
        for step in range(6):
            slot = slot * 2 + differs[(flow + step) % 6]
        slots.append(slot)
    return slots


class Channel:
    def __init__(self, own, core_in, mesh_in, sems, index, flow, total_at):
        self.own, self.core_in, self.mesh_in = own, core_in, mesh_in
        self.core_send, self.core_recv, self.mesh_send, self.mesh_recv = sems
        self.index, self.flow, self.total_at = index, flow, total_at

    def core_copy(self, sibling):
        return pltpu.make_async_remote_copy(
            src_ref=self.own.at[1, self.index],
            dst_ref=self.core_in.at[self.index],
            send_sem=self.core_send.at[self.index],
            recv_sem=self.core_recv.at[self.index],
            device_id=sibling,
            device_id_type=MESH,
        )

    def mesh_copy(self, step, partners):
        count = 32 >> step
        return pltpu.make_async_remote_copy(
            src_ref=self.own.at[0, self.index, pl.ds(count, count)],
            dst_ref=self.mesh_in.at[self.index, pl.ds(count, count)],
            send_sem=self.mesh_send.at[self.index, step],
            recv_sem=self.mesh_recv.at[self.index, step],
            device_id=partners[(self.flow + step) % 6],
            device_id_type=MESH,
        )

    def add(self, source, source_first, first, count):
        own, index = self.own, self.index
        rows, lanes = own.shape[3], own.shape[4]
        chunk = min(count, max(1, 128 // rows))

        def body(turn, carry):
            at = first + turn * chunk
            own[0, index, pl.ds(at, chunk)] = (
                own[0, index, pl.ds(at, chunk)]
                + source[index, pl.ds(source_first + turn * chunk, chunk)]
            )
            return carry

        lax.fori_loop(0, count // chunk, body, 0)

    def after_core(self, partners, sibling):
        self.core_copy(sibling).wait_recv()
        self.add(self.core_in, 32, 32, 32)
        self.mesh_copy(0, partners).start()
        self.add(self.core_in, 0, 0, 32)

    def after_mesh(self, step, partners, total):
        self.mesh_copy(step, partners).wait_recv()
        count = 32 >> step
        if step < 5:
            half = count // 2
            self.add(self.mesh_in, count + half, half, half)
            self.mesh_copy(step + 1, partners).start()
            self.add(self.mesh_in, count, 0, half)
        else:
            rows = self.own.shape[3]
            total[pl.ds(self.total_at, rows)] = self.own[0, self.index, 0].astype(
                jnp.float32
            ) + self.mesh_in[self.index, 1].astype(jnp.float32)

    def finish(self, partners, sibling):
        self.core_copy(sibling).wait_send()
        for step in range(6):
            self.mesh_copy(step, partners).wait_send()


def up_payload(group, mine, core, a2t, b2, a3t, b3, ubuf):
    z = group % 4
    y_hi = group // 4
    left = a2t[pl.ds(pl.multiple_of(96 * group, 32), 96), :]
    lane = lax.broadcasted_iota(jnp.int32, (96, 128), 1)
    for c in range(8):
        x, y = c // 2, y_hi * 2 + c % 2
        slots = flow_slots(mine, link_bits(x, y, z))
        up = jnp.dot(
            left, b2[:, 384 * c : 384 * c + 384], preferred_element_type=jnp.float32
        )
        q, odd = c % 4, c // 4
        tile = 3 * group
        down_left = a3t[192 * q : 192 * q + 192, :]
        main_at = pl.multiple_of((tile + 2 * odd) * 128, 128)
        half_at = pl.multiple_of((tile + 1) * 128, 128)
        main = jnp.dot(
            down_left, b3[:, pl.ds(main_at, 128)], preferred_element_type=jnp.float32
        )
        half = jnp.dot(
            down_left, b3[:, pl.ds(half_at, 128)], preferred_element_type=jnp.float32
        )
        first, second = half[:96], half[96:]
        if odd:
            packed = jnp.where(lane < 64, pltpu.roll(first, 64, 1), second)
        else:
            packed = jnp.where(lane < 64, first, pltpu.roll(second, 64, 1))
        pieces = [
            up[:, :128],
            up[:, 128:256],
            up[:, 256:],
            main[:96],
            main[96:],
            packed,
        ]
        for flow, piece in enumerate(pieces):
            piece = piece.astype(jnp.bfloat16)
            for half_at in range(2):
                ubuf[(core + half_at) % 2, flow, slots[flow]] = piece[
                    48 * half_at : 48 * half_at + 48
                ]


def qkv_payload(group, mine, core, a1t, d_qkv_t, qbuf, rbuf):
    z = group % 4
    y_hi = group // 4
    left = a1t[pl.ds(pl.multiple_of(96 * group, 32), 96), :]
    blank = jnp.zeros((16, 32), jnp.bfloat16)
    for c in range(8):
        x, y = c // 2, y_hi * 2 + c % 2
        slots = flow_slots(mine, link_bits(x, y, z))
        main = dot_nt(left, d_qkv_t[288 * c : 288 * c + 256]).astype(jnp.bfloat16)
        rest = dot_nt(d_qkv_t[288 * c + 256 : 288 * c + 288], left).astype(jnp.bfloat16)
        for half in range(2):
            for flow in range(FLOWS):
                qbuf[(core + half) % 2, flow, slots[flow]] = main[
                    16 * flow : 16 * flow + 16, 128 * half : 128 * half + 128
                ]
            rbuf[(core + half) % 2, 0, slots[0]] = jnp.concatenate(
                [rest[16 * half : 16 * half + 16], blank], axis=1
            )


def grads_kernel(
    a2t,
    b2,
    a3t,
    b3,
    a1t,
    d_qkv_t,
    out,
    ubuf,
    ucore,
    umesh,
    qbuf,
    qcore,
    qmesh,
    rbuf,
    rcore,
    rmesh,
    total,
    other,
    *sems,
):
    x, y, z, core = my_place()
    sibling = device_at(x, y, z, 1 - core)
    partners = link_partners(x, y, z, core)
    mine = link_bits(x, y, z)
    barrier = pltpu.get_barrier_semaphore()
    for partner in (sibling,) + partners:
        pl.semaphore_signal(barrier, inc=1, device_id=partner, device_id_type=MESH)
    pl.semaphore_wait(barrier, 7)

    up = [
        Channel(ubuf, ucore, umesh, sems[0:4], flow, flow, 48 * flow)
        for flow in range(FLOWS)
    ]
    qkv = [
        Channel(qbuf, qcore, qmesh, sems[4:8], flow, flow, 288 + 16 * flow)
        for flow in range(FLOWS)
    ]
    qkv.append(Channel(rbuf, rcore, rmesh, sems[8:12], 0, 0, 384))
    channels = up + qkv

    def up_body(group, carry):
        up_payload(group, mine, core, a2t, b2, a3t, b3, ubuf)
        return carry

    lax.fori_loop(0, 8, up_body, 0)
    for channel in up:
        channel.core_copy(sibling).start()

    def qkv_body(group, carry):
        qkv_payload(group, mine, core, a1t, d_qkv_t, qbuf, rbuf)
        return carry

    lax.fori_loop(0, 8, qkv_body, 0)
    for channel in qkv:
        channel.core_copy(sibling).start()
    for channel in channels:
        channel.after_core(partners, sibling)
    for step in range(6):
        for channel in channels:
            channel.after_mesh(step, partners, total)
    last = pltpu.make_async_remote_copy(
        src_ref=total,
        dst_ref=other,
        send_sem=sems[12],
        recv_sem=sems[13],
        device_id=sibling,
        device_id_type=MESH,
    )
    last.start()
    last.wait_recv()
    own_first = core == 0
    out[0] = jnp.where(own_first, total[...], other[...])
    out[1] = jnp.where(own_first, other[...], total[...])
    for channel in channels:
        channel.finish(partners, sibling)
    last.wait_send()


def summed_grads(a2t, b2, a3t, b3, a1t, d_qkv_t):
    def set_of(count, rows):
        return [
            pltpu.VMEM((2, count, CHIPS, rows, 128), jnp.bfloat16),
            pltpu.VMEM((count, CHIPS, rows, 128), jnp.bfloat16),
            pltpu.VMEM((count, CHIPS, rows, 128), jnp.bfloat16),
        ]

    def sems_of(count):
        return [
            pltpu.SemaphoreType.DMA((count,)),
            pltpu.SemaphoreType.DMA((count,)),
            pltpu.SemaphoreType.DMA((count, 6)),
            pltpu.SemaphoreType.DMA((count, 6)),
        ]

    return pl.pallas_call(
        grads_kernel,
        out_shape=jax.ShapeDtypeStruct((2, 400, 128), jnp.float32),
        in_specs=[pl.BlockSpec(memory_space=pltpu.VMEM)] * 6,
        out_specs=pl.BlockSpec(memory_space=pltpu.VMEM),
        scratch_shapes=set_of(6, 48)
        + set_of(6, 16)
        + set_of(1, 16)
        + [pltpu.VMEM((400, 128), jnp.float32)] * 2
        + sems_of(6)
        + sems_of(6)
        + sems_of(1)
        + [pltpu.SemaphoreType.DMA, pltpu.SemaphoreType.DMA],
        compiler_params=pltpu.CompilerParams(
            collective_id=0, has_side_effects=True, vmem_limit_bytes=56 * 2**20
        ),
    )(a2t, b2, a3t, b3, a1t, d_qkv_t)


def owned_blocks(summed, core, part_odd):
    def rows_of(first):
        return jnp.concatenate(
            [summed[0, first : first + 48], summed[1, first : first + 48]], axis=0
        )

    left, middle, right = rows_of(0), rows_of(48), rows_of(96)
    up = jnp.where(
        core == 0,
        jnp.concatenate([left, middle[:, :64]], axis=1),
        jnp.concatenate([middle[:, 64:], right], axis=1),
    )
    main = jnp.where(core == 0, rows_of(144), rows_of(192))
    packed = rows_of(240)
    half = jnp.where(core == 0, packed[:, :64], packed[:, 64:])
    down = jnp.where(
        part_odd == 1,
        jnp.concatenate([half, main], axis=1),
        jnp.concatenate([main, half], axis=1),
    )
    first, second = summed[0, 288:384], summed[1, 288:384]
    rest = jnp.concatenate([summed[0, 384:400], summed[1, 384:400]], axis=0).T[:96]
    qkv = jnp.where(
        core == 0,
        jnp.concatenate([first, second[:, :16]], axis=1),
        jnp.concatenate([second[:, 16:], rest], axis=1),
    )
    return up, down, qkv


def accumulate(left_stat, right_stat, gradient, scaling):
    scaled = gradient * scaling
    new_left = (
        left_stat
        + jnp.einsum("brc,bsc->brs", scaled, scaled, precision=lax.Precision.HIGHEST)
        / scaled.shape[2]
    )
    new_right = (
        right_stat
        + jnp.einsum("brc,brs->bcs", scaled, scaled, precision=lax.Precision.HIGHEST)
        / scaled.shape[1]
    )
    return (new_left, new_right)


def on_device(
    tokens,
    cotangent,
    gain_attn,
    gain_mlp,
    weight_qkv,
    weight_out,
    weight_up,
    weight_down,
    left_qkv,
    right_qkv,
    left_up,
    right_up,
    left_down,
    right_down,
):
    scaling = float(TOKENS * lax.axis_size("rows") * lax.axis_size("cols")) ** (-0.5)
    mixed, d_tokens, a1t, a2t, a3t, d_up, activated, d_qkv_t = block(
        tokens.reshape(TOKENS, MODEL),
        cotangent.reshape(TOKENS, MODEL),
        gain_attn[None],
        gain_mlp[None],
        (weight_qkv, weight_out, weight_up, weight_down),
    )
    summed = summed_grads(a2t, d_up, a3t, activated, a1t, d_qkv_t)
    col = lax.axis_index("cols")
    up_owned, down_owned, qkv_owned = owned_blocks(summed, col % 2, (col // 8) % 2)
    new_left_qkv, new_right_qkv = accumulate(left_qkv, right_qkv, qkv_owned[None], scaling)
    new_left_up, new_right_up = accumulate(left_up, right_up, up_owned[None], scaling)
    new_left_down, new_right_down = accumulate(
        left_down, right_down, down_owned.T[None], scaling
    )
    return (
        mixed.reshape(TILE, TILE, MODEL),
        d_tokens.reshape(TILE, TILE, MODEL),
        new_left_qkv,
        new_right_qkv,
        new_left_up,
        new_right_up,
        new_left_down,
        new_right_down,
    )


def solution(mesh):
    in_specs = (
        P("rows", "cols", None),
        P("rows", "cols", None),
        P(),
        P(),
        P(),
        P(),
        P(),
        P(),
        P(("rows", "cols"), None, None),
        P(("rows", "cols"), None, None),
        P(("rows", "cols"), None, None),
        P(("rows", "cols"), None, None),
        P(("rows", "cols"), None, None),
        P(("rows", "cols"), None, None),
    )
    out_specs = (
        P("rows", "cols", None),
        P("rows", "cols", None),
        P(("rows", "cols"), None, None),
        P(("rows", "cols"), None, None),
        P(("rows", "cols"), None, None),
        P(("rows", "cols"), None, None),
        P(("rows", "cols"), None, None),
        P(("rows", "cols"), None, None),
    )
    return jax.shard_map(
        on_device, mesh=mesh, in_specs=in_specs, out_specs=out_specs, check_vma=False
    )
```

```python
import functools

import jax
import jax.numpy as jnp
import numpy as np
from jax import lax
from jax.experimental import pallas as pl
from jax.experimental.pallas import tpu as pltpu
from jax.sharding import PartitionSpec as P

HEADS = 12
PAIRS = 6
MODEL = 768
HIDDEN = 3072
TILE = 16
TOKENS = TILE * TILE
FLOWS = 6
CHIPS = 64
KEYS = 896
TOP, BOTTOM, LEFT, LEFT_CORNERS, RIGHT, RIGHT_CORNERS, BLANK = 256, 352, 448, 544, 640, 736, 832

epsilon = 1e-06
window_half = 6
window_span = 13
MESH = pl.DeviceIdType.MESH


def halo_tables():
    sides = np.zeros((192, TOKENS), np.float32)
    corners = np.zeros((192, 192), np.float32)
    for side, first in enumerate((0, TILE - 6)):
        for r in range(TILE):
            for c in range(6):
                sides[96 * side + r * 6 + c, r * TILE + first + c] = 1
        for band in range(2):
            for r in range(6):
                for c in range(6):
                    at = 48 * band + r * 6 + c
                    corners[96 * side + at, 96 * band + r * TILE + first + c] = 1
    return sides, corners


def key_places():
    key = lax.broadcasted_iota(jnp.int32, (KEYS, 1), 0)
    band = jnp.where(key < TOP, key, key - jnp.where(key < BOTTOM, TOP, BOTTOM))
    shift = jnp.where(key < TOP, 0, jnp.where(key < BOTTOM, -6, TILE))
    band_row, band_col = band // TILE + shift, band % TILE
    on_right = key >= RIGHT
    side = key - jnp.where(on_right, RIGHT, LEFT)
    corner = side - 96
    in_corner = corner >= 0
    low = corner >= 48
    at = jnp.where(in_corner, corner - jnp.where(low, 48, 0), side)
    sixth = (at * 171) >> 10
    side_row = sixth + jnp.where(in_corner, jnp.where(low, TILE, -6), 0)
    side_col = at - 6 * sixth + jnp.where(on_right, TILE, -6)
    unused = (key >= BLANK) | (in_corner & (at >= 36))
    in_band = key < LEFT
    key_row = jnp.where(in_band, band_row, jnp.where(unused, -1000, side_row))
    return key_row, jnp.where(in_band, band_col, side_col)


def dot(left, right):
    return jnp.dot(left, right, preferred_element_type=jnp.float32)


def dot_nt(left, right):
    return lax.dot_general(
        left, right, (((1,), (1,)), ((), ())), preferred_element_type=jnp.float32
    )


def inverse_rms(wide):
    return lax.rsqrt(jnp.mean(wide * wide, axis=-1, keepdims=True) + epsilon)


def norm_back(wide, scale, gain, upstream):
    scaled = upstream * gain
    return scale * scaled - wide * (
        scale * scale * scale * jnp.mean(wide * scaled, axis=-1, keepdims=True)
    )


def head_rows(pair_rows, second):
    blank = jnp.zeros((64, pair_rows.shape[1]), pair_rows.dtype)
    if second:
        return jnp.concatenate([blank, pair_rows[64:]], axis=0)
    return jnp.concatenate([pair_rows[:64], blank], axis=0)


def lane_masks():
    lane = lax.broadcasted_iota(jnp.int32, (1, 128), 1)
    low = jnp.where(lane < 64, 1.0, 0.0)
    return low.astype(jnp.bfloat16), (1.0 - low).astype(jnp.bfloat16)


def gray_bits(position):
    high = position // 2
    return (high, (high + position % 2) % 2)


def my_place():
    row = lax.axis_index("rows")
    col = lax.axis_index("cols")
    core = col % 2
    x = col // 4
    y = (row // 4) * 2 + (col // 2) % 2
    z = row % 4
    return x, y, z, core


def device_at(x, y, z, core):
    return ((y // 2) * 4 + z, x * 4 + (y % 2) * 2 + core)


def link_bits(x, y, z):
    gx, gy, gz = gray_bits(x), gray_bits(y), gray_bits(z)
    return (gx[1], gy[1], gz[1], gx[0], gy[0], gz[0])


def link_partners(x, y, z, core):
    return (
        device_at(x + 1 - 2 * (x % 2), y, z, core),
        device_at(x, y + 1 - 2 * (y % 2), z, core),
        device_at(x, y, z + 1 - 2 * (z % 2), core),
        device_at(3 - x, y, z, core),
        device_at(x, 3 - y, z, core),
        device_at(x, y, 3 - z, core),
    )


def flow_slots(mine, theirs):
    differs = [(m + t) % 2 for m, t in zip(mine, theirs)]
    slots = []
    for flow in range(FLOWS):
        slot = 0
        for step in range(6):
            slot = slot * 2 + differs[(flow + step) % 6]
        slots.append(slot)
    return slots


class Channel:
    def __init__(self, own, inbox, sems, index, flow, total_at):
        self.own, self.inbox = own, inbox
        self.core_send, self.core_recv, self.mesh_send, self.mesh_recv, self.credit = sems
        self.index, self.flow, self.total_at = index, flow, total_at

    def core_copy(self, sibling):
        return pltpu.make_async_remote_copy(
            src_ref=self.own.at[1, self.index],
            dst_ref=self.inbox.at[self.index],
            send_sem=self.core_send.at[self.index],
            recv_sem=self.core_recv.at[self.index],
            device_id=sibling,
            device_id_type=MESH,
        )

    def mesh_copy(self, step, partners):
        count = 32 >> step
        return pltpu.make_async_remote_copy(
            src_ref=self.own.at[0, self.index, pl.ds(count, count)],
            dst_ref=self.inbox.at[self.index, pl.ds(count, count)],
            send_sem=self.mesh_send.at[self.index, step],
            recv_sem=self.mesh_recv.at[self.index, step],
            device_id=partners[(self.flow + step) % 6],
            device_id_type=MESH,
        )

    def add(self, source_first, first, count):
        own, inbox, index = self.own, self.inbox, self.index
        rows = own.shape[3]
        chunk = min(count, max(1, 128 // rows))

        def body(turn, carry):
            at = first + turn * chunk
            own[0, index, pl.ds(at, chunk)] = (
                own[0, index, pl.ds(at, chunk)]
                + inbox[index, pl.ds(source_first + turn * chunk, chunk)]
            )
            return carry

        lax.fori_loop(0, count // chunk, body, 0)

    def after_core(self, partners, sibling):
        self.core_copy(sibling).wait_recv()
        self.add(0, 0, 64)
        for step in range(6):
            pl.semaphore_signal(
                self.credit.at[self.index, step],
                inc=1,
                device_id=partners[(self.flow + step) % 6],
                device_id_type=MESH,
            )

    def send_mesh(self, step, partners):
        pl.semaphore_wait(self.credit.at[self.index, step], 1)
        self.mesh_copy(step, partners).start()

    def after_mesh(self, step, partners, total):
        self.mesh_copy(step, partners).wait_recv()
        count = 32 >> step
        if step < 5:
            half = count // 2
            self.add(count + half, half, half)
            self.send_mesh(step + 1, partners)
            self.add(count, 0, half)
        else:
            rows = self.own.shape[3]
            total[pl.ds(self.total_at, rows)] = self.own[0, self.index, 0].astype(
                jnp.float32
            ) + self.inbox[self.index, 1].astype(jnp.float32)

    def finish(self, partners, sibling):
        self.core_copy(sibling).wait_send()
        for step in range(6):
            self.mesh_copy(step, partners).wait_send()


def up_payload(group, mine, core, a2t, b2, a3t, b3, ubuf):
    z = group % 4
    y_hi = group // 4
    left = a2t[pl.ds(pl.multiple_of(96 * group, 32), 96), :]
    lane = lax.broadcasted_iota(jnp.int32, (96, 128), 1)
    for c in range(8):
        x, y = c // 2, y_hi * 2 + c % 2
        slots = flow_slots(mine, link_bits(x, y, z))
        up = jnp.dot(
            left, b2[:, 384 * c : 384 * c + 384], preferred_element_type=jnp.float32
        )
        q, odd = c % 4, c // 4
        tile = 3 * group
        down_left = a3t[192 * q : 192 * q + 192, :]
        main_at = pl.multiple_of((tile + 2 * odd) * 128, 128)
        half_at = pl.multiple_of((tile + 1) * 128, 128)
        main = jnp.dot(
            down_left, b3[:, pl.ds(main_at, 128)], preferred_element_type=jnp.float32
        )
        half = jnp.dot(
            down_left, b3[:, pl.ds(half_at, 128)], preferred_element_type=jnp.float32
        )
        first, second = half[:96], half[96:]
        if odd:
            packed = jnp.where(lane < 64, pltpu.roll(first, 64, 1), second)
        else:
            packed = jnp.where(lane < 64, first, pltpu.roll(second, 64, 1))
        pieces = [
            up[:, :128],
            up[:, 128:256],
            up[:, 256:],
            main[:96],
            main[96:],
            packed,
        ]
        for flow, piece in enumerate(pieces):
            piece = piece.astype(jnp.bfloat16)
            for half_at in range(2):
                ubuf[(core + half_at) % 2, flow, slots[flow]] = piece[
                    48 * half_at : 48 * half_at + 48
                ]


def qkv_payload(group, mine, core, a1t, d_qkv_t, qbuf, rbuf):
    z = group % 4
    y_hi = group // 4
    left = a1t[pl.ds(pl.multiple_of(96 * group, 32), 96), :]
    blank = jnp.zeros((16, 32), jnp.bfloat16)
    for c in range(8):
        x, y = c // 2, y_hi * 2 + c % 2
        slots = flow_slots(mine, link_bits(x, y, z))
        main = dot_nt(left, d_qkv_t[288 * c : 288 * c + 256]).astype(jnp.bfloat16)
        rest = dot_nt(d_qkv_t[288 * c + 256 : 288 * c + 288], left).astype(jnp.bfloat16)
        for half in range(2):
            for flow in range(FLOWS):
                qbuf[(core + half) % 2, flow, slots[flow]] = main[
                    16 * flow : 16 * flow + 16, 128 * half : 128 * half + 128
                ]
            rbuf[(core + half) % 2, 0, slots[0]] = jnp.concatenate(
                [rest[16 * half : 16 * half + 16], blank], axis=1
            )


def exact(left, right):
    return jnp.dot(
        left, right, precision=lax.Precision.HIGHEST, preferred_element_type=jnp.float32
    )


def halves(total, other, own_first, first, rows):
    mine, theirs = total[first : first + rows], other[first : first + rows]
    return jnp.concatenate(
        [jnp.where(own_first, mine, theirs), jnp.where(own_first, theirs, mine)], axis=0
    )


def up_blocks(total, other, core, part_odd):
    first, odd = core == 0, part_odd == 1
    left, middle, right, main_0, main_1, packed = [
        halves(total, other, first, 48 * at, 48) for at in range(6)
    ]
    up = jnp.where(
        first,
        jnp.concatenate([left, middle], axis=1),
        pltpu.roll(jnp.concatenate([middle, right], axis=1), 192, 1),
    )[:, :192]
    main = jnp.where(first, main_0, main_1)
    turned = pltpu.roll(packed, 64, 1)
    low, high = jnp.where(first, packed, turned), jnp.where(first, turned, packed)
    down = jnp.where(
        odd,
        pltpu.roll(jnp.concatenate([high, main], axis=1), 192, 1),
        jnp.concatenate([main, low], axis=1),
    )[:, :192]
    return up, down


def qkv_block(total, other, core):
    first = core == 0
    both = [
        jnp.where(first, total[0:96], other[0:96]),
        jnp.where(first, other[0:96], total[0:96]),
    ]
    rest = halves(total, other, first, 96, 16)
    rest = jnp.concatenate([rest, jnp.zeros((96, 128), jnp.float32)], axis=0).T[:96]
    return jnp.where(
        first,
        jnp.concatenate(both, axis=1),
        pltpu.roll(jnp.concatenate([both[1], rest], axis=1), 240, 1),
    )[:, :144]


def exchange(source, target, sems, device):
    return pltpu.make_async_remote_copy(
        src_ref=source,
        dst_ref=target,
        send_sem=sems[0],
        recv_sem=sems[1],
        device_id=device,
        device_id_type=MESH,
    )


def whole_kernel(scaling, *refs):
    refs = list(refs)

    def take(count):
        taken = refs[:count]
        del refs[:count]
        return taken

    tokens, cotangent, gain_attn, gain_mlp, sides, corners, sides_t, corners_t = take(8)
    left_qkv, right_qkv, left_up, right_up, left_down, right_down = take(6)
    weight_refs = take(4)
    mixed, d_tokens = take(2)
    new_left_qkv, new_right_qkv, new_left_up, new_right_up, new_left_down, new_right_down = take(6)
    w_qkv, w_out, w_up, w_down = take(4)
    kv, query, query_t, chances, hidden, attended_t = take(6)
    d_attended, d_attended_t, d_kv_own, d_kv_far, d_side_in, d_band, d_band_in = take(7)
    a1t, a2t, a3t, d_up, activated, d_qkv_t = take(6)
    ubuf, ubox, qbuf, qbox, rbuf, rbox = take(6)
    total_up, other_up, total_qkv, other_qkv = take(4)
    weight_sems, kv_send, kv_recv, back_send, back_recv = take(5)
    up_sems, qkv_sems, rest_sems = take(5), take(5), take(5)
    last_sems = take(4)

    packed = d_kv_far
    row, col = lax.axis_index("rows"), lax.axis_index("cols")
    rows, cols = lax.axis_size("rows"), lax.axis_size("cols")
    above, below = ((row + rows - 1) % rows, col), ((row + 1) % rows, col)
    to_left, to_right = (row, (col + cols - 1) % cols), (row, (col + 1) % cols)
    x, y, z, core = my_place()
    sibling = device_at(x, y, z, 1 - core)
    partners = link_partners(x, y, z, core)
    mine = link_bits(x, y, z)
    loads = [
        pltpu.make_async_copy(weight_refs[at], place, weight_sems.at[at])
        for at, place in ((0, w_qkv), (3, w_down), (1, w_out), (2, w_up))
    ]
    for load in loads:
        load.start()
    barrier = pltpu.get_barrier_semaphore()
    for place in (above, below, to_left, to_right, sibling) + partners:
        pl.semaphore_signal(barrier, inc=1, device_id=place, device_id_type=MESH)

    def lanes_of(pair):
        return pl.ds(pl.multiple_of(pair * 256, 256), 256)

    def copy_of(source, target, send, recv, at, device):
        return pltpu.make_async_remote_copy(
            src_ref=source,
            dst_ref=target,
            send_sem=send.at[at],
            recv_sem=recv.at[at],
            device_id=device,
            device_id_type=MESH,
        )

    def near_copies(pair, first=0, last=4):
        lanes = lanes_of(pair)
        routes = (
            (kv.at[pl.ds(0, 96), lanes], BOTTOM, above),
            (kv.at[pl.ds(TOKENS - 96, 96), lanes], TOP, below),
            (packed.at[pl.ds(0, 96), lanes], RIGHT, to_left),
            (packed.at[pl.ds(96, 96), lanes], LEFT, to_right),
        )
        return [
            copy_of(source, kv.at[pl.ds(place, 96), lanes], kv_send, kv_recv, pair * 6 + at, device)
            for at, (source, place, device) in list(enumerate(routes))[first:last]
        ]

    def corner_copies(pair, first=0, last=4):
        lanes = lanes_of(pair)
        routes = (
            (packed.at[pl.ds(192, 96), lanes], RIGHT_CORNERS, to_left),
            (packed.at[pl.ds(288, 96), lanes], LEFT_CORNERS, to_right),
        )
        return [
            copy_of(
                source, kv.at[pl.ds(place, 96), lanes], kv_send, kv_recv, pair * 6 + 4 + at, device
            )
            for at, (source, place, device) in list(enumerate(routes))[first:last]
        ]

    def side_copies(pair, first=0, last=4):
        lanes = lanes_of(pair)
        routes = (
            (d_kv_far.at[pl.ds(192, 192), lanes], 192, to_left),
            (d_kv_far.at[pl.ds(384, 192), lanes], 0, to_right),
        )
        return [
            copy_of(
                source, d_side_in.at[pl.ds(place, 192), lanes], back_send, back_recv, pair * 4 + at, device
            )
            for at, (source, place, device) in list(enumerate(routes))[first:last]
        ]

    def band_copies(pair, first=0, last=4):
        lanes = lanes_of(pair)
        routes = (
            (d_band.at[pl.ds(0, 96), lanes], 96, above),
            (d_band.at[pl.ds(96, 96), lanes], 0, below),
        )
        return [
            copy_of(
                source, d_band_in.at[pl.ds(place, 96), lanes], back_send, back_recv, pair * 4 + 2 + at, device
            )
            for at, (source, place, device) in list(enumerate(routes))[first:last]
        ]

    wide = tokens[...].astype(jnp.float32)
    normed_attn = (wide * inverse_rms(wide) * gain_attn[...]).astype(jnp.bfloat16)
    loads[0].wait()
    pl.semaphore_wait(barrier, 11)
    for pair in range(PAIRS):
        for part in range(2):
            at = MODEL * (1 + part) + 128 * pair
            kv[:TOKENS, 256 * pair + 128 * part : 256 * pair + 128 * part + 128] = dot(
                normed_attn, w_qkv[:, at : at + 128]
            ).astype(jnp.bfloat16)
        lanes = slice(256 * pair, 256 * pair + 256)
        packed[:192, lanes] = dot(sides[...], kv[:TOKENS, lanes]).astype(jnp.bfloat16)
        for copy in near_copies(pair):
            copy.start()
    kv[BLANK:] = jnp.zeros((KEYS - BLANK, 2 * MODEL), jnp.bfloat16)

    own_query = dot(normed_attn, w_qkv[:, :MODEL]).astype(jnp.bfloat16)
    own_query = (own_query.astype(jnp.float32) * 0.125).astype(jnp.bfloat16)
    query[...] = own_query
    query_t[...] = own_query.T
    a1t[...] = normed_attn.T
    a3t[...] = cotangent[...].T

    at = lax.broadcasted_iota(jnp.int32, (1, TOKENS), 1)
    row_first = jnp.clip(row * TILE + at // TILE - window_half, 0, rows * TILE - window_span)
    col_first = jnp.clip(col * TILE + at % TILE - window_half, 0, cols * TILE - window_span)
    key_row, key_col = key_places()
    key_row, key_col = row * TILE + key_row, col * TILE + key_col
    visible = (
        (key_row >= row_first)
        & (key_row < row_first + window_span)
        & (key_col >= col_first)
        & (key_col < col_first + window_span)
    )
    hidden[...] = jnp.where(visible, 0.0, -1e30)

    def relay(pair):
        lanes = lanes_of(pair)
        for copy in near_copies(pair, 0, 2):
            copy.wait_recv()
        packed[192:384, lanes] = dot(corners[...], kv[TOP:LEFT, lanes]).astype(jnp.bfloat16)
        for copy in corner_copies(pair):
            copy.start()

    relay(0)

    def attend(pair, carry):
        @pl.when(pair < PAIRS - 1)
        def _():
            relay(pair + 1)

        for copy in near_copies(pair, 2) + corner_copies(pair):
            copy.wait_recv()
        keys = kv[:, pl.ds(pl.multiple_of(pair * 256, 256), 128)]
        values_t = kv[:, pl.ds(pl.multiple_of(pair * 256 + 128, 128), 128)].T
        queries = query_t[pl.ds(pl.multiple_of(pair * 128, 128), 128), :]
        for second in range(2):
            scores = dot(keys, head_rows(queries, second)) + hidden[...]
            most = jnp.max(scores, axis=0, keepdims=True)
            powers = jnp.exp(scores - most)
            total = jnp.sum(powers, axis=0, keepdims=True)
            weights = (powers * (1.0 / total)).astype(jnp.bfloat16)
            chances[pair * 2 + second] = weights
            head = pl.multiple_of(pair * 128 + 64 * second, 64)
            attended_t[pl.ds(head, 64), :] = dot(
                values_t[64 * second : 64 * second + 64], weights
            ).astype(jnp.bfloat16)
        return carry

    lax.fori_loop(0, PAIRS, attend, 0)

    for load in loads[1:]:
        load.wait()
    wide = tokens[...].astype(jnp.float32)
    residual = (wide + dot(attended_t[...].T, w_out[...])).astype(jnp.bfloat16)
    residual_wide = residual.astype(jnp.float32)
    scale_mlp = inverse_rms(residual_wide)
    normed_mlp = (residual_wide * scale_mlp * gain_mlp[...]).astype(jnp.bfloat16)
    a2t[...] = normed_mlp.T
    mix = residual_wide
    d_normed = jnp.zeros((TOKENS, MODEL), jnp.float32)
    slope = float(np.sqrt(2 / np.pi))
    for part in range(6):
        units = slice(512 * part, 512 * part + 512)
        up = dot(normed_mlp, w_up[:, units])
        d_act = dot_nt(cotangent[...], w_down[units])
        square = up * up
        tanh = jnp.tanh(slope * up * (1.0 + 0.044715 * square))
        grown = 0.5 * (1.0 + tanh)
        active = (up * grown).astype(jnp.bfloat16)
        activated[:, units] = active
        mix = mix + dot(active, w_down[units])
        steep = grown + 0.5 * up * (1.0 - tanh * tanh) * (
            slope * (1.0 + 3 * 0.044715 * square)
        )
        d_up_part = (d_act * steep).astype(jnp.bfloat16)
        d_up[:, units] = d_up_part
        d_normed = d_normed + dot_nt(d_up_part, w_up[:, units])
    mixed[...] = mix.astype(jnp.bfloat16)

    up_channels = [
        Channel(ubuf, ubox, up_sems, flow, flow, 48 * flow) for flow in range(FLOWS)
    ]
    qkv_channels = [
        Channel(qbuf, qbox, qkv_sems, flow, flow, 16 * flow) for flow in range(FLOWS)
    ] + [Channel(rbuf, rbox, rest_sems, 0, 0, 96)]

    def up_body(group, carry):
        up_payload(group, mine, core, a2t, d_up, a3t, activated, ubuf)
        return carry

    lax.fori_loop(0, 8, up_body, 0)
    for channel in up_channels:
        channel.core_copy(sibling).start()

    d_residual = (
        cotangent[...].astype(jnp.float32)
        + norm_back(residual_wide, scale_mlp, gain_mlp[...], d_normed)
    ).astype(jnp.bfloat16)
    d_tokens[...] = d_residual
    d_att = dot_nt(d_residual, w_out[...]).astype(jnp.bfloat16)
    d_attended[...] = d_att
    d_attended_t[...] = d_att.T

    masks = lane_masks()
    for pair in range(PAIRS):
        for copy in near_copies(pair, 2) + corner_copies(pair):
            copy.wait_send()

    def relay_back(pair):
        lanes = lanes_of(pair)
        for copy in side_copies(pair):
            copy.wait_recv()
        own, far = d_side_in[0:96, lanes], d_side_in[96:192, lanes]
        own = jnp.concatenate([own, d_side_in[192:288, lanes]], axis=0)
        far = jnp.concatenate([far, d_side_in[288:384, lanes]], axis=0)
        d_band[:, lanes] = (
            d_kv_far[0:192, lanes].astype(jnp.float32) + dot(corners_t[...], far)
        ).astype(jnp.bfloat16)
        for copy in band_copies(pair):
            copy.start()
        d_kv_own[:, lanes] = d_kv_own[:, lanes] + dot(sides_t[...], own)

    def attend_back(pair, carry):
        key_lanes = pl.ds(pl.multiple_of(pair * 256, 256), 128)
        value_lanes = pl.ds(pl.multiple_of(pair * 256 + 128, 128), 128)
        lanes = pl.ds(pl.multiple_of(pair * 128, 128), 128)
        values = kv[:, value_lanes]
        keys_t = kv[:, key_lanes].T
        upstream_t = d_attended_t[lanes, :]
        products = upstream_t.astype(jnp.float32) * attended_t[lanes, :].astype(jnp.float32)
        d_keys = d_values = 0.0
        for second in range(2):
            delta = jnp.sum(products[64 * second : 64 * second + 64], axis=0, keepdims=True)
            weights = chances[pair * 2 + second]
            d_prob = dot(values, head_rows(upstream_t, second))
            d_score = (weights.astype(jnp.float32) * (d_prob - delta)).astype(jnp.bfloat16)
            head = pl.multiple_of(pair * 128 + 64 * second, 64)
            d_qkv_t[pl.ds(head, 64), :] = (
                dot(keys_t[64 * second : 64 * second + 64], d_score) * 0.125
            ).astype(jnp.bfloat16)
            d_keys = d_keys + dot(d_score, query[:, lanes] * masks[second])
            d_values = d_values + dot(weights, d_attended[:, lanes] * masks[second])
        d_kv_own[:, key_lanes] = d_keys[:TOKENS]
        d_kv_own[:, value_lanes] = d_values[:TOKENS]
        d_kv_far[:, key_lanes] = d_keys[TOP:BLANK].astype(jnp.bfloat16)
        d_kv_far[:, value_lanes] = d_values[TOP:BLANK].astype(jnp.bfloat16)
        for copy in side_copies(pair):
            copy.start()

        @pl.when(pair > 0)
        def _():
            relay_back(pair - 1)

        return carry

    lax.fori_loop(0, PAIRS, attend_back, 0)
    relay_back(PAIRS - 1)

    for channel in up_channels:
        channel.after_core(partners, sibling)
    for channel in up_channels:
        channel.send_mesh(0, partners)

    for pair in range(PAIRS):
        lanes = slice(256 * pair, 256 * pair + 256)
        for copy in band_copies(pair):
            copy.wait_recv()
        summed = d_kv_own[:, lanes]
        band = d_band_in[:, lanes].astype(jnp.float32)
        summed = jnp.concatenate(
            [summed[:96] + band[:96], summed[96:160], summed[160:] + band[96:]], axis=0
        ).astype(jnp.bfloat16)
        turned = summed.T
        for part in range(2):
            at = MODEL * (1 + part) + 128 * pair
            d_qkv_t[at : at + 128] = turned[128 * part : 128 * part + 128]

    def qkv_body(group, carry):
        qkv_payload(group, mine, core, a1t, d_qkv_t, qbuf, rbuf)
        return carry

    lax.fori_loop(0, 8, qkv_body, 0)
    for channel in qkv_channels:
        channel.core_copy(sibling).start()

    d_normed = dot(w_qkv[...], d_qkv_t[...]).T
    wide = tokens[...].astype(jnp.float32)
    d_tokens[...] = (
        d_tokens[...].astype(jnp.float32)
        + norm_back(wide, inverse_rms(wide), gain_attn[...], d_normed)
    ).astype(jnp.bfloat16)

    for channel in up_channels:
        channel.after_mesh(0, partners, total_up)
    for channel in qkv_channels:
        channel.after_core(partners, sibling)
    for channel in qkv_channels:
        channel.send_mesh(0, partners)
    for step in range(6):
        if step < 5:
            for channel in up_channels:
                channel.after_mesh(step + 1, partners, total_up)
        if step == 4:
            up_last = exchange(total_up, other_up, last_sems[0:2], sibling)
            up_last.start()
        for channel in qkv_channels:
            channel.after_mesh(step, partners, total_qkv)
    qkv_last = exchange(total_qkv, other_qkv, last_sems[2:4], sibling)
    qkv_last.start()

    up_last.wait_recv()
    up_own, down_own = up_blocks(total_up, other_up, core, (col // 8) % 2)
    up_own, down_own = up_own * scaling, down_own * scaling
    up_turned, down_turned = up_own.T, down_own.T
    new_left_up[0] = left_up[0] + exact(up_own, up_turned) / 192
    new_right_up[0] = right_up[0] + exact(up_turned, up_own) / 96
    new_left_down[0] = left_down[0] + exact(down_turned, down_own) / 96
    new_right_down[0] = right_down[0] + exact(down_own, down_turned) / 192
    qkv_last.wait_recv()
    qkv_own = qkv_block(total_qkv, other_qkv, core) * scaling
    qkv_turned = qkv_own.T
    new_left_qkv[0] = left_qkv[0] + exact(qkv_own, qkv_turned) / 144
    new_right_qkv[0] = right_qkv[0] + exact(qkv_turned, qkv_own) / 96

    for channel in up_channels + qkv_channels:
        channel.finish(partners, sibling)
    up_last.wait_send()
    qkv_last.wait_send()
    for pair in range(PAIRS):
        for copy in near_copies(pair, 0, 2) + side_copies(pair) + band_copies(pair):
            copy.wait_send()


def on_device(
    tokens,
    cotangent,
    gain_attn,
    gain_mlp,
    weight_qkv,
    weight_out,
    weight_up,
    weight_down,
    *stats,
):
    scaling = float(TOKENS * lax.axis_size("rows") * lax.axis_size("cols")) ** (-0.5)
    sides, corners = halo_tables()
    bf16, f32 = jnp.bfloat16, jnp.float32

    def vmem(kind, *shape):
        return pltpu.VMEM(shape, kind)

    def boxes(count, size):
        return [vmem(bf16, 2, count, CHIPS, size, 128), vmem(bf16, count, CHIPS, size, 128)]

    def sems_of(count):
        return [
            pltpu.SemaphoreType.DMA((count,)),
            pltpu.SemaphoreType.DMA((count,)),
            pltpu.SemaphoreType.DMA((count, 6)),
            pltpu.SemaphoreType.DMA((count, 6)),
            pltpu.SemaphoreType.REGULAR((count, 6)),
        ]

    in_vmem = pl.BlockSpec(memory_space=pltpu.VMEM)
    mixed, d_tokens, *new_stats = pl.pallas_call(
        functools.partial(whole_kernel, scaling),
        out_shape=[jax.ShapeDtypeStruct((TOKENS, MODEL), bf16)] * 2
        + [jax.ShapeDtypeStruct(stat.shape, f32) for stat in stats],
        in_specs=[in_vmem] * 14 + [pl.BlockSpec(memory_space=pl.ANY)] * 4,
        out_specs=[in_vmem] * 8,
        scratch_shapes=[
            vmem(bf16, MODEL, 3 * MODEL),
            vmem(bf16, MODEL, MODEL),
            vmem(bf16, MODEL, HIDDEN),
            vmem(bf16, HIDDEN, MODEL),
            vmem(bf16, KEYS, 2 * MODEL),
            vmem(bf16, TOKENS, MODEL),
            vmem(bf16, MODEL, TOKENS),
            vmem(bf16, HEADS, KEYS, TOKENS),
            vmem(f32, KEYS, TOKENS),
            vmem(bf16, MODEL, TOKENS),
            vmem(bf16, TOKENS, MODEL),
            vmem(bf16, MODEL, TOKENS),
            vmem(f32, TOKENS, 2 * MODEL),
            vmem(bf16, 576, 2 * MODEL),
            vmem(bf16, 384, 2 * MODEL),
            vmem(bf16, 192, 2 * MODEL),
            vmem(bf16, 192, 2 * MODEL),
            vmem(bf16, MODEL, TOKENS),
            vmem(bf16, MODEL, TOKENS),
            vmem(bf16, MODEL, TOKENS),
            vmem(bf16, TOKENS, HIDDEN),
            vmem(bf16, TOKENS, HIDDEN),
            vmem(bf16, 3 * MODEL, TOKENS),
        ]
        + boxes(6, 48)
        + boxes(6, 16)
        + boxes(1, 16)
        + [vmem(f32, 288, 128), vmem(f32, 288, 128), vmem(f32, 112, 128), vmem(f32, 112, 128)]
        + [
            pltpu.SemaphoreType.DMA((4,)),
            pltpu.SemaphoreType.DMA((36,)),
            pltpu.SemaphoreType.DMA((36,)),
            pltpu.SemaphoreType.DMA((24,)),
            pltpu.SemaphoreType.DMA((24,)),
        ]
        + sems_of(6)
        + sems_of(6)
        + sems_of(1)
        + [pltpu.SemaphoreType.DMA] * 4,
        compiler_params=pltpu.CompilerParams(
            collective_id=0, has_side_effects=True, vmem_limit_bytes=62 * 2**20 + 2**19
        ),
    )(
        tokens.reshape(TOKENS, MODEL),
        cotangent.reshape(TOKENS, MODEL),
        gain_attn[None],
        gain_mlp[None],
        jnp.asarray(sides, bf16),
        jnp.asarray(corners, bf16),
        jnp.asarray(sides.T, bf16),
        jnp.asarray(corners.T, bf16),
        *stats,
        weight_qkv,
        weight_out,
        weight_up,
        weight_down,
    )
    return (
        mixed.reshape(TILE, TILE, MODEL),
        d_tokens.reshape(TILE, TILE, MODEL),
        *new_stats,
    )


def solution(mesh):
    in_specs = (
        P("rows", "cols", None),
        P("rows", "cols", None),
        P(),
        P(),
        P(),
        P(),
        P(),
        P(),
        P(("rows", "cols"), None, None),
        P(("rows", "cols"), None, None),
        P(("rows", "cols"), None, None),
        P(("rows", "cols"), None, None),
        P(("rows", "cols"), None, None),
        P(("rows", "cols"), None, None),
    )
    out_specs = (
        P("rows", "cols", None),
        P("rows", "cols", None),
        P(("rows", "cols"), None, None),
        P(("rows", "cols"), None, None),
        P(("rows", "cols"), None, None),
        P(("rows", "cols"), None, None),
        P(("rows", "cols"), None, None),
        P(("rows", "cols"), None, None),
    )
    return jax.shard_map(
        on_device, mesh=mesh, in_specs=in_specs, out_specs=out_specs, check_vma=False
    )
```

```python
import functools

import jax
import jax.numpy as jnp
import numpy as np
from jax import lax
from jax.experimental import pallas as pl
from jax.experimental.pallas import tpu as pltpu
from jax.sharding import PartitionSpec as P

HEADS = 12
PAIRS = 6
MODEL = 768
HIDDEN = 3072
TILE = 16
TOKENS = TILE * TILE
FLOWS = 6
CHIPS = 64
TOP, TOP_CORNERS, LEFT, RIGHT, OWN, LOW_CORNERS, BOTTOM, KEYS = 0, 96, 192, 288, 384, 640, 736, 832
SPAN = 640
LATER = KEYS - SPAN

epsilon = 1e-06
window_half = 6
window_span = 13
MESH = pl.DeviceIdType.MESH


def halo_tables():
    sides = np.zeros((192, TOKENS), np.float32)
    corners = np.zeros((192, 192), np.float32)
    for side, first in enumerate((0, TILE - 6)):
        for r in range(TILE):
            for c in range(6):
                sides[96 * side + r * 6 + c, r * TILE + first + c] = 1
        for band in range(2):
            for r in range(6):
                for c in range(6):
                    at = 48 * band + r * 6 + c
                    corners[96 * side + at, 96 * band + r * TILE + first + c] = 1
    return sides, corners


def key_places():
    key = lax.broadcasted_iota(jnp.int32, (KEYS, 1), 0)
    in_band = (key < TOP_CORNERS) | (key >= BOTTOM) | ((key >= OWN) & (key < LOW_CORNERS))
    band = key - jnp.where(key < TOP_CORNERS, TOP, jnp.where(key >= BOTTOM, BOTTOM, OWN))
    shift = jnp.where(key < TOP_CORNERS, -6, jnp.where(key >= BOTTOM, TILE, 0))
    band_row, band_col = band // TILE + shift, band % TILE
    low = key >= LOW_CORNERS
    in_corner = (key < LEFT) | low
    corner = key - jnp.where(low, LOW_CORNERS, TOP_CORNERS)
    on_right = jnp.where(in_corner, corner, key - LEFT - 48) >= 48
    at = jnp.where(
        in_corner, corner - jnp.where(on_right, 48, 0), key - jnp.where(key >= RIGHT, RIGHT, LEFT)
    )
    sixth = (at * 171) >> 10
    side_row = sixth + jnp.where(in_corner, jnp.where(low, TILE, -6), 0)
    side_col = at - 6 * sixth + jnp.where(on_right, TILE, -6)
    unused = in_corner & (at >= 36)
    key_row = jnp.where(in_band, band_row, jnp.where(unused, -1000, side_row))
    return key_row, jnp.where(in_band, band_col, side_col)


def dot(left, right):
    return jnp.dot(left, right, preferred_element_type=jnp.float32)


def dot_nt(left, right):
    return lax.dot_general(
        left, right, (((1,), (1,)), ((), ())), preferred_element_type=jnp.float32
    )


def inverse_rms(wide):
    return lax.rsqrt(jnp.mean(wide * wide, axis=-1, keepdims=True) + epsilon)


def norm_back(wide, scale, gain, upstream):
    scaled = upstream * gain
    return scale * scaled - wide * (
        scale * scale * scale * jnp.mean(wide * scaled, axis=-1, keepdims=True)
    )


def lane_masks():
    lane = lax.broadcasted_iota(jnp.int32, (1, 128), 1)
    low = jnp.where(lane < 64, 1.0, 0.0)
    return low.astype(jnp.bfloat16), (1.0 - low).astype(jnp.bfloat16)


def gray_bits(position):
    high = position // 2
    return (high, (high + position % 2) % 2)


def my_place():
    row = lax.axis_index("rows")
    col = lax.axis_index("cols")
    core = col % 2
    x = col // 4
    y = (row // 4) * 2 + (col // 2) % 2
    z = row % 4
    return x, y, z, core


def device_at(x, y, z, core):
    return ((y // 2) * 4 + z, x * 4 + (y % 2) * 2 + core)


def link_bits(x, y, z):
    gx, gy, gz = gray_bits(x), gray_bits(y), gray_bits(z)
    return (gx[1], gy[1], gz[1], gx[0], gy[0], gz[0])


def link_partners(x, y, z, core):
    return (
        device_at(x + 1 - 2 * (x % 2), y, z, core),
        device_at(x, y + 1 - 2 * (y % 2), z, core),
        device_at(x, y, z + 1 - 2 * (z % 2), core),
        device_at(3 - x, y, z, core),
        device_at(x, 3 - y, z, core),
        device_at(x, y, 3 - z, core),
    )


def slot_terms(mine, theirs, axis):
    near = (mine[axis] + theirs[1]) % 2
    far = (mine[axis + 3] + theirs[0]) % 2
    return [
        near * (32 >> ((axis - flow) % 6)) + far * (32 >> ((axis + 3 - flow) % 6))
        for flow in range(FLOWS)
    ]


class Slots:
    def __init__(self, mine):
        self.mine = mine
        self.along_x = [slot_terms(mine, gray_bits(x), 0) for x in range(4)]

    def of_group(self, group):
        along_z = slot_terms(self.mine, gray_bits(group % 4), 2)
        plane = []
        for y_lo in range(2):
            along_y = slot_terms(self.mine, gray_bits((group // 4) * 2 + y_lo), 1)
            plane.append([a + b for a, b in zip(along_y, along_z)])
        return lambda c, flow: self.along_x[c // 2][flow] + plane[c % 2][flow]


class Channel:
    def __init__(self, own, inbox, sems, index, flow, total_at):
        self.own, self.inbox = own, inbox
        self.core_send, self.core_recv, self.mesh_send, self.mesh_recv, self.credit = sems
        self.index, self.flow, self.total_at = index, flow, total_at

    def core_copy(self, sibling):
        return pltpu.make_async_remote_copy(
            src_ref=self.own.at[1, self.index],
            dst_ref=self.inbox.at[self.index],
            send_sem=self.core_send.at[self.index],
            recv_sem=self.core_recv.at[self.index],
            device_id=sibling,
            device_id_type=MESH,
        )

    def mesh_copy(self, step, partners):
        count = 32 >> step
        return pltpu.make_async_remote_copy(
            src_ref=self.own.at[0, self.index, pl.ds(count, count)],
            dst_ref=self.inbox.at[self.index, pl.ds(count, count)],
            send_sem=self.mesh_send.at[self.index, step],
            recv_sem=self.mesh_recv.at[self.index, step],
            device_id=partners[(self.flow + step) % 6],
            device_id_type=MESH,
        )

    def add(self, source_first, first, count):
        own, inbox, index = self.own, self.inbox, self.index
        rows = own.shape[3]
        chunk = min(count, max(1, 128 // rows))

        def body(turn, carry):
            at = first + turn * chunk
            own[0, index, pl.ds(at, chunk)] = (
                own[0, index, pl.ds(at, chunk)]
                + inbox[index, pl.ds(source_first + turn * chunk, chunk)]
            )
            return carry

        lax.fori_loop(0, count // chunk, body, 0)

    def after_core(self, partners, sibling):
        self.core_copy(sibling).wait_recv()
        self.add(0, 0, 64)
        for step in range(6):
            pl.semaphore_signal(
                self.credit.at[self.index, step],
                inc=1,
                device_id=partners[(self.flow + step) % 6],
                device_id_type=MESH,
            )

    def send_mesh(self, step, partners):
        pl.semaphore_wait(self.credit.at[self.index, step], 1)
        self.mesh_copy(step, partners).start()

    def after_mesh(self, step, partners, total):
        self.mesh_copy(step, partners).wait_recv()
        count = 32 >> step
        if step < 5:
            half = count // 2
            self.add(count + half, half, half)
            self.send_mesh(step + 1, partners)
            self.add(count, 0, half)
        else:
            rows = self.own.shape[3]
            total[pl.ds(self.total_at, rows)] = self.own[0, self.index, 0].astype(
                jnp.float32
            ) + self.inbox[self.index, 1].astype(jnp.float32)

    def finish(self, partners, sibling):
        self.core_copy(sibling).wait_send()
        for step in range(6):
            self.mesh_copy(step, partners).wait_send()


def down_payload(group, slots, core, a3t, activated, ubuf):
    slot = slots.of_group(group)
    lane = lax.broadcasted_iota(jnp.int32, (96, 128), 1)
    for c in range(8):
        q, odd = c % 4, c // 4
        tile = 3 * group
        left = a3t[192 * q : 192 * q + 192, :]
        main = dot(left, activated[:, pl.ds(pl.multiple_of((tile + 2 * odd) * 128, 128), 128)])
        half = dot(left, activated[:, pl.ds(pl.multiple_of((tile + 1) * 128, 128), 128)])
        first, second = half[:96], half[96:]
        if odd:
            packed = jnp.where(lane < 64, pltpu.roll(first, 64, 1), second)
        else:
            packed = jnp.where(lane < 64, first, pltpu.roll(second, 64, 1))
        store_payload(ubuf, core, slot, c, 3, (main[:96], main[96:], packed))


def up_payload(group, slots, core, a2t, d_up, ubuf):
    slot = slots.of_group(group)
    left = a2t[pl.ds(pl.multiple_of(96 * group, 32), 96), :]
    for c in range(8):
        up = dot(left, d_up[:, 384 * c : 384 * c + 384])
        store_payload(ubuf, core, slot, c, 0, (up[:, :128], up[:, 128:256], up[:, 256:]))


def store_payload(ubuf, core, slot, c, first_flow, pieces):
    for at, piece in enumerate(pieces):
        piece = piece.astype(jnp.bfloat16)
        for half in range(2):
            ubuf[(core + half) % 2, first_flow + at, slot(c, first_flow + at)] = piece[
                48 * half : 48 * half + 48
            ]


def qkv_payload(group, slots, core, a1t, d_qkv_t, qbuf, rbuf):
    slot = slots.of_group(group)
    left = a1t[pl.ds(pl.multiple_of(96 * group, 32), 96), :]
    blank = jnp.zeros((16, 32), jnp.bfloat16)
    for c in range(8):
        main = dot_nt(left, d_qkv_t[288 * c : 288 * c + 256]).astype(jnp.bfloat16)
        rest = dot_nt(d_qkv_t[288 * c + 256 : 288 * c + 288], left).astype(jnp.bfloat16)
        for half in range(2):
            for flow in range(FLOWS):
                qbuf[(core + half) % 2, flow, slot(c, flow)] = main[
                    16 * flow : 16 * flow + 16, 128 * half : 128 * half + 128
                ]
            rbuf[(core + half) % 2, 0, slot(c, 0)] = jnp.concatenate(
                [rest[16 * half : 16 * half + 16], blank], axis=1
            )


def exact(left, right):
    return jnp.dot(
        left, right, precision=lax.Precision.HIGHEST, preferred_element_type=jnp.float32
    )


def up_blocks(sums, core, part_odd):
    first, odd = core == 0, part_odd == 1
    left, middle, right, main_0, main_1, packed = [
        jnp.concatenate([sums[0, 48 * at : 48 * at + 48], sums[1, 48 * at : 48 * at + 48]], axis=0)
        for at in range(6)
    ]
    up = jnp.where(
        first,
        jnp.concatenate([left, middle], axis=1),
        pltpu.roll(jnp.concatenate([middle, right], axis=1), 192, 1),
    )[:, :192]
    main = jnp.where(first, main_0, main_1)
    turned = pltpu.roll(packed, 64, 1)
    low, high = jnp.where(first, packed, turned), jnp.where(first, turned, packed)
    down = jnp.where(
        odd,
        pltpu.roll(jnp.concatenate([high, main], axis=1), 192, 1),
        jnp.concatenate([main, low], axis=1),
    )[:, :192]
    return up, down


def qkv_block(sums, core):
    both = [sums[0, 0:96], sums[1, 0:96]]
    rest = jnp.concatenate(
        [sums[0, 96:112], sums[1, 96:112], jnp.zeros((96, 128), jnp.float32)], axis=0
    ).T[:96]
    return jnp.where(
        core == 0,
        jnp.concatenate(both, axis=1),
        pltpu.roll(jnp.concatenate([both[1], rest], axis=1), 240, 1),
    )[:, :144]


def stats_kernel(
    scaling,
    mixed_in,
    d_tokens_in,
    up_sums,
    qkv_sums,
    left_qkv,
    right_qkv,
    left_up,
    right_up,
    left_down,
    right_down,
    mixed,
    d_tokens,
    new_left_qkv,
    new_right_qkv,
    new_left_up,
    new_right_up,
    new_left_down,
    new_right_down,
):
    col = lax.axis_index("cols")
    core = col % 2
    mixed[...] = mixed_in[...]
    d_tokens[...] = d_tokens_in[...]
    up_own, down_own = up_blocks(up_sums, core, (col // 8) % 2)
    up_own, down_own = up_own * scaling, down_own * scaling
    up_turned, down_turned = up_own.T, down_own.T
    new_left_up[0] = left_up[0] + exact(up_own, up_turned) / 192
    new_right_up[0] = right_up[0] + exact(up_turned, up_own) / 96
    new_left_down[0] = left_down[0] + exact(down_turned, down_own) / 96
    new_right_down[0] = right_down[0] + exact(down_own, down_turned) / 192
    qkv_own = qkv_block(qkv_sums, core) * scaling
    qkv_turned = qkv_own.T
    new_left_qkv[0] = left_qkv[0] + exact(qkv_own, qkv_turned) / 144
    new_right_qkv[0] = right_qkv[0] + exact(qkv_turned, qkv_own) / 96


def exchange(source, target, sems, device):
    return pltpu.make_async_remote_copy(
        src_ref=source,
        dst_ref=target,
        send_sem=sems[0],
        recv_sem=sems[1],
        device_id=device,
        device_id_type=MESH,
    )


def gain_row(gain):
    return gain[...].reshape(1, MODEL)


def diagonal(first, second):
    return jnp.concatenate(
        [
            jnp.concatenate([first, jnp.zeros_like(second)], axis=1),
            jnp.concatenate([jnp.zeros_like(first), second], axis=1),
        ],
        axis=0,
    )


def whole_kernel(*refs):
    refs = list(refs)

    def take(count):
        taken = refs[:count]
        del refs[:count]
        return taken

    tokens, cotangent, gain_attn, gain_mlp, sides, corners, sides_t, corners_t = take(8)
    weight_refs = take(4)
    mixed, d_tokens, up_sums, qkv_sums = take(4)
    w_qkv, w_out, w_up, w_down = take(4)
    near, packed, kv, query, query_t, chances, hidden, attended_t = take(8)
    d_attended, d_attended_t, d_norm_own, d_far, d_side_in, d_band, d_band_in = take(7)
    a1t, a2t, a3t, d_up, activated, d_qkv_t = take(6)
    ubuf, ubox, qbuf, qbox, rbuf, rbox = take(6)
    total_up, other_up, total_qkv, other_qkv = take(4)
    weight_sems, halo_send, halo_recv, back_send, back_recv = take(5)
    up_sems, qkv_sems, rest_sems = take(5), take(5), take(5)
    last_sems = take(4)

    row, col = lax.axis_index("rows"), lax.axis_index("cols")
    rows, cols = lax.axis_size("rows"), lax.axis_size("cols")
    above, below = ((row + rows - 1) % rows, col), ((row + 1) % rows, col)
    to_left, to_right = (row, (col + cols - 1) % cols), (row, (col + 1) % cols)
    x, y, z, core = my_place()
    sibling = device_at(x, y, z, 1 - core)
    partners = link_partners(x, y, z, core)
    slots = Slots(link_bits(x, y, z))
    barrier = pltpu.get_barrier_semaphore()
    for place in (above, below, to_left, to_right, sibling) + partners:
        pl.semaphore_signal(barrier, inc=1, device_id=place, device_id_type=MESH)
    loads = [
        pltpu.make_async_copy(weight_refs[at], place, weight_sems.at[at])
        for at, place in ((0, w_qkv), (1, w_out), (3, w_down), (2, w_up))
    ]
    loads[0].start()

    def copies(routes, first_sem, send, recv):
        return [
            pltpu.make_async_remote_copy(
                src_ref=source,
                dst_ref=target,
                send_sem=send.at[first_sem + at],
                recv_sem=recv.at[first_sem + at],
                device_id=device,
                device_id_type=MESH,
            )
            for at, (source, target, device) in enumerate(routes)
        ]

    def part(ref, first, count):
        return ref.at[pl.ds(first, count)]

    packed[:192] = dot(sides[...], tokens[...]).astype(jnp.bfloat16)
    pl.semaphore_wait(barrier, 11)
    near_copies = copies(
        (
            (part(tokens, 0, 96), part(near, BOTTOM, 96), above),
            (part(tokens, TOKENS - 96, 96), part(near, TOP, 96), below),
            (part(packed, 0, 96), part(near, RIGHT, 96), to_left),
            (part(packed, 96, 96), part(near, LEFT, 96), to_right),
        ),
        0,
        halo_send,
        halo_recv,
    )
    for copy in near_copies:
        copy.start()
    corner_copies = copies(
        (
            (part(packed, 192, 48), part(near, TOP_CORNERS + 48, 48), to_left),
            (part(packed, 240, 48), part(near, LOW_CORNERS + 48, 48), to_left),
            (part(packed, 288, 48), part(near, TOP_CORNERS, 48), to_right),
            (part(packed, 336, 48), part(near, LOW_CORNERS, 48), to_right),
        ),
        4,
        halo_send,
        halo_recv,
    )

    wide = tokens[...].astype(jnp.float32)
    normed_attn = (wide * inverse_rms(wide) * gain_row(gain_attn)).astype(jnp.bfloat16)
    near[OWN:LOW_CORNERS] = normed_attn
    a3t[...] = cotangent[...].T
    key_row, key_col = key_places()
    key_row, key_col = row * TILE + key_row, col * TILE + key_col
    for half in range(2):
        at = lax.broadcasted_iota(jnp.int32, (1, 128), 1) + 128 * half
        row_first = jnp.clip(row * TILE + at // TILE - window_half, 0, rows * TILE - window_span)
        col_first = jnp.clip(col * TILE + at % TILE - window_half, 0, cols * TILE - window_span)
        spot_row = key_row[LATER * half : LATER * half + SPAN]
        spot_col = key_col[LATER * half : LATER * half + SPAN]
        visible = (
            (spot_row >= row_first)
            & (spot_row < row_first + window_span)
            & (spot_col >= col_first)
            & (spot_col < col_first + window_span)
        )
        hidden[half] = jnp.where(visible, 0.0, -1e30)

    for copy in near_copies[:2]:
        copy.wait_recv()
    packed[192:384] = (
        dot(corners[:, :96], near[TOP:TOP_CORNERS]) + dot(corners[:, 96:], near[BOTTOM:KEYS])
    ).astype(jnp.bfloat16)
    for copy in corner_copies:
        copy.start()
    loads[0].wait()
    for load in loads[1:]:
        load.start()
    own_query = dot(normed_attn, w_qkv[:, :MODEL]).astype(jnp.bfloat16)
    own_query = (own_query.astype(jnp.float32) * 0.125).astype(jnp.bfloat16)
    query[...] = own_query
    query_t[...] = own_query.T
    kv[OWN:LOW_CORNERS] = dot(normed_attn, w_qkv[:, MODEL:]).astype(jnp.bfloat16)
    for copy in near_copies[2:] + corner_copies:
        copy.wait_recv()
    for first, last in ((TOP, OWN), (LOW_CORNERS, KEYS)):
        halo = near[first:last].astype(jnp.float32)
        halo = (halo * inverse_rms(halo) * gain_row(gain_attn)).astype(jnp.bfloat16)
        near[first:last] = halo
        kv[first:last] = dot(halo, w_qkv[:, MODEL:]).astype(jnp.bfloat16)
    a1t[...] = near[...].T

    def spans(half):
        return pl.ds(LATER * half, SPAN)

    def attend(pair, carry):
        lanes = pl.ds(pl.multiple_of(pair * 128, 128), 128)
        value_lanes = pl.ds(pl.multiple_of(MODEL + pair * 128, 128), 128)
        queries = query_t[lanes, :]
        for half in range(2):
            columns = slice(128 * half, 128 * half + 128)
            both = diagonal(queries[:64, columns], queries[64:, columns])
            bias = jnp.concatenate([hidden[half], hidden[half]], axis=1)
            scores = dot(kv[spans(half), lanes], both) + bias
            most = jnp.max(scores, axis=0, keepdims=True)
            powers = jnp.exp(scores - most)
            total = jnp.sum(powers, axis=0, keepdims=True)
            weights = (powers * (1.0 / total)).astype(jnp.bfloat16)
            chances[pair, half] = weights
            blended = dot(kv[spans(half), value_lanes].T, weights).astype(jnp.bfloat16)
            attended_t[lanes, columns] = jnp.concatenate(
                [blended[:64, :128], blended[64:, 128:]], axis=0
            )
        return carry

    lax.fori_loop(0, PAIRS, attend, 0)

    for load in loads[1:]:
        load.wait()
    wide = tokens[...].astype(jnp.float32)
    residual = (wide + dot(attended_t[...].T, w_out[...])).astype(jnp.bfloat16)
    residual_wide = residual.astype(jnp.float32)
    scale_mlp = inverse_rms(residual_wide)
    normed_mlp = (residual_wide * scale_mlp * gain_row(gain_mlp)).astype(jnp.bfloat16)
    a2t[...] = normed_mlp.T
    mix = residual_wide
    d_normed = jnp.zeros((TOKENS, MODEL), jnp.float32)
    slope = float(np.sqrt(2 / np.pi))
    for step in range(6):
        units = slice(512 * step, 512 * step + 512)
        up = dot(normed_mlp, w_up[:, units])
        d_act = dot_nt(cotangent[...], w_down[units])
        square = up * up
        tanh = jnp.tanh(slope * up * (1.0 + 0.044715 * square))
        grown = 0.5 * (1.0 + tanh)
        active = (up * grown).astype(jnp.bfloat16)
        activated[:, units] = active
        mix = mix + dot(active, w_down[units])
        steep = grown + 0.5 * up * (1.0 - tanh * tanh) * (
            slope * (1.0 + 3 * 0.044715 * square)
        )
        d_up_part = (d_act * steep).astype(jnp.bfloat16)
        d_up[:, units] = d_up_part
        d_normed = d_normed + dot_nt(d_up_part, w_up[:, units])
    mixed[...] = mix.astype(jnp.bfloat16)

    up_channels = [
        Channel(ubuf, ubox, up_sems, flow, flow, 48 * flow) for flow in range(FLOWS)
    ]
    early, late = up_channels[3:], up_channels[:3]
    qkv_channels = [
        Channel(qbuf, qbox, qkv_sems, flow, flow, 16 * flow) for flow in range(FLOWS)
    ] + [Channel(rbuf, rbox, rest_sems, 0, 0, 96)]

    def loop(count, body):
        def turn(at, carry):
            body(at)
            return carry

        lax.fori_loop(0, count, turn, 0)

    loop(8, lambda group: down_payload(group, slots, core, a3t, activated, ubuf))
    for channel in early:
        channel.core_copy(sibling).start()
    loop(8, lambda group: up_payload(group, slots, core, a2t, d_up, ubuf))
    for channel in late:
        channel.core_copy(sibling).start()

    d_residual = (
        cotangent[...].astype(jnp.float32)
        + norm_back(residual_wide, scale_mlp, gain_row(gain_mlp), d_normed)
    ).astype(jnp.bfloat16)
    d_tokens[...] = d_residual
    d_att = dot_nt(d_residual, w_out[...]).astype(jnp.bfloat16)
    d_attended[...] = d_att
    d_attended_t[...] = d_att.T
    d_qkv_t[:MODEL, :OWN] = jnp.zeros((MODEL, OWN), jnp.bfloat16)
    d_qkv_t[:MODEL, LOW_CORNERS:] = jnp.zeros((MODEL, KEYS - LOW_CORNERS), jnp.bfloat16)

    masks = lane_masks()

    def attend_back(pair):
        lanes = pl.ds(pl.multiple_of(pair * 128, 128), 128)
        key_lanes = pl.ds(pl.multiple_of(MODEL + pair * 128, 128), 128)
        value_lanes = pl.ds(pl.multiple_of(2 * MODEL + pair * 128, 128), 128)
        upstream_t = d_attended_t[lanes, :]
        products = upstream_t.astype(jnp.float32) * attended_t[lanes, :].astype(jnp.float32)
        deltas = [
            jnp.sum(products[64 * second : 64 * second + 64], axis=0, keepdims=True)
            for second in range(2)
        ]
        d_keys, d_values, d_query = [], [], []
        for half in range(2):
            columns = slice(128 * half, 128 * half + 128)
            weights = chances[pair, half]
            both = diagonal(upstream_t[:64, columns], upstream_t[64:, columns])
            delta = jnp.concatenate([delta[:, columns] for delta in deltas], axis=1)
            d_prob = dot(kv[spans(half), key_lanes], both)
            d_score = (weights.astype(jnp.float32) * (d_prob - delta)).astype(jnp.bfloat16)
            crossed = dot(kv[spans(half), lanes].T, d_score)
            d_query.append(jnp.concatenate([crossed[:64, :128], crossed[64:, 128:]], axis=0))
            asked = query[columns, lanes]
            d_keys.append(
                dot(d_score, jnp.concatenate([asked * masks[0], asked * masks[1]], axis=0))
            )
            sought = d_attended[columns, lanes]
            d_values.append(
                dot(weights, jnp.concatenate([sought * masks[0], sought * masks[1]], axis=0))
            )
        d_qkv_t[lanes, OWN:LOW_CORNERS] = (
            jnp.concatenate(d_query, axis=1) * 0.125
        ).astype(jnp.bfloat16)
        for place, (one, two) in ((key_lanes, d_keys), (value_lanes, d_values)):
            summed = jnp.concatenate(
                [one[:LATER], one[LATER:] + two[: SPAN - LATER], two[SPAN - LATER :]], axis=0
            )
            d_qkv_t[place, :] = summed.astype(jnp.bfloat16).T

    loop(2, attend_back)
    for channel in early:
        channel.after_core(partners, sibling)
    for channel in early:
        channel.send_mesh(0, partners)
    loop(2, lambda pair: attend_back(pair + 2))
    for channel in late:
        channel.after_core(partners, sibling)
    for channel in late:
        channel.send_mesh(0, partners)
    loop(2, lambda pair: attend_back(pair + 4))
    for channel in early:
        channel.after_mesh(0, partners, total_up)

    loop(8, lambda group: qkv_payload(group, slots, core, a1t, d_qkv_t, qbuf, rbuf))
    for channel in qkv_channels:
        channel.core_copy(sibling).start()
    for channel in late:
        channel.after_mesh(0, partners, total_up)

    for step in range(3):
        lines = slice(256 * step, 256 * step + 256)
        piece = dot(w_qkv[lines, :], d_qkv_t[...]).T
        d_norm_own[:, lines] = piece[OWN:LOW_CORNERS]
        for target, first, count in (
            (0, TOP, 96),
            (96, BOTTOM, 96),
            (192, LEFT, 96),
            (288, TOP_CORNERS, 48),
            (336, LOW_CORNERS, 48),
            (384, RIGHT, 96),
            (480, TOP_CORNERS + 48, 48),
            (528, LOW_CORNERS + 48, 48),
        ):
            d_far[target : target + count, lines] = piece[first : first + count].astype(
                jnp.bfloat16
            )
    side_copies = copies(
        (
            (part(d_far, 192, 192), part(d_side_in, 192, 192), to_left),
            (part(d_far, 384, 192), part(d_side_in, 0, 192), to_right),
        ),
        0,
        back_send,
        back_recv,
    )
    band_copies = copies(
        (
            (part(d_band, 0, 96), part(d_band_in, 96, 96), above),
            (part(d_band, 96, 96), part(d_band_in, 0, 96), below),
        ),
        2,
        back_send,
        back_recv,
    )
    for copy in side_copies:
        copy.start()

    for channel in qkv_channels:
        channel.after_core(partners, sibling)
    for channel in qkv_channels:
        channel.send_mesh(0, partners)
    for channel in early + late:
        channel.after_mesh(1, partners, total_up)

    for copy in side_copies:
        copy.wait_recv()
    own = jnp.concatenate([d_side_in[0:96], d_side_in[192:288]], axis=0)
    far = jnp.concatenate([d_side_in[96:192], d_side_in[288:384]], axis=0)
    d_band[...] = (d_far[0:192].astype(jnp.float32) + dot(corners_t[...], far)).astype(
        jnp.bfloat16
    )
    for copy in band_copies:
        copy.start()
    d_norm_own[...] = d_norm_own[...] + dot(sides_t[...], own)

    for step in range(2, 6):
        for channel in qkv_channels:
            channel.after_mesh(step - 2, partners, total_qkv)
        for channel in early + late:
            channel.after_mesh(step, partners, total_up)
    up_last = exchange(total_up, other_up, last_sems[0:2], sibling)
    up_last.start()

    for copy in band_copies:
        copy.wait_recv()
    band = d_band_in[...].astype(jnp.float32)
    summed = d_norm_own[...]
    d_normed = jnp.concatenate(
        [summed[:96] + band[:96], summed[96:160], summed[160:] + band[96:]], axis=0
    )
    wide = tokens[...].astype(jnp.float32)
    d_tokens[...] = (
        d_tokens[...].astype(jnp.float32)
        + norm_back(wide, inverse_rms(wide), gain_row(gain_attn), d_normed)
    ).astype(jnp.bfloat16)

    for step in range(4, 6):
        for channel in qkv_channels:
            channel.after_mesh(step, partners, total_qkv)
    qkv_last = exchange(total_qkv, other_qkv, last_sems[2:4], sibling)
    qkv_last.start()
    first = core == 0
    for last, mine, theirs, sums in (
        (up_last, total_up, other_up, up_sums),
        (qkv_last, total_qkv, other_qkv, qkv_sums),
    ):
        last.wait_recv()
        sums[0] = jnp.where(first, mine[...], theirs[...])
        sums[1] = jnp.where(first, theirs[...], mine[...])

    for channel in up_channels + qkv_channels:
        channel.finish(partners, sibling)
    for copy in near_copies + corner_copies + side_copies + band_copies + [up_last, qkv_last]:
        copy.wait_send()


def on_device(
    tokens,
    cotangent,
    gain_attn,
    gain_mlp,
    weight_qkv,
    weight_out,
    weight_up,
    weight_down,
    *stats,
):
    scaling = float(TOKENS * lax.axis_size("rows") * lax.axis_size("cols")) ** (-0.5)
    sides, corners = halo_tables()
    bf16, f32 = jnp.bfloat16, jnp.float32

    def vmem(kind, *shape):
        return pltpu.VMEM(shape, kind)

    def boxes(count, size):
        return [vmem(bf16, 2, count, CHIPS, size, 128), vmem(bf16, count, CHIPS, size, 128)]

    def sems_of(count):
        return [
            pltpu.SemaphoreType.DMA((count,)),
            pltpu.SemaphoreType.DMA((count,)),
            pltpu.SemaphoreType.DMA((count, 6)),
            pltpu.SemaphoreType.DMA((count, 6)),
            pltpu.SemaphoreType.REGULAR((count, 6)),
        ]

    in_vmem = pl.BlockSpec(memory_space=pltpu.VMEM)
    tile = jax.ShapeDtypeStruct((TOKENS, MODEL), bf16)
    mixed, d_tokens, up_sums, qkv_sums = pl.pallas_call(
        whole_kernel,
        out_shape=[
            tile,
            tile,
            jax.ShapeDtypeStruct((2, 288, 128), f32),
            jax.ShapeDtypeStruct((2, 112, 128), f32),
        ],
        in_specs=[in_vmem] * 8 + [pl.BlockSpec(memory_space=pl.ANY)] * 4,
        out_specs=[in_vmem] * 4,
        scratch_shapes=[
            vmem(bf16, MODEL, 3 * MODEL),
            vmem(bf16, MODEL, MODEL),
            vmem(bf16, MODEL, HIDDEN),
            vmem(bf16, HIDDEN, MODEL),
            vmem(bf16, KEYS, MODEL),
            vmem(bf16, 384, MODEL),
            vmem(bf16, KEYS, 2 * MODEL),
            vmem(bf16, TOKENS, MODEL),
            vmem(bf16, MODEL, TOKENS),
            vmem(bf16, PAIRS, 2, SPAN, 256),
            vmem(f32, 2, SPAN, 128),
            vmem(bf16, MODEL, TOKENS),
            vmem(bf16, TOKENS, MODEL),
            vmem(bf16, MODEL, TOKENS),
            vmem(f32, TOKENS, MODEL),
            vmem(bf16, 576, MODEL),
            vmem(bf16, 384, MODEL),
            vmem(bf16, 192, MODEL),
            vmem(bf16, 192, MODEL),
            vmem(bf16, MODEL, KEYS),
            vmem(bf16, MODEL, TOKENS),
            vmem(bf16, MODEL, TOKENS),
            vmem(bf16, TOKENS, HIDDEN),
            vmem(bf16, TOKENS, HIDDEN),
            vmem(bf16, 3 * MODEL, KEYS),
        ]
        + boxes(6, 48)
        + boxes(6, 16)
        + boxes(1, 16)
        + [vmem(f32, 288, 128), vmem(f32, 288, 128), vmem(f32, 112, 128), vmem(f32, 112, 128)]
        + [
            pltpu.SemaphoreType.DMA((4,)),
            pltpu.SemaphoreType.DMA((8,)),
            pltpu.SemaphoreType.DMA((8,)),
            pltpu.SemaphoreType.DMA((4,)),
            pltpu.SemaphoreType.DMA((4,)),
        ]
        + sems_of(6)
        + sems_of(6)
        + sems_of(1)
        + [pltpu.SemaphoreType.DMA] * 4,
        compiler_params=pltpu.CompilerParams(
            collective_id=0, has_side_effects=True, vmem_limit_bytes=62 * 2**20 + 2**19
        ),
    )(
        tokens.reshape(TOKENS, MODEL),
        cotangent.reshape(TOKENS, MODEL),
        gain_attn,
        gain_mlp,
        jnp.asarray(sides, bf16),
        jnp.asarray(corners, bf16),
        jnp.asarray(sides.T, bf16),
        jnp.asarray(corners.T, bf16),
        weight_qkv,
        weight_out,
        weight_up,
        weight_down,
    )
    mixed, d_tokens, *new_stats = pl.pallas_call(
        functools.partial(stats_kernel, scaling),
        out_shape=[tile, tile] + [jax.ShapeDtypeStruct(stat.shape, f32) for stat in stats],
        in_specs=[in_vmem] * 10,
        out_specs=[in_vmem] * 8,
        compiler_params=pltpu.CompilerParams(vmem_limit_bytes=32 * 2**20),
    )(mixed, d_tokens, up_sums, qkv_sums, *stats)
    return (
        mixed.reshape(TILE, TILE, MODEL),
        d_tokens.reshape(TILE, TILE, MODEL),
        *new_stats,
    )


def solution(mesh):
    in_specs = (
        P("rows", "cols", None),
        P("rows", "cols", None),
        P(),
        P(),
        P(),
        P(),
        P(),
        P(),
        P(("rows", "cols"), None, None),
        P(("rows", "cols"), None, None),
        P(("rows", "cols"), None, None),
        P(("rows", "cols"), None, None),
        P(("rows", "cols"), None, None),
        P(("rows", "cols"), None, None),
    )
    out_specs = (
        P("rows", "cols", None),
        P("rows", "cols", None),
        P(("rows", "cols"), None, None),
        P(("rows", "cols"), None, None),
        P(("rows", "cols"), None, None),
        P(("rows", "cols"), None, None),
        P(("rows", "cols"), None, None),
        P(("rows", "cols"), None, None),
    )
    return jax.shard_map(
        on_device, mesh=mesh, in_specs=in_specs, out_specs=out_specs, check_vma=False
    )
```

```python
import functools

import jax
import jax.numpy as jnp
import numpy as np
from jax import lax
from jax.experimental import pallas as pl
from jax.experimental.pallas import tpu as pltpu
from jax.sharding import PartitionSpec as P

HEADS = 12
PAIRS = 6
MODEL = 768
HIDDEN = 3072
TILE = 16
TOKENS = TILE * TILE
FLOWS = 6
CHIPS = 64
TOP, TOP_CORNERS, LEFT, RIGHT, OWN, LOW_CORNERS, BOTTOM, KEYS = 0, 96, 192, 288, 384, 640, 736, 832
SPAN = 640
LATER = KEYS - SPAN

epsilon = 1e-06
window_half = 6
window_span = 13
MESH = pl.DeviceIdType.MESH


def halo_tables():
    sides = np.zeros((192, TOKENS), np.float32)
    corners = np.zeros((192, 192), np.float32)
    for side, first in enumerate((0, TILE - 6)):
        for r in range(TILE):
            for c in range(6):
                sides[96 * side + r * 6 + c, r * TILE + first + c] = 1
        for band in range(2):
            for r in range(6):
                for c in range(6):
                    at = 48 * band + r * 6 + c
                    corners[96 * side + at, 96 * band + r * TILE + first + c] = 1
    return sides, corners


def key_places():
    key = lax.broadcasted_iota(jnp.int32, (KEYS, 1), 0)
    in_band = (key < TOP_CORNERS) | (key >= BOTTOM) | ((key >= OWN) & (key < LOW_CORNERS))
    band = key - jnp.where(key < TOP_CORNERS, TOP, jnp.where(key >= BOTTOM, BOTTOM, OWN))
    shift = jnp.where(key < TOP_CORNERS, -6, jnp.where(key >= BOTTOM, TILE, 0))
    band_row, band_col = band // TILE + shift, band % TILE
    low = key >= LOW_CORNERS
    in_corner = (key < LEFT) | low
    corner = key - jnp.where(low, LOW_CORNERS, TOP_CORNERS)
    on_right = jnp.where(in_corner, corner, key - LEFT - 48) >= 48
    at = jnp.where(
        in_corner, corner - jnp.where(on_right, 48, 0), key - jnp.where(key >= RIGHT, RIGHT, LEFT)
    )
    sixth = (at * 171) >> 10
    side_row = sixth + jnp.where(in_corner, jnp.where(low, TILE, -6), 0)
    side_col = at - 6 * sixth + jnp.where(on_right, TILE, -6)
    unused = in_corner & (at >= 36)
    key_row = jnp.where(in_band, band_row, jnp.where(unused, -1000, side_row))
    return key_row, jnp.where(in_band, band_col, side_col)


def dot(left, right):
    return jnp.dot(left, right, preferred_element_type=jnp.float32)


def dot_nt(left, right):
    return lax.dot_general(
        left, right, (((1,), (1,)), ((), ())), preferred_element_type=jnp.float32
    )


def inverse_rms(wide):
    return lax.rsqrt(jnp.mean(wide * wide, axis=-1, keepdims=True) + epsilon)


def norm_back(wide, scale, gain, upstream):
    scaled = upstream * gain
    return scale * scaled - wide * (
        scale * scale * scale * jnp.mean(wide * scaled, axis=-1, keepdims=True)
    )


def lane_masks():
    lane = lax.broadcasted_iota(jnp.int32, (1, 128), 1)
    low = jnp.where(lane < 64, 1.0, 0.0)
    return low.astype(jnp.bfloat16), (1.0 - low).astype(jnp.bfloat16)


def gray_bits(position):
    high = position // 2
    return (high, (high + position % 2) % 2)


def my_place():
    row = lax.axis_index("rows")
    col = lax.axis_index("cols")
    core = col % 2
    x = col // 4
    y = (row // 4) * 2 + (col // 2) % 2
    z = row % 4
    return x, y, z, core


def device_at(x, y, z, core):
    return ((y // 2) * 4 + z, x * 4 + (y % 2) * 2 + core)


def link_bits(x, y, z):
    gx, gy, gz = gray_bits(x), gray_bits(y), gray_bits(z)
    return (gx[1], gy[1], gz[1], gx[0], gy[0], gz[0])


def link_partners(x, y, z, core):
    return (
        device_at(x + 1 - 2 * (x % 2), y, z, core),
        device_at(x, y + 1 - 2 * (y % 2), z, core),
        device_at(x, y, z + 1 - 2 * (z % 2), core),
        device_at(3 - x, y, z, core),
        device_at(x, 3 - y, z, core),
        device_at(x, y, 3 - z, core),
    )


def slot_terms(mine, theirs, axis):
    near = (mine[axis] + theirs[1]) % 2
    far = (mine[axis + 3] + theirs[0]) % 2
    return [
        near * (32 >> ((axis - flow) % 6)) + far * (32 >> ((axis + 3 - flow) % 6))
        for flow in range(FLOWS)
    ]


class Slots:
    def __init__(self, mine):
        self.mine = mine

    def terms(self, axis, position):
        return slot_terms(self.mine, gray_bits(position), axis)

    def table(self, xs, y_los, y_his, zs):
        along_x = {at: self.terms(0, x) for at, x in enumerate(xs)}
        along_y = {
            (i, j): self.terms(1, y_hi * 2 + y_lo)
            for i, y_hi in enumerate(y_his)
            for j, y_lo in enumerate(y_los)
        }
        along_z = {at: self.terms(2, z) for at, z in enumerate(zs)}
        return lambda x, y_lo, y_hi, z, flow: (
            along_x[x][flow] + along_y[y_hi, y_lo][flow] + along_z[z][flow]
        )

    def of_group(self, group):
        slot = self.table(range(4), range(2), [group // 4], [group % 4])
        return lambda c, flow: slot(c // 2, c % 2, 0, 0, flow)

    def of_column(self, c):
        slot = self.table([c // 2], [c % 2], range(2), range(4))
        return lambda group, flow: slot(0, 0, group // 4, group % 4, flow)


class Channel:
    def __init__(self, own, inbox, sems, index, flow, total_at):
        self.own, self.inbox = own, inbox
        self.core_send, self.core_recv, self.mesh_send, self.mesh_recv, self.credit = sems
        self.index, self.flow, self.total_at = index, flow, total_at

    def core_copy(self, sibling):
        return pltpu.make_async_remote_copy(
            src_ref=self.own.at[1, self.index],
            dst_ref=self.inbox.at[self.index],
            send_sem=self.core_send.at[self.index],
            recv_sem=self.core_recv.at[self.index],
            device_id=sibling,
            device_id_type=MESH,
        )

    def mesh_copy(self, step, partners):
        count = 32 >> step
        return pltpu.make_async_remote_copy(
            src_ref=self.own.at[0, self.index, pl.ds(count, count)],
            dst_ref=self.inbox.at[self.index, pl.ds(count, count)],
            send_sem=self.mesh_send.at[self.index, step],
            recv_sem=self.mesh_recv.at[self.index, step],
            device_id=partners[(self.flow + step) % 6],
            device_id_type=MESH,
        )

    def add(self, source_first, first, count):
        own, inbox, index = self.own, self.inbox, self.index
        rows = own.shape[3]
        chunk = min(count, max(1, 128 // rows))

        def body(turn, carry):
            at = first + turn * chunk
            own[0, index, pl.ds(at, chunk)] = (
                own[0, index, pl.ds(at, chunk)]
                + inbox[index, pl.ds(source_first + turn * chunk, chunk)]
            )
            return carry

        lax.fori_loop(0, count // chunk, body, 0)

    def after_core(self, partners, sibling):
        self.core_copy(sibling).wait_recv()
        self.add(0, 0, 64)
        for step in range(6):
            pl.semaphore_signal(
                self.credit.at[self.index, step],
                inc=1,
                device_id=partners[(self.flow + step) % 6],
                device_id_type=MESH,
            )

    def send_mesh(self, step, partners):
        pl.semaphore_wait(self.credit.at[self.index, step], 1)
        self.mesh_copy(step, partners).start()

    def after_mesh(self, step, partners, total):
        self.mesh_copy(step, partners).wait_recv()
        count = 32 >> step
        if step < 5:
            half = count // 2
            self.add(count + half, half, half)
            self.send_mesh(step + 1, partners)
            self.add(count, 0, half)
        else:
            rows = self.own.shape[3]
            total[pl.ds(self.total_at, rows)] = self.own[0, self.index, 0].astype(
                jnp.float32
            ) + self.inbox[self.index, 1].astype(jnp.float32)

    def finish(self, partners, sibling):
        self.core_copy(sibling).wait_send()
        for step in range(6):
            self.mesh_copy(step, partners).wait_send()


def put(box, core, flow, slot, piece):
    rows = piece.shape[0] // 2
    for half in range(2):
        box[(core + half) % 2, flow, slot] = piece[rows * half : rows * half + rows]


def down_payload(group, slots, core, a3t, activated, ubuf):
    slot = slots.of_group(group)
    lane = lax.broadcasted_iota(jnp.int32, (96, 128), 1)
    tiles = dot(a3t[...], activated[:, pl.ds(pl.multiple_of(384 * group, 128), 384)])
    for c in range(8):
        q, odd = c % 4, c // 4
        main = tiles[192 * q : 192 * q + 192, 256 * odd : 256 * odd + 128].astype(jnp.bfloat16)
        first = tiles[192 * q : 192 * q + 96, 128:256]
        second = tiles[192 * q + 96 : 192 * q + 192, 128:256]
        if odd:
            packed = jnp.where(lane < 64, pltpu.roll(first, 64, 1), second)
        else:
            packed = jnp.where(lane < 64, first, pltpu.roll(second, 64, 1))
        put(ubuf, core, 3, slot(c, 3), main[:96])
        put(ubuf, core, 4, slot(c, 4), main[96:])
        put(ubuf, core, 5, slot(c, 5), packed.astype(jnp.bfloat16))


def up_payload(c, slots, core, a2t, d_up, ubuf):
    slot = slots.of_column(c)
    tiles = dot(a2t[...], d_up[:, pl.ds(pl.multiple_of(384 * c, 128), 384)]).astype(jnp.bfloat16)
    for group in range(8):
        for flow in range(3):
            put(
                ubuf,
                core,
                flow,
                slot(group, flow),
                tiles[96 * group : 96 * group + 96, 128 * flow : 128 * flow + 128],
            )


def qkv_payload(c, slots, core, a1t, d_qkv_t, qbuf):
    slot = slots.of_column(c)
    first = pl.multiple_of(288 * c, 32)
    second = pl.multiple_of(288 * c + 144, 16)
    columns = jnp.concatenate(
        [d_qkv_t[pl.ds(first, 128), :], d_qkv_t[pl.ds(second, 128), :]], axis=0
    )
    tiles = dot_nt(a1t[...], columns).astype(jnp.bfloat16)
    for group in range(8):
        for flow in range(FLOWS):
            at = 96 * group + 16 * flow
            for half in range(2):
                qbuf[(core + half) % 2, flow, slot(group, flow)] = tiles[
                    at : at + 16, 128 * half : 128 * half + 128
                ]


def rest_payload(slots, core, a1t, d_qkv_t, rbuf):
    columns = jnp.concatenate(
        [d_qkv_t[144 * block + 128 : 144 * block + 144] for block in range(16)], axis=0
    )
    tiles = dot_nt(a1t[...], columns)
    slot = slots.table(range(4), range(2), range(2), range(4))
    blank = jnp.zeros((256, 32), jnp.bfloat16)
    for group in range(8):
        turned = tiles[96 * group : 96 * group + 96].T.astype(jnp.bfloat16)
        turned = jnp.concatenate([turned, blank], axis=1)
        for c in range(8):
            for half in range(2):
                at = 32 * c + 16 * half
                rbuf[(core + half) % 2, 0, slot(c // 2, c % 2, group // 4, group % 4, 0)] = turned[
                    at : at + 16
                ]


def exact(left, right):
    return jnp.dot(
        left, right, precision=lax.Precision.HIGHEST, preferred_element_type=jnp.float32
    )


def up_blocks(sums, core, part_odd):
    first, odd = core == 0, part_odd == 1
    left, middle, right, main_0, main_1, packed = [
        jnp.concatenate([sums[0, 48 * at : 48 * at + 48], sums[1, 48 * at : 48 * at + 48]], axis=0)
        for at in range(6)
    ]
    up = jnp.where(
        first,
        jnp.concatenate([left, middle], axis=1),
        pltpu.roll(jnp.concatenate([middle, right], axis=1), 192, 1),
    )[:, :192]
    main = jnp.where(first, main_0, main_1)
    turned = pltpu.roll(packed, 64, 1)
    low, high = jnp.where(first, packed, turned), jnp.where(first, turned, packed)
    down = jnp.where(
        odd,
        pltpu.roll(jnp.concatenate([high, main], axis=1), 192, 1),
        jnp.concatenate([main, low], axis=1),
    )[:, :192]
    return up, down


def qkv_block(sums):
    rest = jnp.concatenate([sums[96:112], jnp.zeros((112, 128), jnp.float32)], axis=0).T[:96]
    return jnp.concatenate([sums[0:96], rest], axis=1)[:, :144]


def stats_kernel(
    scaling,
    mixed_in,
    d_tokens_in,
    up_sums,
    qkv_sums,
    left_qkv,
    right_qkv,
    left_up,
    right_up,
    left_down,
    right_down,
    mixed,
    d_tokens,
    new_left_qkv,
    new_right_qkv,
    new_left_up,
    new_right_up,
    new_left_down,
    new_right_down,
):
    col = lax.axis_index("cols")
    core = col % 2
    mixed[...] = mixed_in[...]
    d_tokens[...] = d_tokens_in[...]
    up_own, down_own = up_blocks(up_sums, core, (col // 8) % 2)
    up_own, down_own = up_own * scaling, down_own * scaling
    up_turned, down_turned = up_own.T, down_own.T
    new_left_up[0] = left_up[0] + exact(up_own, up_turned) / 192
    new_right_up[0] = right_up[0] + exact(up_turned, up_own) / 96
    new_left_down[0] = left_down[0] + exact(down_turned, down_own) / 96
    new_right_down[0] = right_down[0] + exact(down_own, down_turned) / 192
    qkv_own = qkv_block(qkv_sums) * scaling
    qkv_turned = qkv_own.T
    new_left_qkv[0] = left_qkv[0] + exact(qkv_own, qkv_turned) / 144
    new_right_qkv[0] = right_qkv[0] + exact(qkv_turned, qkv_own) / 96


def exchange(source, target, sems, device):
    return pltpu.make_async_remote_copy(
        src_ref=source,
        dst_ref=target,
        send_sem=sems[0],
        recv_sem=sems[1],
        device_id=device,
        device_id_type=MESH,
    )


def gain_row(gain):
    return gain[...].reshape(1, MODEL)


def diagonal(first, second):
    return jnp.concatenate(
        [
            jnp.concatenate([first, jnp.zeros_like(second)], axis=1),
            jnp.concatenate([jnp.zeros_like(first), second], axis=1),
        ],
        axis=0,
    )


def whole_kernel(*refs):
    refs = list(refs)

    def take(count):
        taken = refs[:count]
        del refs[:count]
        return taken

    tokens, cotangent, gain_attn, gain_mlp, sides, corners, sides_t, corners_t = take(8)
    weight_refs = take(4)
    mixed, d_tokens, up_sums, qkv_sums = take(4)
    w_qkv, w_out, w_up, w_down = take(4)
    near, packed, kv, query, query_t, chances, hidden, attended_t = take(8)
    d_attended, d_attended_t, d_norm_own, d_far, d_side_in, d_band, d_band_in = take(7)
    a1t, a2t, a3t, d_up, activated, d_qkv_t = take(6)
    ubuf, ubox, qbuf, qbox, rbuf, rbox = take(6)
    total_up, other_up = take(2)
    weight_sems, halo_send, halo_recv, back_send, back_recv = take(5)
    up_sems, qkv_sems, rest_sems = take(5), take(5), take(5)
    last_sems = take(2)

    row, col = lax.axis_index("rows"), lax.axis_index("cols")
    rows, cols = lax.axis_size("rows"), lax.axis_size("cols")
    above, below = ((row + rows - 1) % rows, col), ((row + 1) % rows, col)
    to_left, to_right = (row, (col + cols - 1) % cols), (row, (col + 1) % cols)
    x, y, z, core = my_place()
    sibling = device_at(x, y, z, 1 - core)
    partners = link_partners(x, y, z, core)
    slots = Slots(link_bits(x, y, z))
    barrier = pltpu.get_barrier_semaphore()
    for place in (above, below, to_left, to_right, sibling) + partners:
        pl.semaphore_signal(barrier, inc=1, device_id=place, device_id_type=MESH)
    loads = [
        pltpu.make_async_copy(weight_refs[at], place, weight_sems.at[at])
        for at, place in ((0, w_qkv), (1, w_out), (3, w_down), (2, w_up))
    ]
    loads[0].start()

    def copies(routes, first_sem, send, recv):
        return [
            pltpu.make_async_remote_copy(
                src_ref=source,
                dst_ref=target,
                send_sem=send.at[first_sem + at],
                recv_sem=recv.at[first_sem + at],
                device_id=device,
                device_id_type=MESH,
            )
            for at, (source, target, device) in enumerate(routes)
        ]

    def part(ref, first, count):
        return ref.at[pl.ds(first, count)]

    packed[:192] = dot(sides[...], tokens[...]).astype(jnp.bfloat16)
    pl.semaphore_wait(barrier, 11)
    near_copies = copies(
        (
            (part(tokens, 0, 96), part(near, BOTTOM, 96), above),
            (part(tokens, TOKENS - 96, 96), part(near, TOP, 96), below),
            (part(packed, 0, 96), part(near, RIGHT, 96), to_left),
            (part(packed, 96, 96), part(near, LEFT, 96), to_right),
        ),
        0,
        halo_send,
        halo_recv,
    )
    for copy in near_copies:
        copy.start()
    corner_copies = copies(
        (
            (part(packed, 192, 48), part(near, TOP_CORNERS + 48, 48), to_left),
            (part(packed, 240, 48), part(near, LOW_CORNERS + 48, 48), to_left),
            (part(packed, 288, 48), part(near, TOP_CORNERS, 48), to_right),
            (part(packed, 336, 48), part(near, LOW_CORNERS, 48), to_right),
        ),
        4,
        halo_send,
        halo_recv,
    )

    wide = tokens[...].astype(jnp.float32)
    normed_attn = (wide * inverse_rms(wide) * gain_row(gain_attn)).astype(jnp.bfloat16)
    near[OWN:LOW_CORNERS] = normed_attn
    a3t[...] = cotangent[...].T
    key_row, key_col = key_places()
    key_row, key_col = row * TILE + key_row, col * TILE + key_col
    for half in range(2):
        at = lax.broadcasted_iota(jnp.int32, (1, 128), 1) + 128 * half
        row_first = jnp.clip(row * TILE + at // TILE - window_half, 0, rows * TILE - window_span)
        col_first = jnp.clip(col * TILE + at % TILE - window_half, 0, cols * TILE - window_span)
        spot_row = key_row[LATER * half : LATER * half + SPAN]
        spot_col = key_col[LATER * half : LATER * half + SPAN]
        visible = (
            (spot_row >= row_first)
            & (spot_row < row_first + window_span)
            & (spot_col >= col_first)
            & (spot_col < col_first + window_span)
        )
        hidden[half] = jnp.where(visible, 0.0, -1e30)

    for copy in near_copies[:2]:
        copy.wait_recv()
    packed[192:384] = (
        dot(corners[:, :96], near[TOP:TOP_CORNERS]) + dot(corners[:, 96:], near[BOTTOM:KEYS])
    ).astype(jnp.bfloat16)
    for copy in corner_copies:
        copy.start()
    loads[0].wait()
    for load in loads[1:]:
        load.start()
    own_query = dot(normed_attn, w_qkv[:, :MODEL]).astype(jnp.bfloat16)
    own_query = (own_query.astype(jnp.float32) * 0.125).astype(jnp.bfloat16)
    query[...] = own_query
    query_t[...] = own_query.T
    kv[OWN:LOW_CORNERS] = dot(normed_attn, w_qkv[:, MODEL:]).astype(jnp.bfloat16)
    for copy in near_copies[2:] + corner_copies:
        copy.wait_recv()
    for first, last in ((TOP, OWN), (LOW_CORNERS, KEYS)):
        halo = near[first:last].astype(jnp.float32)
        halo = (halo * inverse_rms(halo) * gain_row(gain_attn)).astype(jnp.bfloat16)
        near[first:last] = halo
        kv[first:last] = dot(halo, w_qkv[:, MODEL:]).astype(jnp.bfloat16)
    a1t[...] = near[...].T

    def spans(half):
        return pl.ds(LATER * half, SPAN)

    def attend(pair, carry):
        lanes = pl.ds(pl.multiple_of(pair * 128, 128), 128)
        value_lanes = pl.ds(pl.multiple_of(MODEL + pair * 128, 128), 128)
        queries = query_t[lanes, :]
        for half in range(2):
            columns = slice(128 * half, 128 * half + 128)
            both = diagonal(queries[:64, columns], queries[64:, columns])
            bias = jnp.concatenate([hidden[half], hidden[half]], axis=1)
            scores = dot(kv[spans(half), lanes], both) + bias
            most = jnp.max(scores, axis=0, keepdims=True)
            powers = jnp.exp(scores - most)
            total = jnp.sum(powers, axis=0, keepdims=True)
            weights = (powers * (1.0 / total)).astype(jnp.bfloat16)
            chances[pair, half] = weights
            blended = dot(kv[spans(half), value_lanes].T, weights).astype(jnp.bfloat16)
            attended_t[lanes, columns] = jnp.concatenate(
                [blended[:64, :128], blended[64:, 128:]], axis=0
            )
        return carry

    lax.fori_loop(0, PAIRS, attend, 0)

    for load in loads[1:]:
        load.wait()
    wide = tokens[...].astype(jnp.float32)
    residual = (wide + dot(attended_t[...].T, w_out[...])).astype(jnp.bfloat16)
    residual_wide = residual.astype(jnp.float32)
    scale_mlp = inverse_rms(residual_wide)
    normed_mlp = (residual_wide * scale_mlp * gain_row(gain_mlp)).astype(jnp.bfloat16)
    a2t[...] = normed_mlp.T
    mix = residual_wide
    d_normed = jnp.zeros((TOKENS, MODEL), jnp.float32)
    slope = float(np.sqrt(2 / np.pi))
    for step in range(6):
        units = slice(512 * step, 512 * step + 512)
        up = dot(normed_mlp, w_up[:, units])
        d_act = dot_nt(cotangent[...], w_down[units])
        square = up * up
        tanh = jnp.tanh(slope * up * (1.0 + 0.044715 * square))
        grown = 0.5 * (1.0 + tanh)
        active = (up * grown).astype(jnp.bfloat16)
        activated[:, units] = active
        mix = mix + dot(active, w_down[units])
        steep = grown + 0.5 * up * (1.0 - tanh * tanh) * (
            slope * (1.0 + 3 * 0.044715 * square)
        )
        d_up_part = (d_act * steep).astype(jnp.bfloat16)
        d_up[:, units] = d_up_part
        d_normed = d_normed + dot_nt(d_up_part, w_up[:, units])
    mixed[...] = mix.astype(jnp.bfloat16)

    up_channels = [
        Channel(ubuf, ubox, up_sems, flow, flow, 48 * flow) for flow in range(FLOWS)
    ]
    early, late = up_channels[3:], up_channels[:3]
    qkv_channels = [
        Channel(qbuf, qbox, qkv_sems, flow, flow, 16 * flow) for flow in range(FLOWS)
    ] + [Channel(rbuf, rbox, rest_sems, 0, 0, 96)]

    def loop(count, body):
        def turn(at, carry):
            body(at)
            return carry

        lax.fori_loop(0, count, turn, 0)

    loop(8, lambda group: down_payload(group, slots, core, a3t, activated, ubuf))
    for channel in early:
        channel.core_copy(sibling).start()
    loop(8, lambda c: up_payload(c, slots, core, a2t, d_up, ubuf))
    for channel in late:
        channel.core_copy(sibling).start()

    d_residual = (
        cotangent[...].astype(jnp.float32)
        + norm_back(residual_wide, scale_mlp, gain_row(gain_mlp), d_normed)
    ).astype(jnp.bfloat16)
    d_tokens[...] = d_residual
    d_att = dot_nt(d_residual, w_out[...]).astype(jnp.bfloat16)
    d_attended[...] = d_att
    d_attended_t[...] = d_att.T
    d_qkv_t[:MODEL, :OWN] = jnp.zeros((MODEL, OWN), jnp.bfloat16)
    d_qkv_t[:MODEL, LOW_CORNERS:] = jnp.zeros((MODEL, KEYS - LOW_CORNERS), jnp.bfloat16)

    masks = lane_masks()

    def attend_back(pair):
        lanes = pl.ds(pl.multiple_of(pair * 128, 128), 128)
        key_lanes = pl.ds(pl.multiple_of(MODEL + pair * 128, 128), 128)
        value_lanes = pl.ds(pl.multiple_of(2 * MODEL + pair * 128, 128), 128)
        upstream_t = d_attended_t[lanes, :]
        products = upstream_t.astype(jnp.float32) * attended_t[lanes, :].astype(jnp.float32)
        deltas = [
            jnp.sum(products[64 * second : 64 * second + 64], axis=0, keepdims=True)
            for second in range(2)
        ]
        d_keys, d_values, d_query = [], [], []
        for half in range(2):
            columns = slice(128 * half, 128 * half + 128)
            weights = chances[pair, half]
            both = diagonal(upstream_t[:64, columns], upstream_t[64:, columns])
            delta = jnp.concatenate([delta[:, columns] for delta in deltas], axis=1)
            d_prob = dot(kv[spans(half), key_lanes], both)
            d_score = (weights.astype(jnp.float32) * (d_prob - delta)).astype(jnp.bfloat16)
            crossed = dot(kv[spans(half), lanes].T, d_score)
            d_query.append(jnp.concatenate([crossed[:64, :128], crossed[64:, 128:]], axis=0))
            asked = query[columns, lanes]
            d_keys.append(
                dot(d_score, jnp.concatenate([asked * masks[0], asked * masks[1]], axis=0))
            )
            sought = d_attended[columns, lanes]
            d_values.append(
                dot(weights, jnp.concatenate([sought * masks[0], sought * masks[1]], axis=0))
            )
        d_qkv_t[lanes, OWN:LOW_CORNERS] = (
            jnp.concatenate(d_query, axis=1) * 0.125
        ).astype(jnp.bfloat16)
        for place, (one, two) in ((key_lanes, d_keys), (value_lanes, d_values)):
            summed = jnp.concatenate(
                [one[:LATER], one[LATER:] + two[: SPAN - LATER], two[SPAN - LATER :]], axis=0
            )
            d_qkv_t[place, :] = summed.astype(jnp.bfloat16).T

    loop(2, attend_back)
    for channel in early:
        channel.after_core(partners, sibling)
    for channel in early:
        channel.send_mesh(0, partners)
    loop(2, lambda pair: attend_back(pair + 2))
    for channel in late:
        channel.after_core(partners, sibling)
    for channel in late:
        channel.send_mesh(0, partners)
    loop(2, lambda pair: attend_back(pair + 4))
    for channel in early:
        channel.after_mesh(0, partners, total_up)

    loop(8, lambda c: qkv_payload(c, slots, core, a1t, d_qkv_t, qbuf))
    rest_payload(slots, core, a1t, d_qkv_t, rbuf)
    for channel in qkv_channels:
        channel.core_copy(sibling).start()
    for channel in late:
        channel.after_mesh(0, partners, total_up)

    for step in range(3):
        lines = slice(256 * step, 256 * step + 256)
        piece = dot(w_qkv[lines, :], d_qkv_t[...]).T
        d_norm_own[:, lines] = piece[OWN:LOW_CORNERS]
        for target, first, count in (
            (0, TOP, 96),
            (96, BOTTOM, 96),
            (192, LEFT, 96),
            (288, TOP_CORNERS, 48),
            (336, LOW_CORNERS, 48),
            (384, RIGHT, 96),
            (480, TOP_CORNERS + 48, 48),
            (528, LOW_CORNERS + 48, 48),
        ):
            d_far[target : target + count, lines] = piece[first : first + count].astype(
                jnp.bfloat16
            )
    side_copies = copies(
        (
            (part(d_far, 192, 192), part(d_side_in, 192, 192), to_left),
            (part(d_far, 384, 192), part(d_side_in, 0, 192), to_right),
        ),
        0,
        back_send,
        back_recv,
    )
    band_copies = copies(
        (
            (part(d_band, 0, 96), part(d_band_in, 96, 96), above),
            (part(d_band, 96, 96), part(d_band_in, 0, 96), below),
        ),
        2,
        back_send,
        back_recv,
    )
    for copy in side_copies:
        copy.start()

    for channel in qkv_channels:
        channel.after_core(partners, sibling)
    for channel in qkv_channels:
        channel.send_mesh(0, partners)
    for channel in early + late:
        channel.after_mesh(1, partners, total_up)

    for copy in side_copies:
        copy.wait_recv()
    own = jnp.concatenate([d_side_in[0:96], d_side_in[192:288]], axis=0)
    far = jnp.concatenate([d_side_in[96:192], d_side_in[288:384]], axis=0)
    d_band[...] = (d_far[0:192].astype(jnp.float32) + dot(corners_t[...], far)).astype(
        jnp.bfloat16
    )
    for copy in band_copies:
        copy.start()
    d_norm_own[...] = d_norm_own[...] + dot(sides_t[...], own)

    for step in range(2, 6):
        for channel in qkv_channels:
            channel.after_mesh(step - 2, partners, qkv_sums)
        for channel in early + late:
            channel.after_mesh(step, partners, total_up)
    up_last = exchange(total_up, other_up, last_sems[0:2], sibling)
    up_last.start()

    for copy in band_copies:
        copy.wait_recv()
    band = d_band_in[...].astype(jnp.float32)
    summed = d_norm_own[...]
    d_normed = jnp.concatenate(
        [summed[:96] + band[:96], summed[96:160], summed[160:] + band[96:]], axis=0
    )
    wide = tokens[...].astype(jnp.float32)
    d_tokens[...] = (
        d_tokens[...].astype(jnp.float32)
        + norm_back(wide, inverse_rms(wide), gain_row(gain_attn), d_normed)
    ).astype(jnp.bfloat16)

    for step in range(4, 6):
        for channel in qkv_channels:
            channel.after_mesh(step, partners, qkv_sums)
    first = core == 0
    up_last.wait_recv()
    up_sums[0] = jnp.where(first, total_up[...], other_up[...])
    up_sums[1] = jnp.where(first, other_up[...], total_up[...])

    for channel in up_channels + qkv_channels:
        channel.finish(partners, sibling)
    for copy in near_copies + corner_copies + side_copies + band_copies + [up_last]:
        copy.wait_send()


def on_device(
    tokens,
    cotangent,
    gain_attn,
    gain_mlp,
    weight_qkv,
    weight_out,
    weight_up,
    weight_down,
    *stats,
):
    scaling = float(TOKENS * lax.axis_size("rows") * lax.axis_size("cols")) ** (-0.5)
    sides, corners = halo_tables()
    bf16, f32 = jnp.bfloat16, jnp.float32

    def vmem(kind, *shape):
        return pltpu.VMEM(shape, kind)

    def boxes(count, size):
        return [vmem(bf16, 2, count, CHIPS, size, 128), vmem(bf16, count, CHIPS, size, 128)]

    def sems_of(count):
        return [
            pltpu.SemaphoreType.DMA((count,)),
            pltpu.SemaphoreType.DMA((count,)),
            pltpu.SemaphoreType.DMA((count, 6)),
            pltpu.SemaphoreType.DMA((count, 6)),
            pltpu.SemaphoreType.REGULAR((count, 6)),
        ]

    in_vmem = pl.BlockSpec(memory_space=pltpu.VMEM)
    tile = jax.ShapeDtypeStruct((TOKENS, MODEL), bf16)
    mixed, d_tokens, up_sums, qkv_sums = pl.pallas_call(
        whole_kernel,
        out_shape=[
            tile,
            tile,
            jax.ShapeDtypeStruct((2, 288, 128), f32),
            jax.ShapeDtypeStruct((112, 128), f32),
        ],
        in_specs=[in_vmem] * 8 + [pl.BlockSpec(memory_space=pl.ANY)] * 4,
        out_specs=[in_vmem] * 4,
        scratch_shapes=[
            vmem(bf16, MODEL, 3 * MODEL),
            vmem(bf16, MODEL, MODEL),
            vmem(bf16, MODEL, HIDDEN),
            vmem(bf16, HIDDEN, MODEL),
            vmem(bf16, KEYS, MODEL),
            vmem(bf16, 384, MODEL),
            vmem(bf16, KEYS, 2 * MODEL),
            vmem(bf16, TOKENS, MODEL),
            vmem(bf16, MODEL, TOKENS),
            vmem(bf16, PAIRS, 2, SPAN, 256),
            vmem(f32, 2, SPAN, 128),
            vmem(bf16, MODEL, TOKENS),
            vmem(bf16, TOKENS, MODEL),
            vmem(bf16, MODEL, TOKENS),
            vmem(f32, TOKENS, MODEL),
            vmem(bf16, 576, MODEL),
            vmem(bf16, 384, MODEL),
            vmem(bf16, 192, MODEL),
            vmem(bf16, 192, MODEL),
            vmem(bf16, MODEL, KEYS),
            vmem(bf16, MODEL, TOKENS),
            vmem(bf16, MODEL, TOKENS),
            vmem(bf16, TOKENS, HIDDEN),
            vmem(bf16, TOKENS, HIDDEN),
            vmem(bf16, 3 * MODEL, KEYS),
        ]
        + boxes(6, 48)
        + boxes(6, 16)
        + boxes(1, 16)
        + [vmem(f32, 288, 128), vmem(f32, 288, 128)]
        + [
            pltpu.SemaphoreType.DMA((4,)),
            pltpu.SemaphoreType.DMA((8,)),
            pltpu.SemaphoreType.DMA((8,)),
            pltpu.SemaphoreType.DMA((4,)),
            pltpu.SemaphoreType.DMA((4,)),
        ]
        + sems_of(6)
        + sems_of(6)
        + sems_of(1)
        + [pltpu.SemaphoreType.DMA] * 2,
        compiler_params=pltpu.CompilerParams(
            collective_id=0, has_side_effects=True, vmem_limit_bytes=62 * 2**20 + 2**19
        ),
    )(
        tokens.reshape(TOKENS, MODEL),
        cotangent.reshape(TOKENS, MODEL),
        gain_attn,
        gain_mlp,
        jnp.asarray(sides, bf16),
        jnp.asarray(corners, bf16),
        jnp.asarray(sides.T, bf16),
        jnp.asarray(corners.T, bf16),
        weight_qkv,
        weight_out,
        weight_up,
        weight_down,
    )
    mixed, d_tokens, *new_stats = pl.pallas_call(
        functools.partial(stats_kernel, scaling),
        out_shape=[tile, tile] + [jax.ShapeDtypeStruct(stat.shape, f32) for stat in stats],
        in_specs=[in_vmem] * 10,
        out_specs=[in_vmem] * 8,
        compiler_params=pltpu.CompilerParams(vmem_limit_bytes=62 * 2**20 + 2**19),
    )(mixed, d_tokens, up_sums, qkv_sums, *stats)
    return (
        mixed.reshape(TILE, TILE, MODEL),
        d_tokens.reshape(TILE, TILE, MODEL),
        *new_stats,
    )


def solution(mesh):
    in_specs = (
        P("rows", "cols", None),
        P("rows", "cols", None),
        P(),
        P(),
        P(),
        P(),
        P(),
        P(),
        P(("rows", "cols"), None, None),
        P(("rows", "cols"), None, None),
        P(("rows", "cols"), None, None),
        P(("rows", "cols"), None, None),
        P(("rows", "cols"), None, None),
        P(("rows", "cols"), None, None),
    )
    out_specs = (
        P("rows", "cols", None),
        P("rows", "cols", None),
        P(("rows", "cols"), None, None),
        P(("rows", "cols"), None, None),
        P(("rows", "cols"), None, None),
        P(("rows", "cols"), None, None),
        P(("rows", "cols"), None, None),
        P(("rows", "cols"), None, None),
    )
    return jax.shard_map(
        on_device, mesh=mesh, in_specs=in_specs, out_specs=out_specs, check_vma=False
    )
```

```python
import functools

import jax
import jax.numpy as jnp
import numpy as np
from jax import lax
from jax.experimental import pallas as pl
from jax.experimental.pallas import tpu as pltpu
from jax.sharding import PartitionSpec as P

HEADS = 12
PAIRS = 6
MODEL = 768
HIDDEN = 3072
TILE = 16
TOKENS = TILE * TILE
FLOWS = 6
CHIPS = 64
TOP, TOP_CORNERS, LEFT, RIGHT, OWN, LOW_CORNERS, BOTTOM, KEYS = 0, 96, 192, 288, 384, 640, 736, 832
SPAN = 640
LATER = KEYS - SPAN

epsilon = 1e-06
window_half = 6
window_span = 13
MESH = pl.DeviceIdType.MESH


def halo_tables():
    sides = np.zeros((192, TOKENS), np.float32)
    corners = np.zeros((192, 192), np.float32)
    for side, first in enumerate((0, TILE - 6)):
        for r in range(TILE):
            for c in range(6):
                sides[96 * side + r * 6 + c, r * TILE + first + c] = 1
        for band in range(2):
            for r in range(6):
                for c in range(6):
                    at = 48 * band + r * 6 + c
                    corners[96 * side + at, 96 * band + r * TILE + first + c] = 1
    return sides, corners


def key_places():
    key = lax.broadcasted_iota(jnp.int32, (KEYS, 1), 0)
    in_band = (key < TOP_CORNERS) | (key >= BOTTOM) | ((key >= OWN) & (key < LOW_CORNERS))
    band = key - jnp.where(key < TOP_CORNERS, TOP, jnp.where(key >= BOTTOM, BOTTOM, OWN))
    shift = jnp.where(key < TOP_CORNERS, -6, jnp.where(key >= BOTTOM, TILE, 0))
    band_row, band_col = band // TILE + shift, band % TILE
    low = key >= LOW_CORNERS
    in_corner = (key < LEFT) | low
    corner = key - jnp.where(low, LOW_CORNERS, TOP_CORNERS)
    on_right = jnp.where(in_corner, corner, key - LEFT - 48) >= 48
    at = jnp.where(
        in_corner, corner - jnp.where(on_right, 48, 0), key - jnp.where(key >= RIGHT, RIGHT, LEFT)
    )
    sixth = (at * 171) >> 10
    side_row = sixth + jnp.where(in_corner, jnp.where(low, TILE, -6), 0)
    side_col = at - 6 * sixth + jnp.where(on_right, TILE, -6)
    unused = in_corner & (at >= 36)
    key_row = jnp.where(in_band, band_row, jnp.where(unused, -1000, side_row))
    return key_row, jnp.where(in_band, band_col, side_col)


def dot(left, right):
    return jnp.dot(left, right, preferred_element_type=jnp.float32)


def dot_nt(left, right):
    return lax.dot_general(
        left, right, (((1,), (1,)), ((), ())), preferred_element_type=jnp.float32
    )


def inverse_rms(wide):
    return lax.rsqrt(jnp.mean(wide * wide, axis=-1, keepdims=True) + epsilon)


def norm_back(wide, scale, gain, upstream):
    scaled = upstream * gain
    return scale * scaled - wide * (
        scale * scale * scale * jnp.mean(wide * scaled, axis=-1, keepdims=True)
    )


def lane_masks():
    lane = lax.broadcasted_iota(jnp.int32, (1, 128), 1)
    low = jnp.where(lane < 64, 1.0, 0.0)
    return low.astype(jnp.bfloat16), (1.0 - low).astype(jnp.bfloat16)


def gray_bits(position):
    high = position // 2
    return (high, (high + position % 2) % 2)


def my_place():
    row = lax.axis_index("rows")
    col = lax.axis_index("cols")
    core = col % 2
    x = col // 4
    y = (row // 4) * 2 + (col // 2) % 2
    z = row % 4
    return x, y, z, core


def device_at(x, y, z, core):
    return ((y // 2) * 4 + z, x * 4 + (y % 2) * 2 + core)


def link_bits(x, y, z):
    gx, gy, gz = gray_bits(x), gray_bits(y), gray_bits(z)
    return (gx[1], gy[1], gz[1], gx[0], gy[0], gz[0])


def link_partners(x, y, z, core):
    return (
        device_at(x + 1 - 2 * (x % 2), y, z, core),
        device_at(x, y + 1 - 2 * (y % 2), z, core),
        device_at(x, y, z + 1 - 2 * (z % 2), core),
        device_at(3 - x, y, z, core),
        device_at(x, 3 - y, z, core),
        device_at(x, y, 3 - z, core),
    )


def slot_terms(mine, theirs, axis):
    near = (mine[axis] + theirs[1]) % 2
    far = (mine[axis + 3] + theirs[0]) % 2
    return [
        near * (32 >> ((axis - flow) % 6)) + far * (32 >> ((axis + 3 - flow) % 6))
        for flow in range(FLOWS)
    ]


class Slots:
    def __init__(self, mine):
        self.mine = mine

    def terms(self, axis, position):
        return slot_terms(self.mine, gray_bits(position), axis)

    def table(self, xs, y_los, y_his, zs):
        along_x = {at: self.terms(0, x) for at, x in enumerate(xs)}
        along_y = {
            (i, j): self.terms(1, y_hi * 2 + y_lo)
            for i, y_hi in enumerate(y_his)
            for j, y_lo in enumerate(y_los)
        }
        along_z = {at: self.terms(2, z) for at, z in enumerate(zs)}
        return lambda x, y_lo, y_hi, z, flow: (
            along_x[x][flow] + along_y[y_hi, y_lo][flow] + along_z[z][flow]
        )

    def of_group(self, group):
        slot = self.table(range(4), range(2), [group // 4], [group % 4])
        return lambda c, flow: slot(c // 2, c % 2, 0, 0, flow)

    def of_column(self, c):
        slot = self.table([c // 2], [c % 2], range(2), range(4))
        return lambda group, flow: slot(0, 0, group // 4, group % 4, flow)


class Channel:
    def __init__(self, own, inbox, mesh_in, sems, index, flow, total_at):
        self.own, self.inbox, self.mesh_in = own, inbox, mesh_in
        self.core_send, self.core_recv, self.mesh_send, self.mesh_recv, self.credit = sems
        self.index, self.flow, self.total_at = index, flow, total_at

    def core_copy(self, sibling):
        return pltpu.make_async_remote_copy(
            src_ref=self.own.at[1, self.index],
            dst_ref=self.inbox.at[self.index],
            send_sem=self.core_send.at[self.index],
            recv_sem=self.core_recv.at[self.index],
            device_id=sibling,
            device_id_type=MESH,
        )

    def mesh_copy(self, step, partners):
        count = 32 >> step
        return pltpu.make_async_remote_copy(
            src_ref=self.own.at[0, self.index, pl.ds(count, count)],
            dst_ref=self.mesh_in.at[self.index, pl.ds(count, count)],
            send_sem=self.mesh_send.at[self.index, step],
            recv_sem=self.mesh_recv.at[self.index, step],
            device_id=partners[(self.flow + step) % 6],
            device_id_type=MESH,
        )

    def add(self, inbox, source_first, first, count):
        own, index = self.own, self.index
        rows = own.shape[3]
        chunk = min(count, max(1, 128 // rows))

        def body(turn, carry):
            at = first + turn * chunk
            own[0, index, pl.ds(at, chunk)] = (
                own[0, index, pl.ds(at, chunk)]
                + inbox[index, pl.ds(source_first + turn * chunk, chunk)]
            )
            return carry

        lax.fori_loop(0, count // chunk, body, 0)

    def after_core(self, partners, sibling):
        self.core_copy(sibling).wait_recv()
        self.add(self.inbox, 0, 0, 64)
        if self.mesh_in is not self.inbox:
            return
        for step in range(6):
            pl.semaphore_signal(
                self.credit.at[self.index, step],
                inc=1,
                device_id=partners[(self.flow + step) % 6],
                device_id_type=MESH,
            )

    def send_mesh(self, step, partners):
        if self.mesh_in is self.inbox:
            pl.semaphore_wait(self.credit.at[self.index, step], 1)
        self.mesh_copy(step, partners).start()

    def after_mesh(self, step, partners, total):
        self.mesh_copy(step, partners).wait_recv()
        count = 32 >> step
        if step < 5:
            half = count // 2
            self.add(self.mesh_in, count + half, half, half)
            self.send_mesh(step + 1, partners)
            self.add(self.mesh_in, count, 0, half)
        else:
            rows = self.own.shape[3]
            total[pl.ds(self.total_at, rows)] = self.own[0, self.index, 0].astype(
                jnp.float32
            ) + self.mesh_in[self.index, 1].astype(jnp.float32)

    def finish(self, partners, sibling):
        self.core_copy(sibling).wait_send()
        for step in range(6):
            self.mesh_copy(step, partners).wait_send()


def put(box, core, flow, slot, piece):
    rows = piece.shape[0] // 2
    for half in range(2):
        box[(core + half) % 2, flow, slot] = piece[rows * half : rows * half + rows]


def down_payload(group, slots, core, a3t, activated, ubuf):
    slot = slots.of_group(group)
    lane = lax.broadcasted_iota(jnp.int32, (96, 128), 1)
    tiles = dot(a3t[...], activated[:, pl.ds(pl.multiple_of(384 * group, 128), 384)])
    for c in range(8):
        q, odd = c % 4, c // 4
        main = tiles[192 * q : 192 * q + 192, 256 * odd : 256 * odd + 128].astype(jnp.bfloat16)
        first = tiles[192 * q : 192 * q + 96, 128:256]
        second = tiles[192 * q + 96 : 192 * q + 192, 128:256]
        if odd:
            packed = jnp.where(lane < 64, pltpu.roll(first, 64, 1), second)
        else:
            packed = jnp.where(lane < 64, first, pltpu.roll(second, 64, 1))
        put(ubuf, core, 3, slot(c, 3), main[:96])
        put(ubuf, core, 4, slot(c, 4), main[96:])
        put(ubuf, core, 5, slot(c, 5), packed.astype(jnp.bfloat16))


def up_payload(c, slots, core, a2t, d_up, ubuf):
    slot = slots.of_column(c)
    tiles = dot(a2t[...], d_up[:, pl.ds(pl.multiple_of(384 * c, 128), 384)]).astype(jnp.bfloat16)
    for group in range(8):
        for flow in range(3):
            put(
                ubuf,
                core,
                flow,
                slot(group, flow),
                tiles[96 * group : 96 * group + 96, 128 * flow : 128 * flow + 128],
            )


def qkv_payload(c, slots, core, a1t, d_qkv_t, qbuf):
    slot = slots.of_column(c)
    first = pl.multiple_of(288 * c, 32)
    second = pl.multiple_of(288 * c + 144, 16)
    columns = jnp.concatenate(
        [d_qkv_t[pl.ds(first, 128), :], d_qkv_t[pl.ds(second, 128), :]], axis=0
    )
    tiles = dot_nt(a1t[...], columns).astype(jnp.bfloat16)
    for group in range(8):
        for flow in range(FLOWS):
            at = 96 * group + 16 * flow
            for half in range(2):
                qbuf[(core + half) % 2, flow, slot(group, flow)] = tiles[
                    at : at + 16, 128 * half : 128 * half + 128
                ]


def rest_payload(slots, core, a1t, d_qkv_t, rbuf):
    columns = jnp.concatenate(
        [d_qkv_t[144 * block + 128 : 144 * block + 144] for block in range(16)], axis=0
    )
    tiles = dot_nt(a1t[...], columns)
    slot = slots.table(range(4), range(2), range(2), range(4))
    blank = jnp.zeros((256, 32), jnp.bfloat16)
    for group in range(8):
        turned = tiles[96 * group : 96 * group + 96].T.astype(jnp.bfloat16)
        turned = jnp.concatenate([turned, blank], axis=1)
        for c in range(8):
            for half in range(2):
                at = 32 * c + 16 * half
                rbuf[(core + half) % 2, 0, slot(c // 2, c % 2, group // 4, group % 4, 0)] = turned[
                    at : at + 16
                ]


def exact(left, right):
    return jnp.dot(
        left, right, precision=lax.Precision.HIGHEST, preferred_element_type=jnp.float32
    )


def up_blocks(sums, core, part_odd):
    first, odd = core == 0, part_odd == 1
    left, middle, right, main_0, main_1, packed = [
        jnp.concatenate([sums[0, 48 * at : 48 * at + 48], sums[1, 48 * at : 48 * at + 48]], axis=0)
        for at in range(6)
    ]
    up = jnp.where(
        first,
        jnp.concatenate([left, middle], axis=1),
        pltpu.roll(jnp.concatenate([middle, right], axis=1), 192, 1),
    )[:, :192]
    main = jnp.where(first, main_0, main_1)
    turned = pltpu.roll(packed, 64, 1)
    low, high = jnp.where(first, packed, turned), jnp.where(first, turned, packed)
    down = jnp.where(
        odd,
        pltpu.roll(jnp.concatenate([high, main], axis=1), 192, 1),
        jnp.concatenate([main, low], axis=1),
    )[:, :192]
    return up, down


def qkv_block(sums):
    rest = jnp.concatenate([sums[96:112], jnp.zeros((112, 128), jnp.float32)], axis=0).T[:96]
    return jnp.concatenate([sums[0:96], rest], axis=1)[:, :144]


def stats_kernel(
    scaling,
    mixed_in,
    d_tokens_in,
    up_sums,
    qkv_sums,
    left_qkv,
    right_qkv,
    left_up,
    right_up,
    left_down,
    right_down,
    mixed,
    d_tokens,
    new_left_qkv,
    new_right_qkv,
    new_left_up,
    new_right_up,
    new_left_down,
    new_right_down,
):
    col = lax.axis_index("cols")
    core = col % 2
    mixed[...] = mixed_in[...]
    d_tokens[...] = d_tokens_in[...]
    up_own, down_own = up_blocks(up_sums, core, (col // 8) % 2)
    up_own, down_own = up_own * scaling, down_own * scaling
    up_turned, down_turned = up_own.T, down_own.T
    new_left_up[0] = left_up[0] + exact(up_own, up_turned) / 192
    new_right_up[0] = right_up[0] + exact(up_turned, up_own) / 96
    new_left_down[0] = left_down[0] + exact(down_turned, down_own) / 96
    new_right_down[0] = right_down[0] + exact(down_own, down_turned) / 192
    qkv_own = qkv_block(qkv_sums) * scaling
    qkv_turned = qkv_own.T
    new_left_qkv[0] = left_qkv[0] + exact(qkv_own, qkv_turned) / 144
    new_right_qkv[0] = right_qkv[0] + exact(qkv_turned, qkv_own) / 96


def exchange(source, target, sems, device):
    return pltpu.make_async_remote_copy(
        src_ref=source,
        dst_ref=target,
        send_sem=sems[0],
        recv_sem=sems[1],
        device_id=device,
        device_id_type=MESH,
    )


def gain_row(gain):
    return gain[...].reshape(1, MODEL)


def diagonal(first, second):
    return jnp.concatenate(
        [
            jnp.concatenate([first, jnp.zeros_like(second)], axis=1),
            jnp.concatenate([jnp.zeros_like(first), second], axis=1),
        ],
        axis=0,
    )


def whole_kernel(*refs):
    refs = list(refs)

    def take(count):
        taken = refs[:count]
        del refs[:count]
        return taken

    tokens, cotangent, gain_attn, gain_mlp, sides, corners, sides_t, corners_t = take(8)
    weight_refs = take(4)
    mixed, d_tokens, up_sums, qkv_sums = take(4)
    w_qkv, w_out, w_up, w_down = take(4)
    near, packed, kv, query, query_t, chances, hidden, attended_t = take(8)
    d_attended, d_attended_t, d_norm_own, d_side_in, d_band_in = take(5)
    d_far, d_band = near, packed
    a1t, a2t, a3t, d_up, activated, d_qkv_t = take(6)
    ubuf, ubox, qbuf, qbox, qmesh, rbuf, rbox, rmesh = take(8)
    total_up, other_up = take(2)
    weight_sems, halo_send, halo_recv, back_send, back_recv = take(5)
    up_sems, qkv_sems, rest_sems = take(5), take(5), take(5)
    last_sems = take(2)

    row, col = lax.axis_index("rows"), lax.axis_index("cols")
    rows, cols = lax.axis_size("rows"), lax.axis_size("cols")
    above, below = ((row + rows - 1) % rows, col), ((row + 1) % rows, col)
    to_left, to_right = (row, (col + cols - 1) % cols), (row, (col + 1) % cols)
    x, y, z, core = my_place()
    sibling = device_at(x, y, z, 1 - core)
    partners = link_partners(x, y, z, core)
    slots = Slots(link_bits(x, y, z))
    barrier = pltpu.get_barrier_semaphore()
    for place in (above, below, to_left, to_right, sibling) + partners:
        pl.semaphore_signal(barrier, inc=1, device_id=place, device_id_type=MESH)
    loads = [
        pltpu.make_async_copy(weight_refs[at], place, weight_sems.at[at])
        for at, place in ((0, w_qkv), (1, w_out), (3, w_down), (2, w_up))
    ]
    loads[0].start()

    def copies(routes, first_sem, send, recv):
        return [
            pltpu.make_async_remote_copy(
                src_ref=source,
                dst_ref=target,
                send_sem=send.at[first_sem + at],
                recv_sem=recv.at[first_sem + at],
                device_id=device,
                device_id_type=MESH,
            )
            for at, (source, target, device) in enumerate(routes)
        ]

    def part(ref, first, count):
        return ref.at[pl.ds(first, count)]

    packed[:192] = dot(sides[...], tokens[...]).astype(jnp.bfloat16)
    pl.semaphore_wait(barrier, 11)
    near_copies = copies(
        (
            (part(tokens, 0, 96), part(near, BOTTOM, 96), above),
            (part(tokens, TOKENS - 96, 96), part(near, TOP, 96), below),
            (part(packed, 0, 96), part(near, RIGHT, 96), to_left),
            (part(packed, 96, 96), part(near, LEFT, 96), to_right),
        ),
        0,
        halo_send,
        halo_recv,
    )
    for copy in near_copies:
        copy.start()
    corner_copies = copies(
        (
            (part(packed, 192, 48), part(near, TOP_CORNERS + 48, 48), to_left),
            (part(packed, 240, 48), part(near, LOW_CORNERS + 48, 48), to_left),
            (part(packed, 288, 48), part(near, TOP_CORNERS, 48), to_right),
            (part(packed, 336, 48), part(near, LOW_CORNERS, 48), to_right),
        ),
        4,
        halo_send,
        halo_recv,
    )

    wide = tokens[...].astype(jnp.float32)
    normed_attn = (wide * inverse_rms(wide) * gain_row(gain_attn)).astype(jnp.bfloat16)
    near[OWN:LOW_CORNERS] = normed_attn
    a3t[...] = cotangent[...].T
    key_row, key_col = key_places()
    key_row, key_col = row * TILE + key_row, col * TILE + key_col
    for half in range(2):
        at = lax.broadcasted_iota(jnp.int32, (1, 128), 1) + 128 * half
        row_first = jnp.clip(row * TILE + at // TILE - window_half, 0, rows * TILE - window_span)
        col_first = jnp.clip(col * TILE + at % TILE - window_half, 0, cols * TILE - window_span)
        spot_row = key_row[LATER * half : LATER * half + SPAN]
        spot_col = key_col[LATER * half : LATER * half + SPAN]
        visible = (
            (spot_row >= row_first)
            & (spot_row < row_first + window_span)
            & (spot_col >= col_first)
            & (spot_col < col_first + window_span)
        )
        hidden[half] = jnp.where(visible, 0.0, -1e30)

    loads[0].wait()
    for load in loads[1:]:
        load.start()
    own_query = dot(normed_attn, w_qkv[:, :MODEL]).astype(jnp.bfloat16)
    own_query = (own_query.astype(jnp.float32) * 0.125).astype(jnp.bfloat16)
    query[...] = own_query
    query_t[...] = own_query.T
    kv[OWN:LOW_CORNERS] = dot(normed_attn, w_qkv[:, MODEL:]).astype(jnp.bfloat16)
    a1t[:, OWN:LOW_CORNERS] = normed_attn.T

    for copy in near_copies[:2]:
        copy.wait_recv()
    packed[192:384] = (
        dot(corners[:, :96], near[TOP:TOP_CORNERS]) + dot(corners[:, 96:], near[BOTTOM:KEYS])
    ).astype(jnp.bfloat16)
    for copy in corner_copies:
        copy.start()
    for copy in near_copies[2:] + corner_copies:
        copy.wait_recv()
    for first, last in ((TOP, OWN), (LOW_CORNERS, KEYS)):
        halo = near[first:last].astype(jnp.float32)
        halo = (halo * inverse_rms(halo) * gain_row(gain_attn)).astype(jnp.bfloat16)
        near[first:last] = halo
        kv[first:last] = dot(halo, w_qkv[:, MODEL:]).astype(jnp.bfloat16)
        a1t[:, first:last] = halo.T

    def spans(half):
        return pl.ds(LATER * half, SPAN)

    def attend(pair, carry):
        lanes = pl.ds(pl.multiple_of(pair * 128, 128), 128)
        value_lanes = pl.ds(pl.multiple_of(MODEL + pair * 128, 128), 128)
        queries = query_t[lanes, :]
        for half in range(2):
            columns = slice(128 * half, 128 * half + 128)
            both = diagonal(queries[:64, columns], queries[64:, columns])
            bias = jnp.concatenate([hidden[half], hidden[half]], axis=1)
            scores = dot(kv[spans(half), lanes], both) + bias
            most = jnp.max(scores, axis=0, keepdims=True)
            powers = jnp.exp(scores - most)
            total = jnp.sum(powers, axis=0, keepdims=True)
            weights = (powers * (1.0 / total)).astype(jnp.bfloat16)
            chances[pair, half] = weights
            blended = dot(kv[spans(half), value_lanes].T, weights).astype(jnp.bfloat16)
            attended_t[lanes, columns] = jnp.concatenate(
                [blended[:64, :128], blended[64:, 128:]], axis=0
            )
        return carry

    lax.fori_loop(0, PAIRS, attend, 0)

    for load in loads[1:]:
        load.wait()
    wide = tokens[...].astype(jnp.float32)
    residual = (wide + dot(attended_t[...].T, w_out[...])).astype(jnp.bfloat16)
    residual_wide = residual.astype(jnp.float32)
    scale_mlp = inverse_rms(residual_wide)
    normed_mlp = (residual_wide * scale_mlp * gain_row(gain_mlp)).astype(jnp.bfloat16)
    a2t[...] = normed_mlp.T
    mix = residual_wide
    d_normed = jnp.zeros((TOKENS, MODEL), jnp.float32)
    slope = float(np.sqrt(2 / np.pi))
    for step in range(6):
        units = slice(512 * step, 512 * step + 512)
        up = dot(normed_mlp, w_up[:, units])
        d_act = dot_nt(cotangent[...], w_down[units])
        square = up * up
        tanh = jnp.tanh(slope * up * (1.0 + 0.044715 * square))
        grown = 0.5 * (1.0 + tanh)
        active = (up * grown).astype(jnp.bfloat16)
        activated[:, units] = active
        mix = mix + dot(active, w_down[units])
        steep = grown + 0.5 * up * (1.0 - tanh * tanh) * (
            slope * (1.0 + 3 * 0.044715 * square)
        )
        d_up_part = (d_act * steep).astype(jnp.bfloat16)
        d_up[:, units] = d_up_part
        d_normed = d_normed + dot_nt(d_up_part, w_up[:, units])
    mixed[...] = mix.astype(jnp.bfloat16)

    up_channels = [
        Channel(ubuf, ubox, ubox, up_sems, flow, flow, 48 * flow) for flow in range(FLOWS)
    ]
    early, late = up_channels[3:], up_channels[:3]
    qkv_channels = [
        Channel(qbuf, qbox, qmesh, qkv_sems, flow, flow, 16 * flow) for flow in range(FLOWS)
    ] + [Channel(rbuf, rbox, rmesh, rest_sems, 0, 0, 96)]

    def loop(count, body):
        def turn(at, carry):
            body(at)
            return carry

        lax.fori_loop(0, count, turn, 0)

    loop(8, lambda group: down_payload(group, slots, core, a3t, activated, ubuf))
    for channel in early:
        channel.core_copy(sibling).start()
    loop(8, lambda c: up_payload(c, slots, core, a2t, d_up, ubuf))
    for channel in late:
        channel.core_copy(sibling).start()

    d_residual = (
        cotangent[...].astype(jnp.float32)
        + norm_back(residual_wide, scale_mlp, gain_row(gain_mlp), d_normed)
    ).astype(jnp.bfloat16)
    d_tokens[...] = d_residual
    d_att = dot_nt(d_residual, w_out[...]).astype(jnp.bfloat16)
    d_attended[...] = d_att
    d_attended_t[...] = d_att.T
    d_qkv_t[:MODEL, :OWN] = jnp.zeros((MODEL, OWN), jnp.bfloat16)
    d_qkv_t[:MODEL, LOW_CORNERS:] = jnp.zeros((MODEL, KEYS - LOW_CORNERS), jnp.bfloat16)

    masks = lane_masks()

    def attend_back(pair):
        lanes = pl.ds(pl.multiple_of(pair * 128, 128), 128)
        key_lanes = pl.ds(pl.multiple_of(MODEL + pair * 128, 128), 128)
        value_lanes = pl.ds(pl.multiple_of(2 * MODEL + pair * 128, 128), 128)
        upstream_t = d_attended_t[lanes, :]
        products = upstream_t.astype(jnp.float32) * attended_t[lanes, :].astype(jnp.float32)
        deltas = [
            jnp.sum(products[64 * second : 64 * second + 64], axis=0, keepdims=True)
            for second in range(2)
        ]
        d_keys, d_values, d_query = [], [], []
        for half in range(2):
            columns = slice(128 * half, 128 * half + 128)
            weights = chances[pair, half]
            both = diagonal(upstream_t[:64, columns], upstream_t[64:, columns])
            delta = jnp.concatenate([delta[:, columns] for delta in deltas], axis=1)
            d_prob = dot(kv[spans(half), key_lanes], both)
            d_score = (weights.astype(jnp.float32) * (d_prob - delta)).astype(jnp.bfloat16)
            crossed = dot(kv[spans(half), lanes].T, d_score)
            d_query.append(jnp.concatenate([crossed[:64, :128], crossed[64:, 128:]], axis=0))
            asked = query[columns, lanes]
            d_keys.append(
                dot(d_score, jnp.concatenate([asked * masks[0], asked * masks[1]], axis=0))
            )
            sought = d_attended[columns, lanes]
            d_values.append(
                dot(weights, jnp.concatenate([sought * masks[0], sought * masks[1]], axis=0))
            )
        d_qkv_t[lanes, OWN:LOW_CORNERS] = (
            jnp.concatenate(d_query, axis=1) * 0.125
        ).astype(jnp.bfloat16)
        for place, (one, two) in ((key_lanes, d_keys), (value_lanes, d_values)):
            summed = jnp.concatenate(
                [one[:LATER], one[LATER:] + two[: SPAN - LATER], two[SPAN - LATER :]], axis=0
            )
            d_qkv_t[place, :] = summed.astype(jnp.bfloat16).T

    def after_core(channels):
        for channel in channels:
            channel.after_core(partners, sibling)
        for channel in channels:
            channel.send_mesh(0, partners)

    def after_mesh(channels, step, total):
        for channel in channels:
            channel.after_mesh(step, partners, total)

    after_core(early)
    loop(2, attend_back)
    after_core(late)
    loop(4, lambda pair: attend_back(pair + 2))
    after_mesh(early, 0, total_up)

    loop(8, lambda c: qkv_payload(c, slots, core, a1t, d_qkv_t, qbuf))
    rest_payload(slots, core, a1t, d_qkv_t, rbuf)
    for channel in qkv_channels:
        channel.core_copy(sibling).start()
    after_mesh(late, 0, total_up)
    after_mesh(early, 1, total_up)

    for step in range(3):
        lines = slice(256 * step, 256 * step + 256)
        piece = dot(w_qkv[lines, :], d_qkv_t[...]).T
        d_norm_own[:, lines] = piece[OWN:LOW_CORNERS]
        for target, first, count in (
            (0, TOP, 96),
            (96, BOTTOM, 96),
            (192, LEFT, 96),
            (288, TOP_CORNERS, 48),
            (336, LOW_CORNERS, 48),
            (384, RIGHT, 96),
            (480, TOP_CORNERS + 48, 48),
            (528, LOW_CORNERS + 48, 48),
        ):
            d_far[target : target + count, lines] = piece[first : first + count].astype(
                jnp.bfloat16
            )
    side_copies = copies(
        (
            (part(d_far, 192, 192), part(d_side_in, 192, 192), to_left),
            (part(d_far, 384, 192), part(d_side_in, 0, 192), to_right),
        ),
        0,
        back_send,
        back_recv,
    )
    band_copies = copies(
        (
            (part(d_band, 0, 96), part(d_band_in, 96, 96), above),
            (part(d_band, 96, 96), part(d_band_in, 0, 96), below),
        ),
        2,
        back_send,
        back_recv,
    )
    for copy in side_copies:
        copy.start()

    after_core(qkv_channels)
    after_mesh(late, 1, total_up)
    after_mesh(early, 2, total_up)

    for copy in side_copies:
        copy.wait_recv()
    own = jnp.concatenate([d_side_in[0:96], d_side_in[192:288]], axis=0)
    far = jnp.concatenate([d_side_in[96:192], d_side_in[288:384]], axis=0)
    for copy in near_copies + corner_copies:
        copy.wait_send()
    d_band[0:192] = (d_far[0:192].astype(jnp.float32) + dot(corners_t[...], far)).astype(
        jnp.bfloat16
    )
    for copy in band_copies:
        copy.start()
    d_norm_own[...] = d_norm_own[...] + dot(sides_t[...], own)

    after_mesh(qkv_channels, 0, qkv_sums)
    after_mesh(late, 2, total_up)
    after_mesh(early, 3, total_up)
    after_mesh(qkv_channels, 1, qkv_sums)
    after_mesh(late, 3, total_up)
    after_mesh(early, 4, total_up)
    after_mesh(qkv_channels, 2, qkv_sums)
    after_mesh(late, 4, total_up)
    after_mesh(early, 5, total_up)
    after_mesh(qkv_channels, 3, qkv_sums)
    after_mesh(late, 5, total_up)
    up_last = exchange(total_up, other_up, last_sems[0:2], sibling)
    up_last.start()

    for copy in band_copies:
        copy.wait_recv()
    band = d_band_in[...].astype(jnp.float32)
    summed = d_norm_own[...]
    d_normed = jnp.concatenate(
        [summed[:96] + band[:96], summed[96:160], summed[160:] + band[96:]], axis=0
    )
    wide = tokens[...].astype(jnp.float32)
    d_tokens[...] = (
        d_tokens[...].astype(jnp.float32)
        + norm_back(wide, inverse_rms(wide), gain_row(gain_attn), d_normed)
    ).astype(jnp.bfloat16)

    after_mesh(qkv_channels, 4, qkv_sums)
    after_mesh(qkv_channels, 5, qkv_sums)
    first = core == 0
    up_last.wait_recv()
    up_sums[0] = jnp.where(first, total_up[...], other_up[...])
    up_sums[1] = jnp.where(first, other_up[...], total_up[...])

    for channel in up_channels + qkv_channels:
        channel.finish(partners, sibling)
    for copy in side_copies + band_copies + [up_last]:
        copy.wait_send()


def on_device(
    tokens,
    cotangent,
    gain_attn,
    gain_mlp,
    weight_qkv,
    weight_out,
    weight_up,
    weight_down,
    *stats,
):
    scaling = float(TOKENS * lax.axis_size("rows") * lax.axis_size("cols")) ** (-0.5)
    sides, corners = halo_tables()
    bf16, f32 = jnp.bfloat16, jnp.float32

    def vmem(kind, *shape):
        return pltpu.VMEM(shape, kind)

    def boxes(count, size):
        return [vmem(bf16, 2, count, CHIPS, size, 128), vmem(bf16, count, CHIPS, size, 128)]

    def sems_of(count):
        return [
            pltpu.SemaphoreType.DMA((count,)),
            pltpu.SemaphoreType.DMA((count,)),
            pltpu.SemaphoreType.DMA((count, 6)),
            pltpu.SemaphoreType.DMA((count, 6)),
            pltpu.SemaphoreType.REGULAR((count, 6)),
        ]

    in_vmem = pl.BlockSpec(memory_space=pltpu.VMEM)
    tile = jax.ShapeDtypeStruct((TOKENS, MODEL), bf16)
    mixed, d_tokens, up_sums, qkv_sums = pl.pallas_call(
        whole_kernel,
        out_shape=[
            tile,
            tile,
            jax.ShapeDtypeStruct((2, 288, 128), f32),
            jax.ShapeDtypeStruct((112, 128), f32),
        ],
        in_specs=[in_vmem] * 8 + [pl.BlockSpec(memory_space=pl.ANY)] * 4,
        out_specs=[in_vmem] * 4,
        scratch_shapes=[
            vmem(bf16, MODEL, 3 * MODEL),
            vmem(bf16, MODEL, MODEL),
            vmem(bf16, MODEL, HIDDEN),
            vmem(bf16, HIDDEN, MODEL),
            vmem(bf16, KEYS, MODEL),
            vmem(bf16, 384, MODEL),
            vmem(bf16, KEYS, 2 * MODEL),
            vmem(bf16, TOKENS, MODEL),
            vmem(bf16, MODEL, TOKENS),
            vmem(bf16, PAIRS, 2, SPAN, 256),
            vmem(f32, 2, SPAN, 128),
            vmem(bf16, MODEL, TOKENS),
            vmem(bf16, TOKENS, MODEL),
            vmem(bf16, MODEL, TOKENS),
            vmem(f32, TOKENS, MODEL),
            vmem(bf16, 384, MODEL),
            vmem(bf16, 192, MODEL),
            vmem(bf16, MODEL, KEYS),
            vmem(bf16, MODEL, TOKENS),
            vmem(bf16, MODEL, TOKENS),
            vmem(bf16, TOKENS, HIDDEN),
            vmem(bf16, TOKENS, HIDDEN),
            vmem(bf16, 3 * MODEL, KEYS),
        ]
        + boxes(6, 48)
        + boxes(6, 16)
        + [vmem(bf16, 6, CHIPS, 16, 128)]
        + boxes(1, 16)
        + [vmem(bf16, 1, CHIPS, 16, 128)]
        + [vmem(f32, 288, 128), vmem(f32, 288, 128)]
        + [
            pltpu.SemaphoreType.DMA((4,)),
            pltpu.SemaphoreType.DMA((8,)),
            pltpu.SemaphoreType.DMA((8,)),
            pltpu.SemaphoreType.DMA((4,)),
            pltpu.SemaphoreType.DMA((4,)),
        ]
        + sems_of(6)
        + sems_of(6)
        + sems_of(1)
        + [pltpu.SemaphoreType.DMA] * 2,
        compiler_params=pltpu.CompilerParams(
            collective_id=0, has_side_effects=True, vmem_limit_bytes=63 * 2**20 + 2**18
        ),
    )(
        tokens.reshape(TOKENS, MODEL),
        cotangent.reshape(TOKENS, MODEL),
        gain_attn,
        gain_mlp,
        jnp.asarray(sides, bf16),
        jnp.asarray(corners, bf16),
        jnp.asarray(sides.T, bf16),
        jnp.asarray(corners.T, bf16),
        weight_qkv,
        weight_out,
        weight_up,
        weight_down,
    )
    mixed, d_tokens, *new_stats = pl.pallas_call(
        functools.partial(stats_kernel, scaling),
        out_shape=[tile, tile] + [jax.ShapeDtypeStruct(stat.shape, f32) for stat in stats],
        in_specs=[in_vmem] * 10,
        out_specs=[in_vmem] * 8,
        compiler_params=pltpu.CompilerParams(vmem_limit_bytes=62 * 2**20 + 2**19),
    )(mixed, d_tokens, up_sums, qkv_sums, *stats)
    return (
        mixed.reshape(TILE, TILE, MODEL),
        d_tokens.reshape(TILE, TILE, MODEL),
        *new_stats,
    )


def solution(mesh):
    in_specs = (
        P("rows", "cols", None),
        P("rows", "cols", None),
        P(),
        P(),
        P(),
        P(),
        P(),
        P(),
        P(("rows", "cols"), None, None),
        P(("rows", "cols"), None, None),
        P(("rows", "cols"), None, None),
        P(("rows", "cols"), None, None),
        P(("rows", "cols"), None, None),
        P(("rows", "cols"), None, None),
    )
    out_specs = (
        P("rows", "cols", None),
        P("rows", "cols", None),
        P(("rows", "cols"), None, None),
        P(("rows", "cols"), None, None),
        P(("rows", "cols"), None, None),
        P(("rows", "cols"), None, None),
        P(("rows", "cols"), None, None),
        P(("rows", "cols"), None, None),
    )
    return jax.shard_map(
        on_device, mesh=mesh, in_specs=in_specs, out_specs=out_specs, check_vma=False
    )
```

```python
import functools

import jax
import jax.numpy as jnp
import numpy as np
from jax import lax
from jax.experimental import pallas as pl
from jax.experimental.pallas import tpu as pltpu
from jax.sharding import PartitionSpec as P

HEADS = 12
PAIRS = 6
MODEL = 768
HIDDEN = 3072
TILE = 16
TOKENS = TILE * TILE
FLOWS = 6
CHIPS = 64
TOP, TOP_CORNERS, LEFT, RIGHT, OWN, LOW_CORNERS, BOTTOM, KEYS = 0, 96, 192, 288, 384, 640, 736, 832
SPAN = 640
LATER = KEYS - SPAN

epsilon = 1e-06
window_half = 6
window_span = 13
MESH = pl.DeviceIdType.MESH


def halo_tables():
    sides = np.zeros((192, TOKENS), np.float32)
    corners = np.zeros((192, 192), np.float32)
    for side, first in enumerate((0, TILE - 6)):
        for r in range(TILE):
            for c in range(6):
                sides[96 * side + r * 6 + c, r * TILE + first + c] = 1
        for band in range(2):
            for r in range(6):
                for c in range(6):
                    at = 48 * band + r * 6 + c
                    corners[96 * side + at, 96 * band + r * TILE + first + c] = 1
    return sides, corners


def key_places():
    key = lax.broadcasted_iota(jnp.int32, (KEYS, 1), 0)
    in_band = (key < TOP_CORNERS) | (key >= BOTTOM) | ((key >= OWN) & (key < LOW_CORNERS))
    band = key - jnp.where(key < TOP_CORNERS, TOP, jnp.where(key >= BOTTOM, BOTTOM, OWN))
    shift = jnp.where(key < TOP_CORNERS, -6, jnp.where(key >= BOTTOM, TILE, 0))
    band_row, band_col = band // TILE + shift, band % TILE
    low = key >= LOW_CORNERS
    in_corner = (key < LEFT) | low
    corner = key - jnp.where(low, LOW_CORNERS, TOP_CORNERS)
    on_right = jnp.where(in_corner, corner, key - LEFT - 48) >= 48
    at = jnp.where(
        in_corner, corner - jnp.where(on_right, 48, 0), key - jnp.where(key >= RIGHT, RIGHT, LEFT)
    )
    sixth = (at * 171) >> 10
    side_row = sixth + jnp.where(in_corner, jnp.where(low, TILE, -6), 0)
    side_col = at - 6 * sixth + jnp.where(on_right, TILE, -6)
    unused = in_corner & (at >= 36)
    key_row = jnp.where(in_band, band_row, jnp.where(unused, -1000, side_row))
    return key_row, jnp.where(in_band, band_col, side_col)


def dot(left, right):
    return jnp.dot(left, right, preferred_element_type=jnp.float32)


def dot_nt(left, right):
    return lax.dot_general(
        left, right, (((1,), (1,)), ((), ())), preferred_element_type=jnp.float32
    )


def inverse_rms(wide):
    return lax.rsqrt(jnp.mean(wide * wide, axis=-1, keepdims=True) + epsilon)


def norm_back(wide, scale, gain, upstream):
    scaled = upstream * gain
    return scale * scaled - wide * (
        scale * scale * scale * jnp.mean(wide * scaled, axis=-1, keepdims=True)
    )


def lane_masks():
    lane = lax.broadcasted_iota(jnp.int32, (1, 128), 1)
    low = jnp.where(lane < 64, 1.0, 0.0)
    return low.astype(jnp.bfloat16), (1.0 - low).astype(jnp.bfloat16)


def gray_bits(position):
    high = position // 2
    return (high, (high + position % 2) % 2)


def my_place():
    row = lax.axis_index("rows")
    col = lax.axis_index("cols")
    core = col % 2
    x = col // 4
    y = (row // 4) * 2 + (col // 2) % 2
    z = row % 4
    return x, y, z, core


def device_at(x, y, z, core):
    return ((y // 2) * 4 + z, x * 4 + (y % 2) * 2 + core)


def link_bits(x, y, z):
    gx, gy, gz = gray_bits(x), gray_bits(y), gray_bits(z)
    return (gx[1], gy[1], gz[1], gx[0], gy[0], gz[0])


def link_partners(x, y, z, core):
    return (
        device_at(x + 1 - 2 * (x % 2), y, z, core),
        device_at(x, y + 1 - 2 * (y % 2), z, core),
        device_at(x, y, z + 1 - 2 * (z % 2), core),
        device_at(3 - x, y, z, core),
        device_at(x, 3 - y, z, core),
        device_at(x, y, 3 - z, core),
    )


def link_of(flow, step):
    return (flow + step) % 3 + 3 * ((flow // 3 + step // 3) % 2)


def slot_terms(mine, theirs, axis):
    near = (mine[axis] + theirs[1]) % 2
    far = (mine[axis + 3] + theirs[0]) % 2
    terms = []
    for flow in range(FLOWS):
        weight = {link_of(flow, step): 32 >> step for step in range(6)}
        terms.append(near * weight[axis] + far * weight[axis + 3])
    return terms


def cube_place(flow, slot, x, y, z, core):
    places = [x, y, z]
    for step in range(3):
        if (slot >> (2 - step)) & 1:
            link = link_of(flow, 3 + step)
            at = places[link % 3]
            places[link % 3] = 3 - at if link >= 3 else at + 1 - 2 * (at % 2)
    return device_at(places[0], places[1], places[2], core)


class Slots:
    def __init__(self, mine):
        self.mine = mine

    def terms(self, axis, position):
        return slot_terms(self.mine, gray_bits(position), axis)

    def table(self, xs, y_los, y_his, zs):
        along_x = {at: self.terms(0, x) for at, x in enumerate(xs)}
        along_y = {
            (i, j): self.terms(1, y_hi * 2 + y_lo)
            for i, y_hi in enumerate(y_his)
            for j, y_lo in enumerate(y_los)
        }
        along_z = {at: self.terms(2, z) for at, z in enumerate(zs)}
        return lambda x, y_lo, y_hi, z, flow: (
            along_x[x][flow] + along_y[y_hi, y_lo][flow] + along_z[z][flow]
        )

    def of_group(self, group):
        slot = self.table(range(4), range(2), [group // 4], [group % 4])
        return lambda c, flow: slot(c // 2, c % 2, 0, 0, flow)

    def of_column(self, c):
        slot = self.table([c // 2], [c % 2], range(2), range(4))
        return lambda group, flow: slot(0, 0, group // 4, group % 4, flow)


class Channel:
    def __init__(self, own, inbox, mesh_in, cube_in, sems, index, flow, total_at):
        self.own, self.inbox, self.mesh_in, self.cube_in = own, inbox, mesh_in, cube_in
        self.core_send, self.core_recv, self.mesh_send, self.mesh_recv, self.credit = sems
        self.index, self.flow, self.total_at = index, flow, total_at

    def core_copy(self, sibling):
        return pltpu.make_async_remote_copy(
            src_ref=self.own.at[1, self.index],
            dst_ref=self.inbox.at[self.index],
            send_sem=self.core_send.at[self.index],
            recv_sem=self.core_recv.at[self.index],
            device_id=sibling,
            device_id_type=MESH,
        )

    def mesh_copy(self, step, partners):
        count = 32 >> step
        return pltpu.make_async_remote_copy(
            src_ref=self.own.at[0, self.index, pl.ds(count, count)],
            dst_ref=self.mesh_in.at[self.index, pl.ds(count, count)],
            send_sem=self.mesh_send.at[self.index, step],
            recv_sem=self.mesh_recv.at[self.index, step],
            device_id=partners[link_of(self.flow, step)],
            device_id_type=MESH,
        )

    def cube_copy(self, slot, count, place):
        return pltpu.make_async_remote_copy(
            src_ref=self.own.at[0, self.index, pl.ds(slot, count)],
            dst_ref=self.cube_in.at[self.index, pl.ds(slot, count)],
            send_sem=self.mesh_send.at[self.index, 3],
            recv_sem=self.mesh_recv.at[self.index, 3],
            device_id=place,
            device_id_type=MESH,
        )

    def add(self, inbox, source_first, first, count):
        own, index = self.own, self.index
        rows = own.shape[3]
        chunk = min(count, max(1, 128 // rows))

        def body(turn, carry):
            at = first + turn * chunk
            own[0, index, pl.ds(at, chunk)] = (
                own[0, index, pl.ds(at, chunk)]
                + inbox[index, pl.ds(source_first + turn * chunk, chunk)]
            )
            return carry

        lax.fori_loop(0, count // chunk, body, 0)

    def after_core(self, partners, sibling):
        self.core_copy(sibling).wait_recv()
        self.add(self.inbox, 0, 0, 64)
        if self.mesh_in is not self.inbox:
            return
        for step in range(3):
            pl.semaphore_signal(
                self.credit.at[self.index, step],
                inc=1,
                device_id=partners[link_of(self.flow, step)],
                device_id_type=MESH,
            )

    def send_mesh(self, step, partners):
        if self.mesh_in is self.inbox:
            pl.semaphore_wait(self.credit.at[self.index, step], 1)
        self.mesh_copy(step, partners).start()

    def after_mesh(self, step, partners, cubes):
        self.mesh_copy(step, partners).wait_recv()
        count = 32 >> step
        half = count // 2
        if step < 2:
            self.add(self.mesh_in, count + half, half, half)
            self.send_mesh(step + 1, partners)
            self.add(self.mesh_in, count, 0, half)
        else:
            self.add(self.mesh_in, count, 0, count)
            for slot in range(1, 8):
                self.cube_copy(slot, 1, cubes[self.flow][slot]).start()

    def after_cube(self, sibling, total):
        self.cube_copy(1, 7, sibling).wait_recv()
        summed = self.own[0, self.index, 0].astype(jnp.float32)
        for slot in range(1, 8):
            summed = summed + self.cube_in[self.index, slot].astype(jnp.float32)
        total[pl.ds(self.total_at, self.own.shape[3])] = summed

    def finish(self, partners, sibling):
        self.core_copy(sibling).wait_send()
        for step in range(3):
            self.mesh_copy(step, partners).wait_send()
        self.cube_copy(1, 7, sibling).wait_send()


def put(box, core, flow, slot, piece):
    rows = piece.shape[0] // 2
    for half in range(2):
        box[(core + half) % 2, flow, slot] = piece[rows * half : rows * half + rows]


def down_payload(group, slots, core, a3t, activated, ubuf):
    slot = slots.of_group(group)
    lane = lax.broadcasted_iota(jnp.int32, (96, 128), 1)
    tiles = dot(a3t[...], activated[:, pl.ds(pl.multiple_of(384 * group, 128), 384)])
    for c in range(8):
        q, odd = c % 4, c // 4
        main = tiles[192 * q : 192 * q + 192, 256 * odd : 256 * odd + 128].astype(jnp.bfloat16)
        first = tiles[192 * q : 192 * q + 96, 128:256]
        second = tiles[192 * q + 96 : 192 * q + 192, 128:256]
        if odd:
            packed = jnp.where(lane < 64, pltpu.roll(first, 64, 1), second)
        else:
            packed = jnp.where(lane < 64, first, pltpu.roll(second, 64, 1))
        put(ubuf, core, 3, slot(c, 3), main[:96])
        put(ubuf, core, 4, slot(c, 4), main[96:])
        put(ubuf, core, 5, slot(c, 5), packed.astype(jnp.bfloat16))


def up_payload(c, slots, core, a2t, d_up, ubuf):
    slot = slots.of_column(c)
    tiles = dot(a2t[...], d_up[:, pl.ds(pl.multiple_of(384 * c, 128), 384)]).astype(jnp.bfloat16)
    for group in range(8):
        for flow in range(3):
            put(
                ubuf,
                core,
                flow,
                slot(group, flow),
                tiles[96 * group : 96 * group + 96, 128 * flow : 128 * flow + 128],
            )


def qkv_payload(c, slots, core, a1t, d_qkv_t, qbuf):
    slot = slots.of_column(c)
    first = pl.multiple_of(288 * c, 32)
    second = pl.multiple_of(288 * c + 144, 16)
    columns = jnp.concatenate(
        [d_qkv_t[pl.ds(first, 128), :], d_qkv_t[pl.ds(second, 128), :]], axis=0
    )
    tiles = dot_nt(a1t[...], columns).astype(jnp.bfloat16)
    for group in range(8):
        for flow in range(FLOWS):
            at = 96 * group + 16 * flow
            for half in range(2):
                qbuf[(core + half) % 2, flow, slot(group, flow)] = tiles[
                    at : at + 16, 128 * half : 128 * half + 128
                ]


def rest_payload(slots, core, a1t, d_qkv_t, rbuf):
    columns = jnp.concatenate(
        [d_qkv_t[144 * block + 128 : 144 * block + 144] for block in range(16)], axis=0
    )
    tiles = dot_nt(a1t[...], columns)
    slot = slots.table(range(4), range(2), range(2), range(4))
    blank = jnp.zeros((256, 32), jnp.bfloat16)
    for group in range(8):
        turned = tiles[96 * group : 96 * group + 96].T.astype(jnp.bfloat16)
        turned = jnp.concatenate([turned, blank], axis=1)
        for c in range(8):
            for half in range(2):
                at = 32 * c + 16 * half
                rbuf[(core + half) % 2, 0, slot(c // 2, c % 2, group // 4, group % 4, 0)] = turned[
                    at : at + 16
                ]


def exact(left, right):
    return jnp.dot(
        left, right, precision=lax.Precision.HIGHEST, preferred_element_type=jnp.float32
    )


def up_blocks(sums, core, part_odd):
    first, odd = core == 0, part_odd == 1
    left, middle, right, main_0, main_1, packed = [
        jnp.concatenate([sums[0, 48 * at : 48 * at + 48], sums[1, 48 * at : 48 * at + 48]], axis=0)
        for at in range(6)
    ]
    up = jnp.where(
        first,
        jnp.concatenate([left, middle], axis=1),
        pltpu.roll(jnp.concatenate([middle, right], axis=1), 192, 1),
    )[:, :192]
    main = jnp.where(first, main_0, main_1)
    turned = pltpu.roll(packed, 64, 1)
    low, high = jnp.where(first, packed, turned), jnp.where(first, turned, packed)
    down = jnp.where(
        odd,
        pltpu.roll(jnp.concatenate([high, main], axis=1), 192, 1),
        jnp.concatenate([main, low], axis=1),
    )[:, :192]
    return up, down


def qkv_block(sums):
    rest = jnp.concatenate([sums[96:112], jnp.zeros((112, 128), jnp.float32)], axis=0).T[:96]
    return jnp.concatenate([sums[0:96], rest], axis=1)[:, :144]


def stats_kernel(
    scaling,
    mixed_in,
    d_tokens_in,
    up_sums,
    qkv_sums,
    left_qkv,
    right_qkv,
    left_up,
    right_up,
    left_down,
    right_down,
    mixed,
    d_tokens,
    new_left_qkv,
    new_right_qkv,
    new_left_up,
    new_right_up,
    new_left_down,
    new_right_down,
):
    col = lax.axis_index("cols")
    core = col % 2
    mixed[...] = mixed_in[...]
    d_tokens[...] = d_tokens_in[...]
    up_own, down_own = up_blocks(up_sums, core, (col // 8) % 2)
    up_own, down_own = up_own * scaling, down_own * scaling
    up_turned, down_turned = up_own.T, down_own.T
    new_left_up[0] = left_up[0] + exact(up_own, up_turned) / 192
    new_right_up[0] = right_up[0] + exact(up_turned, up_own) / 96
    new_left_down[0] = left_down[0] + exact(down_turned, down_own) / 96
    new_right_down[0] = right_down[0] + exact(down_own, down_turned) / 192
    qkv_own = qkv_block(qkv_sums) * scaling
    qkv_turned = qkv_own.T
    new_left_qkv[0] = left_qkv[0] + exact(qkv_own, qkv_turned) / 144
    new_right_qkv[0] = right_qkv[0] + exact(qkv_turned, qkv_own) / 96


def exchange(source, target, sems, device):
    return pltpu.make_async_remote_copy(
        src_ref=source,
        dst_ref=target,
        send_sem=sems[0],
        recv_sem=sems[1],
        device_id=device,
        device_id_type=MESH,
    )


def gain_row(gain):
    return gain[...].reshape(1, MODEL)


def diagonal(first, second):
    return jnp.concatenate(
        [
            jnp.concatenate([first, jnp.zeros_like(second)], axis=1),
            jnp.concatenate([jnp.zeros_like(first), second], axis=1),
        ],
        axis=0,
    )


def whole_kernel(*refs):
    refs = list(refs)

    def take(count):
        taken = refs[:count]
        del refs[:count]
        return taken

    tokens, cotangent, gain_attn, gain_mlp, sides, corners, sides_t, corners_t = take(8)
    weight_refs = take(4)
    mixed, d_tokens, up_sums, qkv_sums = take(4)
    w_qkv, w_out, w_up, w_down = take(4)
    near, packed, kv, query, query_t, chances, hidden, attended_t = take(8)
    d_attended, d_attended_t, d_norm_own, d_side_in, d_band_in = take(5)
    d_far, d_band = near, packed
    a1t, a2t, a3t, d_up, activated, d_qkv_t = take(6)
    ubuf, ubox, ucube, qbuf, qbox, qmesh, rbuf, rbox, rmesh = take(9)
    total_up, other_up = take(2)
    weight_sems, halo_send, halo_recv, back_send, back_recv = take(5)
    up_sems, qkv_sems, rest_sems = take(5), take(5), take(5)
    last_sems = take(2)

    row, col = lax.axis_index("rows"), lax.axis_index("cols")
    rows, cols = lax.axis_size("rows"), lax.axis_size("cols")
    above, below = ((row + rows - 1) % rows, col), ((row + 1) % rows, col)
    to_left, to_right = (row, (col + cols - 1) % cols), (row, (col + 1) % cols)
    x, y, z, core = my_place()
    sibling = device_at(x, y, z, 1 - core)
    partners = link_partners(x, y, z, core)
    slots = Slots(link_bits(x, y, z))
    barrier = pltpu.get_barrier_semaphore()
    cubes = [
        [cube_place(flow, slot, x, y, z, core) for slot in range(8)] for flow in range(FLOWS)
    ]
    corners_of_cubes = tuple(cubes[flow][slot] for flow in (0, 3) for slot in (3, 5, 6, 7))
    for place in (above, below, to_left, to_right, sibling) + partners + corners_of_cubes:
        pl.semaphore_signal(barrier, inc=1, device_id=place, device_id_type=MESH)
    loads = [
        pltpu.make_async_copy(weight_refs[at], place, weight_sems.at[at])
        for at, place in ((0, w_qkv), (1, w_out), (3, w_down), (2, w_up))
    ]
    loads[0].start()

    def copies(routes, first_sem, send, recv):
        return [
            pltpu.make_async_remote_copy(
                src_ref=source,
                dst_ref=target,
                send_sem=send.at[first_sem + at],
                recv_sem=recv.at[first_sem + at],
                device_id=device,
                device_id_type=MESH,
            )
            for at, (source, target, device) in enumerate(routes)
        ]

    def part(ref, first, count):
        return ref.at[pl.ds(first, count)]

    packed[:192] = dot(sides[...], tokens[...]).astype(jnp.bfloat16)
    pl.semaphore_wait(barrier, 19)
    near_copies = copies(
        (
            (part(tokens, 0, 96), part(near, BOTTOM, 96), above),
            (part(tokens, TOKENS - 96, 96), part(near, TOP, 96), below),
            (part(packed, 0, 96), part(near, RIGHT, 96), to_left),
            (part(packed, 96, 96), part(near, LEFT, 96), to_right),
        ),
        0,
        halo_send,
        halo_recv,
    )
    for copy in near_copies:
        copy.start()
    corner_copies = copies(
        (
            (part(packed, 192, 48), part(near, TOP_CORNERS + 48, 48), to_left),
            (part(packed, 240, 48), part(near, LOW_CORNERS + 48, 48), to_left),
            (part(packed, 288, 48), part(near, TOP_CORNERS, 48), to_right),
            (part(packed, 336, 48), part(near, LOW_CORNERS, 48), to_right),
        ),
        4,
        halo_send,
        halo_recv,
    )

    wide = tokens[...].astype(jnp.float32)
    normed_attn = (wide * inverse_rms(wide) * gain_row(gain_attn)).astype(jnp.bfloat16)
    near[OWN:LOW_CORNERS] = normed_attn
    a3t[...] = cotangent[...].T
    key_row, key_col = key_places()
    key_row, key_col = row * TILE + key_row, col * TILE + key_col
    for half in range(2):
        at = lax.broadcasted_iota(jnp.int32, (1, 128), 1) + 128 * half
        row_first = jnp.clip(row * TILE + at // TILE - window_half, 0, rows * TILE - window_span)
        col_first = jnp.clip(col * TILE + at % TILE - window_half, 0, cols * TILE - window_span)
        spot_row = key_row[LATER * half : LATER * half + SPAN]
        spot_col = key_col[LATER * half : LATER * half + SPAN]
        visible = (
            (spot_row >= row_first)
            & (spot_row < row_first + window_span)
            & (spot_col >= col_first)
            & (spot_col < col_first + window_span)
        )
        hidden[half] = jnp.where(visible, 0.0, -1e30).astype(jnp.bfloat16)

    loads[0].wait()
    for load in loads[1:]:
        load.start()
    own_query = dot(normed_attn, w_qkv[:, :MODEL]).astype(jnp.bfloat16)
    own_query = (own_query.astype(jnp.float32) * 0.125).astype(jnp.bfloat16)
    query[...] = own_query
    query_t[...] = own_query.T
    kv[OWN:LOW_CORNERS] = dot(normed_attn, w_qkv[:, MODEL:]).astype(jnp.bfloat16)
    a1t[:, OWN:LOW_CORNERS] = normed_attn.T

    for copy in near_copies[:2]:
        copy.wait_recv()
    packed[192:384] = (
        dot(corners[:, :96], near[TOP:TOP_CORNERS]) + dot(corners[:, 96:], near[BOTTOM:KEYS])
    ).astype(jnp.bfloat16)
    for copy in corner_copies:
        copy.start()
    for copy in near_copies[2:] + corner_copies:
        copy.wait_recv()
    for first, last in ((TOP, OWN), (LOW_CORNERS, KEYS)):
        halo = near[first:last].astype(jnp.float32)
        halo = (halo * inverse_rms(halo) * gain_row(gain_attn)).astype(jnp.bfloat16)
        near[first:last] = halo
        kv[first:last] = dot(halo, w_qkv[:, MODEL:]).astype(jnp.bfloat16)
        a1t[:, first:last] = halo.T

    def spans(half):
        return pl.ds(LATER * half, SPAN)

    def attend(pair, carry):
        lanes = pl.ds(pl.multiple_of(pair * 128, 128), 128)
        value_lanes = pl.ds(pl.multiple_of(MODEL + pair * 128, 128), 128)
        queries = query_t[lanes, :]
        for half in range(2):
            columns = slice(128 * half, 128 * half + 128)
            both = diagonal(queries[:64, columns], queries[64:, columns])
            bias = hidden[half].astype(jnp.float32)
            bias = jnp.concatenate([bias, bias], axis=1)
            scores = dot(kv[spans(half), lanes], both) + bias
            most = jnp.max(scores, axis=0, keepdims=True)
            powers = jnp.exp(scores - most)
            total = jnp.sum(powers, axis=0, keepdims=True)
            weights = (powers * (1.0 / total)).astype(jnp.bfloat16)
            chances[pair, half] = weights
            blended = dot(kv[spans(half), value_lanes].T, weights).astype(jnp.bfloat16)
            attended_t[lanes, columns] = jnp.concatenate(
                [blended[:64, :128], blended[64:, 128:]], axis=0
            )
        return carry

    lax.fori_loop(0, PAIRS, attend, 0)

    for load in loads[1:]:
        load.wait()
    wide = tokens[...].astype(jnp.float32)
    residual = (wide + dot(attended_t[...].T, w_out[...])).astype(jnp.bfloat16)
    residual_wide = residual.astype(jnp.float32)
    scale_mlp = inverse_rms(residual_wide)
    normed_mlp = (residual_wide * scale_mlp * gain_row(gain_mlp)).astype(jnp.bfloat16)
    a2t[...] = normed_mlp.T
    mix = residual_wide
    d_normed = jnp.zeros((TOKENS, MODEL), jnp.float32)
    slope = float(np.sqrt(2 / np.pi))
    for step in range(6):
        units = slice(512 * step, 512 * step + 512)
        up = dot(normed_mlp, w_up[:, units])
        d_act = dot_nt(cotangent[...], w_down[units])
        square = up * up
        tanh = jnp.tanh(slope * up * (1.0 + 0.044715 * square))
        grown = 0.5 * (1.0 + tanh)
        active = (up * grown).astype(jnp.bfloat16)
        activated[:, units] = active
        mix = mix + dot(active, w_down[units])
        steep = grown + 0.5 * up * (1.0 - tanh * tanh) * (
            slope * (1.0 + 3 * 0.044715 * square)
        )
        d_up_part = (d_act * steep).astype(jnp.bfloat16)
        d_up[:, units] = d_up_part
        d_normed = d_normed + dot_nt(d_up_part, w_up[:, units])
    mixed[...] = mix.astype(jnp.bfloat16)

    up_channels = [
        Channel(ubuf, ubox, ubox, ucube, up_sems, flow, flow, 48 * flow) for flow in range(FLOWS)
    ]
    early, late = up_channels[3:], up_channels[:3]
    qkv_channels = [
        Channel(qbuf, qbox, qmesh, qmesh, qkv_sems, flow, flow, 16 * flow) for flow in range(FLOWS)
    ] + [Channel(rbuf, rbox, rmesh, rmesh, rest_sems, 0, 0, 96)]

    def loop(count, body):
        def turn(at, carry):
            body(at)
            return carry

        lax.fori_loop(0, count, turn, 0)

    loop(8, lambda group: down_payload(group, slots, core, a3t, activated, ubuf))
    for channel in early:
        channel.core_copy(sibling).start()
    loop(8, lambda c: up_payload(c, slots, core, a2t, d_up, ubuf))
    for channel in late:
        channel.core_copy(sibling).start()

    d_residual = (
        cotangent[...].astype(jnp.float32)
        + norm_back(residual_wide, scale_mlp, gain_row(gain_mlp), d_normed)
    ).astype(jnp.bfloat16)
    d_tokens[...] = d_residual
    d_att = dot_nt(d_residual, w_out[...]).astype(jnp.bfloat16)
    d_attended[...] = d_att
    d_attended_t[...] = d_att.T
    d_qkv_t[:MODEL, :OWN] = jnp.zeros((MODEL, OWN), jnp.bfloat16)
    d_qkv_t[:MODEL, LOW_CORNERS:] = jnp.zeros((MODEL, KEYS - LOW_CORNERS), jnp.bfloat16)

    masks = lane_masks()

    def attend_back(pair):
        lanes = pl.ds(pl.multiple_of(pair * 128, 128), 128)
        key_lanes = pl.ds(pl.multiple_of(MODEL + pair * 128, 128), 128)
        value_lanes = pl.ds(pl.multiple_of(2 * MODEL + pair * 128, 128), 128)
        upstream_t = d_attended_t[lanes, :]
        products = upstream_t.astype(jnp.float32) * attended_t[lanes, :].astype(jnp.float32)
        deltas = [
            jnp.sum(products[64 * second : 64 * second + 64], axis=0, keepdims=True)
            for second in range(2)
        ]
        d_keys, d_values, d_query = [], [], []
        for half in range(2):
            columns = slice(128 * half, 128 * half + 128)
            weights = chances[pair, half]
            both = diagonal(upstream_t[:64, columns], upstream_t[64:, columns])
            delta = jnp.concatenate([delta[:, columns] for delta in deltas], axis=1)
            d_prob = dot(kv[spans(half), key_lanes], both)
            d_score = (weights.astype(jnp.float32) * (d_prob - delta)).astype(jnp.bfloat16)
            crossed = dot(kv[spans(half), lanes].T, d_score)
            d_query.append(jnp.concatenate([crossed[:64, :128], crossed[64:, 128:]], axis=0))
            asked = query[columns, lanes]
            d_keys.append(
                dot(d_score, jnp.concatenate([asked * masks[0], asked * masks[1]], axis=0))
            )
            sought = d_attended[columns, lanes]
            d_values.append(
                dot(weights, jnp.concatenate([sought * masks[0], sought * masks[1]], axis=0))
            )
        d_qkv_t[lanes, OWN:LOW_CORNERS] = (
            jnp.concatenate(d_query, axis=1) * 0.125
        ).astype(jnp.bfloat16)
        for place, (one, two) in ((key_lanes, d_keys), (value_lanes, d_values)):
            summed = jnp.concatenate(
                [one[:LATER], one[LATER:] + two[: SPAN - LATER], two[SPAN - LATER :]], axis=0
            )
            d_qkv_t[place, :] = summed.astype(jnp.bfloat16).T

    def after_core(channels):
        for channel in channels:
            channel.after_core(partners, sibling)
        for channel in channels:
            channel.send_mesh(0, partners)

    def after_mesh(channels, step):
        for channel in channels:
            channel.after_mesh(step, partners, cubes)

    def after_cube(channels, total):
        for channel in channels:
            channel.after_cube(sibling, total)

    after_core(early)
    loop(2, attend_back)
    after_core(late)
    loop(4, lambda pair: attend_back(pair + 2))
    after_mesh(early, 0)

    loop(8, lambda c: qkv_payload(c, slots, core, a1t, d_qkv_t, qbuf))
    rest_payload(slots, core, a1t, d_qkv_t, rbuf)
    for channel in qkv_channels:
        channel.core_copy(sibling).start()
    after_mesh(late, 0)
    after_mesh(early, 1)

    for step in range(3):
        lines = slice(256 * step, 256 * step + 256)
        piece = dot(w_qkv[lines, :], d_qkv_t[...]).T
        d_norm_own[:, lines] = piece[OWN:LOW_CORNERS]
        for target, first, count in (
            (0, TOP, 96),
            (96, BOTTOM, 96),
            (192, LEFT, 96),
            (288, TOP_CORNERS, 48),
            (336, LOW_CORNERS, 48),
            (384, RIGHT, 96),
            (480, TOP_CORNERS + 48, 48),
            (528, LOW_CORNERS + 48, 48),
        ):
            d_far[target : target + count, lines] = piece[first : first + count].astype(
                jnp.bfloat16
            )
    side_copies = copies(
        (
            (part(d_far, 192, 192), part(d_side_in, 192, 192), to_left),
            (part(d_far, 384, 192), part(d_side_in, 0, 192), to_right),
        ),
        0,
        back_send,
        back_recv,
    )
    band_copies = copies(
        (
            (part(d_band, 0, 96), part(d_band_in, 96, 96), above),
            (part(d_band, 96, 96), part(d_band_in, 0, 96), below),
        ),
        2,
        back_send,
        back_recv,
    )
    for copy in side_copies:
        copy.start()

    after_core(qkv_channels)
    after_mesh(late, 1)
    after_mesh(early, 2)

    for copy in side_copies:
        copy.wait_recv()
    own = jnp.concatenate([d_side_in[0:96], d_side_in[192:288]], axis=0)
    far = jnp.concatenate([d_side_in[96:192], d_side_in[288:384]], axis=0)
    for copy in near_copies + corner_copies:
        copy.wait_send()
    d_band[0:192] = (d_far[0:192].astype(jnp.float32) + dot(corners_t[...], far)).astype(
        jnp.bfloat16
    )
    for copy in band_copies:
        copy.start()
    d_norm_own[...] = d_norm_own[...] + dot(sides_t[...], own)

    after_mesh(qkv_channels, 0)
    after_mesh(late, 2)
    after_mesh(qkv_channels, 1)
    after_cube(early, total_up)
    after_mesh(qkv_channels, 2)
    after_cube(late, total_up)
    up_last = exchange(total_up, other_up, last_sems[0:2], sibling)
    up_last.start()

    for copy in band_copies:
        copy.wait_recv()
    band = d_band_in[...].astype(jnp.float32)
    summed = d_norm_own[...]
    d_normed = jnp.concatenate(
        [summed[:96] + band[:96], summed[96:160], summed[160:] + band[96:]], axis=0
    )
    wide = tokens[...].astype(jnp.float32)
    d_tokens[...] = (
        d_tokens[...].astype(jnp.float32)
        + norm_back(wide, inverse_rms(wide), gain_row(gain_attn), d_normed)
    ).astype(jnp.bfloat16)

    after_cube(qkv_channels, qkv_sums)
    first = core == 0
    up_last.wait_recv()
    up_sums[0] = jnp.where(first, total_up[...], other_up[...])
    up_sums[1] = jnp.where(first, other_up[...], total_up[...])

    for channel in up_channels + qkv_channels:
        channel.finish(partners, sibling)
    for copy in side_copies + band_copies + [up_last]:
        copy.wait_send()


def on_device(
    tokens,
    cotangent,
    gain_attn,
    gain_mlp,
    weight_qkv,
    weight_out,
    weight_up,
    weight_down,
    *stats,
):
    scaling = float(TOKENS * lax.axis_size("rows") * lax.axis_size("cols")) ** (-0.5)
    sides, corners = halo_tables()
    bf16, f32 = jnp.bfloat16, jnp.float32

    def vmem(kind, *shape):
        return pltpu.VMEM(shape, kind)

    def boxes(count, size):
        return [vmem(bf16, 2, count, CHIPS, size, 128), vmem(bf16, count, CHIPS, size, 128)]

    def sems_of(count):
        return [
            pltpu.SemaphoreType.DMA((count,)),
            pltpu.SemaphoreType.DMA((count,)),
            pltpu.SemaphoreType.DMA((count, 4)),
            pltpu.SemaphoreType.DMA((count, 4)),
            pltpu.SemaphoreType.REGULAR((count, 3)),
        ]

    in_vmem = pl.BlockSpec(memory_space=pltpu.VMEM)
    tile = jax.ShapeDtypeStruct((TOKENS, MODEL), bf16)
    mixed, d_tokens, up_sums, qkv_sums = pl.pallas_call(
        whole_kernel,
        out_shape=[
            tile,
            tile,
            jax.ShapeDtypeStruct((2, 288, 128), f32),
            jax.ShapeDtypeStruct((112, 128), f32),
        ],
        in_specs=[in_vmem] * 8 + [pl.BlockSpec(memory_space=pl.ANY)] * 4,
        out_specs=[in_vmem] * 4,
        scratch_shapes=[
            vmem(bf16, MODEL, 3 * MODEL),
            vmem(bf16, MODEL, MODEL),
            vmem(bf16, MODEL, HIDDEN),
            vmem(bf16, HIDDEN, MODEL),
            vmem(bf16, KEYS, MODEL),
            vmem(bf16, 384, MODEL),
            vmem(bf16, KEYS, 2 * MODEL),
            vmem(bf16, TOKENS, MODEL),
            vmem(bf16, MODEL, TOKENS),
            vmem(bf16, PAIRS, 2, SPAN, 256),
            vmem(bf16, 2, SPAN, 128),
            vmem(bf16, MODEL, TOKENS),
            vmem(bf16, TOKENS, MODEL),
            vmem(bf16, MODEL, TOKENS),
            vmem(f32, TOKENS, MODEL),
            vmem(bf16, 384, MODEL),
            vmem(bf16, 192, MODEL),
            vmem(bf16, MODEL, KEYS),
            vmem(bf16, MODEL, TOKENS),
            vmem(bf16, MODEL, TOKENS),
            vmem(bf16, TOKENS, HIDDEN),
            vmem(bf16, TOKENS, HIDDEN),
            vmem(bf16, 3 * MODEL, KEYS),
        ]
        + boxes(6, 48)
        + [vmem(bf16, 6, 8, 48, 128)]
        + boxes(6, 16)
        + [vmem(bf16, 6, CHIPS, 16, 128)]
        + boxes(1, 16)
        + [vmem(bf16, 1, CHIPS, 16, 128)]
        + [vmem(f32, 288, 128), vmem(f32, 288, 128)]
        + [
            pltpu.SemaphoreType.DMA((4,)),
            pltpu.SemaphoreType.DMA((8,)),
            pltpu.SemaphoreType.DMA((8,)),
            pltpu.SemaphoreType.DMA((4,)),
            pltpu.SemaphoreType.DMA((4,)),
        ]
        + sems_of(6)
        + sems_of(6)
        + sems_of(1)
        + [pltpu.SemaphoreType.DMA] * 2,
        compiler_params=pltpu.CompilerParams(
            collective_id=0, has_side_effects=True, vmem_limit_bytes=63 * 2**20 + 2**19
        ),
    )(
        tokens.reshape(TOKENS, MODEL),
        cotangent.reshape(TOKENS, MODEL),
        gain_attn,
        gain_mlp,
        jnp.asarray(sides, bf16),
        jnp.asarray(corners, bf16),
        jnp.asarray(sides.T, bf16),
        jnp.asarray(corners.T, bf16),
        weight_qkv,
        weight_out,
        weight_up,
        weight_down,
    )
    mixed, d_tokens, *new_stats = pl.pallas_call(
        functools.partial(stats_kernel, scaling),
        out_shape=[tile, tile] + [jax.ShapeDtypeStruct(stat.shape, f32) for stat in stats],
        in_specs=[in_vmem] * 10,
        out_specs=[in_vmem] * 8,
        compiler_params=pltpu.CompilerParams(vmem_limit_bytes=62 * 2**20 + 2**19),
    )(mixed, d_tokens, up_sums, qkv_sums, *stats)
    return (
        mixed.reshape(TILE, TILE, MODEL),
        d_tokens.reshape(TILE, TILE, MODEL),
        *new_stats,
    )


def solution(mesh):
    in_specs = (
        P("rows", "cols", None),
        P("rows", "cols", None),
        P(),
        P(),
        P(),
        P(),
        P(),
        P(),
        P(("rows", "cols"), None, None),
        P(("rows", "cols"), None, None),
        P(("rows", "cols"), None, None),
        P(("rows", "cols"), None, None),
        P(("rows", "cols"), None, None),
        P(("rows", "cols"), None, None),
    )
    out_specs = (
        P("rows", "cols", None),
        P("rows", "cols", None),
        P(("rows", "cols"), None, None),
        P(("rows", "cols"), None, None),
        P(("rows", "cols"), None, None),
        P(("rows", "cols"), None, None),
        P(("rows", "cols"), None, None),
        P(("rows", "cols"), None, None),
    )
    return jax.shard_map(
        on_device, mesh=mesh, in_specs=in_specs, out_specs=out_specs, check_vma=False
    )
```

```python
import functools

import jax
import jax.numpy as jnp
import numpy as np
from jax import lax
from jax.experimental import pallas as pl
from jax.experimental.pallas import tpu as pltpu
from jax.sharding import PartitionSpec as P

HEADS = 12
PAIRS = 6
MODEL = 768
HIDDEN = 3072
TILE = 16
TOKENS = TILE * TILE
FLOWS = 6
CHIPS = 64
TOP, TOP_CORNERS, LEFT, RIGHT, OWN, LOW_CORNERS, BOTTOM, KEYS = 0, 96, 192, 288, 384, 640, 736, 832
SPAN = 640
LATER = KEYS - SPAN

epsilon = 1e-06
window_half = 6
window_span = 13
MESH = pl.DeviceIdType.MESH


def halo_tables():
    sides = np.zeros((192, TOKENS), np.float32)
    corners = np.zeros((192, 192), np.float32)
    for side, first in enumerate((0, TILE - 6)):
        for r in range(TILE):
            for c in range(6):
                sides[96 * side + r * 6 + c, r * TILE + first + c] = 1
        for band in range(2):
            for r in range(6):
                for c in range(6):
                    at = 48 * band + r * 6 + c
                    corners[96 * side + at, 96 * band + r * TILE + first + c] = 1
    return sides, corners


def key_places():
    key = lax.broadcasted_iota(jnp.int32, (KEYS, 1), 0)
    in_band = (key < TOP_CORNERS) | (key >= BOTTOM) | ((key >= OWN) & (key < LOW_CORNERS))
    band = key - jnp.where(key < TOP_CORNERS, TOP, jnp.where(key >= BOTTOM, BOTTOM, OWN))
    shift = jnp.where(key < TOP_CORNERS, -6, jnp.where(key >= BOTTOM, TILE, 0))
    band_row, band_col = band // TILE + shift, band % TILE
    low = key >= LOW_CORNERS
    in_corner = (key < LEFT) | low
    corner = key - jnp.where(low, LOW_CORNERS, TOP_CORNERS)
    on_right = jnp.where(in_corner, corner, key - LEFT - 48) >= 48
    at = jnp.where(
        in_corner, corner - jnp.where(on_right, 48, 0), key - jnp.where(key >= RIGHT, RIGHT, LEFT)
    )
    sixth = (at * 171) >> 10
    side_row = sixth + jnp.where(in_corner, jnp.where(low, TILE, -6), 0)
    side_col = at - 6 * sixth + jnp.where(on_right, TILE, -6)
    unused = in_corner & (at >= 36)
    key_row = jnp.where(in_band, band_row, jnp.where(unused, -1000, side_row))
    return key_row, jnp.where(in_band, band_col, side_col)


def dot(left, right):
    return jnp.dot(left, right, preferred_element_type=jnp.float32)


def dot_nt(left, right):
    return lax.dot_general(
        left, right, (((1,), (1,)), ((), ())), preferred_element_type=jnp.float32
    )


def inverse_rms(wide):
    return lax.rsqrt(jnp.mean(wide * wide, axis=-1, keepdims=True) + epsilon)


def norm_back(wide, scale, gain, upstream):
    scaled = upstream * gain
    return scale * scaled - wide * (
        scale * scale * scale * jnp.mean(wide * scaled, axis=-1, keepdims=True)
    )


def lane_masks():
    lane = lax.broadcasted_iota(jnp.int32, (1, 128), 1)
    low = jnp.where(lane < 64, 1.0, 0.0)
    return low.astype(jnp.bfloat16), (1.0 - low).astype(jnp.bfloat16)


def gray_bits(position):
    high = position // 2
    return (high, (high + position % 2) % 2)


def my_place():
    row = lax.axis_index("rows")
    col = lax.axis_index("cols")
    core = col % 2
    x = col // 4
    y = (row // 4) * 2 + (col // 2) % 2
    z = row % 4
    return x, y, z, core


def device_at(x, y, z, core):
    return ((y // 2) * 4 + z, x * 4 + (y % 2) * 2 + core)


def link_bits(x, y, z):
    gx, gy, gz = gray_bits(x), gray_bits(y), gray_bits(z)
    return (gx[1], gy[1], gz[1], gx[0], gy[0], gz[0])


def link_partners(x, y, z, core):
    return (
        device_at(x + 1 - 2 * (x % 2), y, z, core),
        device_at(x, y + 1 - 2 * (y % 2), z, core),
        device_at(x, y, z + 1 - 2 * (z % 2), core),
        device_at(3 - x, y, z, core),
        device_at(x, 3 - y, z, core),
        device_at(x, y, 3 - z, core),
    )


def link_of(flow, step):
    return (flow + step) % 3 + 3 * ((flow // 3 + step // 3) % 2)


def slot_terms(mine, theirs, axis):
    near = (mine[axis] + theirs[1]) % 2
    far = (mine[axis + 3] + theirs[0]) % 2
    terms = []
    for flow in range(FLOWS):
        weight = {link_of(flow, step): 32 >> step for step in range(6)}
        terms.append(near * weight[axis] + far * weight[axis + 3])
    return terms


def cube_place(flow, slot, x, y, z, core):
    places = [x, y, z]
    for step in range(3):
        if (slot >> (2 - step)) & 1:
            link = link_of(flow, 3 + step)
            at = places[link % 3]
            places[link % 3] = 3 - at if link >= 3 else at + 1 - 2 * (at % 2)
    return device_at(places[0], places[1], places[2], core)


class Slots:
    def __init__(self, mine):
        self.mine = mine

    def terms(self, axis, position):
        return slot_terms(self.mine, gray_bits(position), axis)

    def table(self, xs, y_los, y_his, zs):
        along_x = {at: self.terms(0, x) for at, x in enumerate(xs)}
        along_y = {
            (i, j): self.terms(1, y_hi * 2 + y_lo)
            for i, y_hi in enumerate(y_his)
            for j, y_lo in enumerate(y_los)
        }
        along_z = {at: self.terms(2, z) for at, z in enumerate(zs)}
        return lambda x, y_lo, y_hi, z, flow: (
            along_x[x][flow] + along_y[y_hi, y_lo][flow] + along_z[z][flow]
        )

    def of_group(self, group):
        slot = self.table(range(4), range(2), [group // 4], [group % 4])
        return lambda c, flow: slot(c // 2, c % 2, 0, 0, flow)

    def of_column(self, c):
        slot = self.table([c // 2], [c % 2], range(2), range(4))
        return lambda group, flow: slot(0, 0, group // 4, group % 4, flow)


class Channel:
    def __init__(self, own, inbox, mesh_in, cube_in, sems, index, flow, total_at):
        self.own, self.inbox, self.mesh_in, self.cube_in = own, inbox, mesh_in, cube_in
        self.core_send, self.core_recv, self.mesh_send, self.mesh_recv, self.credit = sems
        self.index, self.flow, self.total_at = index, flow, total_at

    def core_copy(self, sibling):
        return pltpu.make_async_remote_copy(
            src_ref=self.own.at[1, self.index],
            dst_ref=self.inbox.at[self.index],
            send_sem=self.core_send.at[self.index],
            recv_sem=self.core_recv.at[self.index],
            device_id=sibling,
            device_id_type=MESH,
        )

    def mesh_copy(self, step, partners):
        count = 32 >> step
        return pltpu.make_async_remote_copy(
            src_ref=self.own.at[0, self.index, pl.ds(count, count)],
            dst_ref=self.mesh_in.at[self.index, pl.ds(count, count)],
            send_sem=self.mesh_send.at[self.index, step],
            recv_sem=self.mesh_recv.at[self.index, step],
            device_id=partners[link_of(self.flow, step)],
            device_id_type=MESH,
        )

    def cube_copy(self, slot, count, place):
        return pltpu.make_async_remote_copy(
            src_ref=self.own.at[0, self.index, pl.ds(slot, count)],
            dst_ref=self.cube_in.at[self.index, pl.ds(slot, count)],
            send_sem=self.mesh_send.at[self.index, 3],
            recv_sem=self.mesh_recv.at[self.index, 3],
            device_id=place,
            device_id_type=MESH,
        )

    def add(self, inbox, source_first, first, count):
        own, index = self.own, self.index
        rows = own.shape[3]
        chunk = min(count, max(1, 128 // rows))

        def body(turn, carry):
            at = first + turn * chunk
            own[0, index, pl.ds(at, chunk)] = (
                own[0, index, pl.ds(at, chunk)]
                + inbox[index, pl.ds(source_first + turn * chunk, chunk)]
            )
            return carry

        lax.fori_loop(0, count // chunk, body, 0)

    def after_core(self, partners, sibling):
        self.core_copy(sibling).wait_recv()
        self.add(self.inbox, 0, 0, 64)
        if self.mesh_in is not self.inbox:
            return
        for step in range(3):
            pl.semaphore_signal(
                self.credit.at[self.index, step],
                inc=1,
                device_id=partners[link_of(self.flow, step)],
                device_id_type=MESH,
            )

    def send_mesh(self, step, partners):
        if self.mesh_in is self.inbox:
            pl.semaphore_wait(self.credit.at[self.index, step], 1)
        self.mesh_copy(step, partners).start()

    def after_mesh(self, step, partners, cubes):
        self.mesh_copy(step, partners).wait_recv()
        count = 32 >> step
        half = count // 2
        if step < 2:
            self.add(self.mesh_in, count + half, half, half)
            self.send_mesh(step + 1, partners)
            self.add(self.mesh_in, count, 0, half)
        else:
            self.add(self.mesh_in, count, 0, count)
            for slot in range(1, 8):
                self.cube_copy(slot, 1, cubes[self.flow][slot]).start()

    def after_cube(self, sibling, total):
        self.cube_copy(1, 7, sibling).wait_recv()
        summed = self.own[0, self.index, 0].astype(jnp.float32)
        for slot in range(1, 8):
            summed = summed + self.cube_in[self.index, slot].astype(jnp.float32)
        total[pl.ds(self.total_at, self.own.shape[3])] = summed

    def finish(self, partners, sibling):
        self.core_copy(sibling).wait_send()
        for step in range(3):
            self.mesh_copy(step, partners).wait_send()
        self.cube_copy(1, 7, sibling).wait_send()


def put(box, core, flow, slot, piece):
    rows = piece.shape[0] // 2
    for half in range(2):
        box[(core + half) % 2, flow, slot] = piece[rows * half : rows * half + rows]


def down_payload(group, slots, core, a3t, activated, ubuf):
    slot = slots.of_group(group)
    lane = lax.broadcasted_iota(jnp.int32, (96, 128), 1)
    tiles = dot(a3t[...], activated[:, pl.ds(pl.multiple_of(384 * group, 128), 384)])
    for c in range(8):
        q, odd = c % 4, c // 4
        main = tiles[192 * q : 192 * q + 192, 256 * odd : 256 * odd + 128].astype(jnp.bfloat16)
        first = tiles[192 * q : 192 * q + 96, 128:256]
        second = tiles[192 * q + 96 : 192 * q + 192, 128:256]
        if odd:
            packed = jnp.where(lane < 64, pltpu.roll(first, 64, 1), second)
        else:
            packed = jnp.where(lane < 64, first, pltpu.roll(second, 64, 1))
        put(ubuf, core, 3, slot(c, 3), main[:96])
        put(ubuf, core, 4, slot(c, 4), main[96:])
        put(ubuf, core, 5, slot(c, 5), packed.astype(jnp.bfloat16))


def up_payload(c, slots, core, a2t, d_up, ubuf):
    slot = slots.of_column(c)
    tiles = dot(a2t[...], d_up[:, pl.ds(pl.multiple_of(384 * c, 128), 384)]).astype(jnp.bfloat16)
    for group in range(8):
        for flow in range(3):
            put(
                ubuf,
                core,
                flow,
                slot(group, flow),
                tiles[96 * group : 96 * group + 96, 128 * flow : 128 * flow + 128],
            )


def qkv_payload(c, slots, core, a1t, d_qkv_t, qbuf):
    slot = slots.of_column(c)
    first = pl.multiple_of(288 * c, 32)
    second = pl.multiple_of(288 * c + 144, 16)
    columns = jnp.concatenate(
        [d_qkv_t[pl.ds(first, 128), :], d_qkv_t[pl.ds(second, 128), :]], axis=0
    )
    tiles = dot_nt(a1t[...], columns).astype(jnp.bfloat16)
    for group in range(8):
        for flow in range(FLOWS):
            at = 96 * group + 16 * flow
            for half in range(2):
                qbuf[(core + half) % 2, flow, slot(group, flow)] = tiles[
                    at : at + 16, 128 * half : 128 * half + 128
                ]


def rest_payload(slots, core, a1t, d_qkv_t, rbuf):
    columns = jnp.concatenate(
        [d_qkv_t[144 * block + 128 : 144 * block + 144] for block in range(16)], axis=0
    )
    tiles = dot_nt(a1t[...], columns)
    slot = slots.table(range(4), range(2), range(2), range(4))
    blank = jnp.zeros((256, 32), jnp.bfloat16)
    for group in range(8):
        turned = tiles[96 * group : 96 * group + 96].T.astype(jnp.bfloat16)
        turned = jnp.concatenate([turned, blank], axis=1)
        for c in range(8):
            for half in range(2):
                at = 32 * c + 16 * half
                rbuf[(core + half) % 2, 0, slot(c // 2, c % 2, group // 4, group % 4, 0)] = turned[
                    at : at + 16
                ]


def exact(left, right):
    return jnp.dot(
        left, right, precision=lax.Precision.HIGHEST, preferred_element_type=jnp.float32
    )


def up_blocks(sums, core, part_odd):
    first, odd = core == 0, part_odd == 1
    left, middle, right, main_0, main_1, packed = [
        jnp.concatenate([sums[0, 48 * at : 48 * at + 48], sums[1, 48 * at : 48 * at + 48]], axis=0)
        for at in range(6)
    ]
    up = jnp.where(
        first,
        jnp.concatenate([left, middle], axis=1),
        pltpu.roll(jnp.concatenate([middle, right], axis=1), 192, 1),
    )[:, :192]
    main = jnp.where(first, main_0, main_1)
    turned = pltpu.roll(packed, 64, 1)
    low, high = jnp.where(first, packed, turned), jnp.where(first, turned, packed)
    down = jnp.where(
        odd,
        pltpu.roll(jnp.concatenate([high, main], axis=1), 192, 1),
        jnp.concatenate([main, low], axis=1),
    )[:, :192]
    return up, down


def qkv_block(sums):
    rest = jnp.concatenate([sums[96:112], jnp.zeros((112, 128), jnp.float32)], axis=0).T[:96]
    return jnp.concatenate([sums[0:96], rest], axis=1)[:, :144]


def stats_kernel(
    scaling,
    mixed_in,
    d_tokens_in,
    up_sums,
    qkv_sums,
    left_qkv,
    right_qkv,
    left_up,
    right_up,
    left_down,
    right_down,
    mixed,
    d_tokens,
    new_left_qkv,
    new_right_qkv,
    new_left_up,
    new_right_up,
    new_left_down,
    new_right_down,
):
    col = lax.axis_index("cols")
    core = col % 2
    mixed[...] = mixed_in[...]
    d_tokens[...] = d_tokens_in[...]
    up_own, down_own = up_blocks(up_sums, core, (col // 8) % 2)
    up_own, down_own = up_own * scaling, down_own * scaling
    up_turned, down_turned = up_own.T, down_own.T
    new_left_up[0] = left_up[0] + exact(up_own, up_turned) / 192
    new_right_up[0] = right_up[0] + exact(up_turned, up_own) / 96
    new_left_down[0] = left_down[0] + exact(down_turned, down_own) / 96
    new_right_down[0] = right_down[0] + exact(down_own, down_turned) / 192
    qkv_own = qkv_block(qkv_sums) * scaling
    qkv_turned = qkv_own.T
    new_left_qkv[0] = left_qkv[0] + exact(qkv_own, qkv_turned) / 144
    new_right_qkv[0] = right_qkv[0] + exact(qkv_turned, qkv_own) / 96


def exchange(source, target, sems, device):
    return pltpu.make_async_remote_copy(
        src_ref=source,
        dst_ref=target,
        send_sem=sems[0],
        recv_sem=sems[1],
        device_id=device,
        device_id_type=MESH,
    )


def gain_row(gain):
    return gain[...].reshape(1, MODEL)


def diagonal(first, second):
    return jnp.concatenate(
        [
            jnp.concatenate([first, jnp.zeros_like(second)], axis=1),
            jnp.concatenate([jnp.zeros_like(first), second], axis=1),
        ],
        axis=0,
    )


def whole_kernel(*refs):
    refs = list(refs)

    def take(count):
        taken = refs[:count]
        del refs[:count]
        return taken

    tokens, cotangent, gain_attn, gain_mlp, sides, corners, sides_t, corners_t = take(8)
    weight_refs = take(4)
    mixed, d_tokens, up_sums, qkv_sums = take(4)
    w_qkv, w_out, w_up, w_down = take(4)
    near, packed, kv, query, query_t, chances, hidden, attended_t = take(8)
    d_attended, d_attended_t, d_norm_own, d_side_in, d_band_in = take(5)
    d_far, d_band = near, packed
    a1t, a2t, a3t, d_up, activated, d_qkv_t = take(6)
    ubuf, ubox, ucube, qbuf, qbox, qmesh, rbuf, rbox, rmesh = take(9)
    total_up, other_up = take(2)
    weight_sems, halo_send, halo_recv, back_send, back_recv = take(5)
    up_sems, qkv_sems, rest_sems = take(5), take(5), take(5)
    last_sems = take(2)

    row, col = lax.axis_index("rows"), lax.axis_index("cols")
    rows, cols = lax.axis_size("rows"), lax.axis_size("cols")
    above, below = ((row + rows - 1) % rows, col), ((row + 1) % rows, col)
    to_left, to_right = (row, (col + cols - 1) % cols), (row, (col + 1) % cols)
    x, y, z, core = my_place()
    sibling = device_at(x, y, z, 1 - core)
    partners = link_partners(x, y, z, core)
    slots = Slots(link_bits(x, y, z))
    barrier = pltpu.get_barrier_semaphore()
    cubes = [
        [cube_place(flow, slot, x, y, z, core) for slot in range(8)] for flow in range(FLOWS)
    ]
    corners_of_cubes = tuple(cubes[flow][slot] for flow in (0, 3) for slot in (3, 5, 6, 7))
    for place in (above, below, to_left, to_right, sibling) + partners + corners_of_cubes:
        pl.semaphore_signal(barrier, inc=1, device_id=place, device_id_type=MESH)
    loads = [
        pltpu.make_async_copy(weight_refs[at], place, weight_sems.at[at])
        for at, place in ((0, w_qkv), (1, w_out), (3, w_down), (2, w_up))
    ]
    loads[0].start()

    def copies(routes, first_sem, send, recv):
        return [
            pltpu.make_async_remote_copy(
                src_ref=source,
                dst_ref=target,
                send_sem=send.at[first_sem + at],
                recv_sem=recv.at[first_sem + at],
                device_id=device,
                device_id_type=MESH,
            )
            for at, (source, target, device) in enumerate(routes)
        ]

    def part(ref, first, count):
        return ref.at[pl.ds(first, count)]

    packed[:192] = dot(sides[...], tokens[...]).astype(jnp.bfloat16)
    pl.semaphore_wait(barrier, 19)
    near_copies = copies(
        (
            (part(tokens, 0, 96), part(near, BOTTOM, 96), above),
            (part(tokens, TOKENS - 96, 96), part(near, TOP, 96), below),
            (part(packed, 0, 96), part(near, RIGHT, 96), to_left),
            (part(packed, 96, 96), part(near, LEFT, 96), to_right),
        ),
        0,
        halo_send,
        halo_recv,
    )
    for copy in near_copies:
        copy.start()
    corner_copies = copies(
        (
            (part(packed, 192, 48), part(near, TOP_CORNERS + 48, 48), to_left),
            (part(packed, 240, 48), part(near, LOW_CORNERS + 48, 48), to_left),
            (part(packed, 288, 48), part(near, TOP_CORNERS, 48), to_right),
            (part(packed, 336, 48), part(near, LOW_CORNERS, 48), to_right),
        ),
        4,
        halo_send,
        halo_recv,
    )

    wide = tokens[...].astype(jnp.float32)
    normed_attn = (wide * inverse_rms(wide) * gain_row(gain_attn)).astype(jnp.bfloat16)
    near[OWN:LOW_CORNERS] = normed_attn
    a3t[...] = cotangent[...].T
    key_row, key_col = key_places()
    key_row, key_col = row * TILE + key_row, col * TILE + key_col
    for half in range(2):
        at = lax.broadcasted_iota(jnp.int32, (1, 128), 1) + 128 * half
        row_first = jnp.clip(row * TILE + at // TILE - window_half, 0, rows * TILE - window_span)
        col_first = jnp.clip(col * TILE + at % TILE - window_half, 0, cols * TILE - window_span)
        spot_row = key_row[LATER * half : LATER * half + SPAN]
        spot_col = key_col[LATER * half : LATER * half + SPAN]
        visible = (
            (spot_row >= row_first)
            & (spot_row < row_first + window_span)
            & (spot_col >= col_first)
            & (spot_col < col_first + window_span)
        )
        hidden[half] = jnp.where(visible, 0.0, -1e30).astype(jnp.bfloat16)

    loads[0].wait()
    for load in loads[1:]:
        load.start()
    own_query = dot(normed_attn, w_qkv[:, :MODEL]).astype(jnp.bfloat16)
    own_query = (own_query.astype(jnp.float32) * 0.125).astype(jnp.bfloat16)
    query[...] = own_query
    query_t[...] = own_query.T
    kv[OWN:LOW_CORNERS] = dot(normed_attn, w_qkv[:, MODEL:]).astype(jnp.bfloat16)
    a1t[:, OWN:LOW_CORNERS] = normed_attn.T

    for copy in near_copies[:2]:
        copy.wait_recv()
    packed[192:384] = (
        dot(corners[:, :96], near[TOP:TOP_CORNERS]) + dot(corners[:, 96:], near[BOTTOM:KEYS])
    ).astype(jnp.bfloat16)
    for copy in corner_copies:
        copy.start()
    for copy in near_copies[2:] + corner_copies:
        copy.wait_recv()
    for first, last in ((TOP, OWN), (LOW_CORNERS, KEYS)):
        halo = near[first:last].astype(jnp.float32)
        halo = (halo * inverse_rms(halo) * gain_row(gain_attn)).astype(jnp.bfloat16)
        near[first:last] = halo
        kv[first:last] = dot(halo, w_qkv[:, MODEL:]).astype(jnp.bfloat16)
        a1t[:, first:last] = halo.T

    def spans(half):
        return pl.ds(LATER * half, SPAN)

    def attend(pair, carry):
        lanes = pl.ds(pl.multiple_of(pair * 128, 128), 128)
        value_lanes = pl.ds(pl.multiple_of(MODEL + pair * 128, 128), 128)
        queries = query_t[lanes, :]
        for half in range(2):
            columns = slice(128 * half, 128 * half + 128)
            both = diagonal(queries[:64, columns], queries[64:, columns])
            bias = hidden[half].astype(jnp.float32)
            bias = jnp.concatenate([bias, bias], axis=1)
            scores = dot(kv[spans(half), lanes], both) + bias
            most = jnp.max(scores, axis=0, keepdims=True)
            powers = jnp.exp(scores - most)
            total = jnp.sum(powers, axis=0, keepdims=True)
            weights = (powers * (1.0 / total)).astype(jnp.bfloat16)
            chances[pair, half] = weights
            blended = dot(kv[spans(half), value_lanes].T, weights).astype(jnp.bfloat16)
            attended_t[lanes, columns] = jnp.concatenate(
                [blended[:64, :128], blended[64:, 128:]], axis=0
            )
        return carry

    lax.fori_loop(0, PAIRS, attend, 0)

    for load in loads[1:]:
        load.wait()
    wide = tokens[...].astype(jnp.float32)
    residual = (wide + dot(attended_t[...].T, w_out[...])).astype(jnp.bfloat16)
    residual_wide = residual.astype(jnp.float32)
    scale_mlp = inverse_rms(residual_wide)
    normed_mlp = (residual_wide * scale_mlp * gain_row(gain_mlp)).astype(jnp.bfloat16)
    a2t[...] = normed_mlp.T
    mix = residual_wide
    d_normed = jnp.zeros((TOKENS, MODEL), jnp.float32)
    slope = float(np.sqrt(2 / np.pi))
    for step in range(6):
        units = slice(512 * step, 512 * step + 512)
        up = dot(normed_mlp, w_up[:, units])
        d_act = dot_nt(cotangent[...], w_down[units])
        square = up * up
        tanh = jnp.tanh(slope * up * (1.0 + 0.044715 * square))
        grown = 0.5 * (1.0 + tanh)
        active = (up * grown).astype(jnp.bfloat16)
        activated[:, units] = active
        mix = mix + dot(active, w_down[units])
        steep = grown + 0.5 * up * (1.0 - tanh * tanh) * (
            slope * (1.0 + 3 * 0.044715 * square)
        )
        d_up_part = (d_act * steep).astype(jnp.bfloat16)
        d_up[:, units] = d_up_part
        d_normed = d_normed + dot_nt(d_up_part, w_up[:, units])
    mixed[...] = mix.astype(jnp.bfloat16)

    up_channels = [
        Channel(ubuf, ubox, ubox, ucube, up_sems, flow, flow, 48 * flow) for flow in range(FLOWS)
    ]
    early, late = up_channels[3:], up_channels[:3]
    qkv_channels = [
        Channel(qbuf, qbox, qmesh, qmesh, qkv_sems, flow, flow, 16 * flow) for flow in range(FLOWS)
    ] + [Channel(rbuf, rbox, rmesh, rmesh, rest_sems, 0, 0, 96)]

    def loop(count, body):
        def turn(at, carry):
            body(at)
            return carry

        lax.fori_loop(0, count, turn, 0)

    loop(8, lambda group: down_payload(group, slots, core, a3t, activated, ubuf))
    for channel in early:
        channel.core_copy(sibling).start()
    loop(8, lambda c: up_payload(c, slots, core, a2t, d_up, ubuf))
    for channel in late:
        channel.core_copy(sibling).start()

    d_residual = (
        cotangent[...].astype(jnp.float32)
        + norm_back(residual_wide, scale_mlp, gain_row(gain_mlp), d_normed)
    ).astype(jnp.bfloat16)
    d_tokens[...] = d_residual
    d_att = dot_nt(d_residual, w_out[...]).astype(jnp.bfloat16)
    d_attended[...] = d_att
    d_attended_t[...] = d_att.T
    d_qkv_t[:MODEL, :OWN] = jnp.zeros((MODEL, OWN), jnp.bfloat16)
    d_qkv_t[:MODEL, LOW_CORNERS:] = jnp.zeros((MODEL, KEYS - LOW_CORNERS), jnp.bfloat16)

    masks = lane_masks()

    def attend_back(pair):
        lanes = pl.ds(pl.multiple_of(pair * 128, 128), 128)
        key_lanes = pl.ds(pl.multiple_of(MODEL + pair * 128, 128), 128)
        value_lanes = pl.ds(pl.multiple_of(2 * MODEL + pair * 128, 128), 128)
        upstream_t = d_attended_t[lanes, :]
        products = upstream_t.astype(jnp.float32) * attended_t[lanes, :].astype(jnp.float32)
        deltas = [
            jnp.sum(products[64 * second : 64 * second + 64], axis=0, keepdims=True)
            for second in range(2)
        ]
        d_keys, d_values, d_query = [], [], []
        for half in range(2):
            columns = slice(128 * half, 128 * half + 128)
            weights = chances[pair, half]
            both = diagonal(upstream_t[:64, columns], upstream_t[64:, columns])
            delta = jnp.concatenate([delta[:, columns] for delta in deltas], axis=1)
            d_prob = dot(kv[spans(half), key_lanes], both)
            d_score = (weights.astype(jnp.float32) * (d_prob - delta)).astype(jnp.bfloat16)
            crossed = dot(kv[spans(half), lanes].T, d_score)
            d_query.append(jnp.concatenate([crossed[:64, :128], crossed[64:, 128:]], axis=0))
            asked = query[columns, lanes]
            d_keys.append(
                dot(d_score, jnp.concatenate([asked * masks[0], asked * masks[1]], axis=0))
            )
            sought = d_attended[columns, lanes]
            d_values.append(
                dot(weights, jnp.concatenate([sought * masks[0], sought * masks[1]], axis=0))
            )
        d_qkv_t[lanes, OWN:LOW_CORNERS] = (
            jnp.concatenate(d_query, axis=1) * 0.125
        ).astype(jnp.bfloat16)
        for place, (one, two) in ((key_lanes, d_keys), (value_lanes, d_values)):
            summed = jnp.concatenate(
                [one[:LATER], one[LATER:] + two[: SPAN - LATER], two[SPAN - LATER :]], axis=0
            )
            d_qkv_t[place, :] = summed.astype(jnp.bfloat16).T

    def after_core(channels):
        for channel in channels:
            channel.after_core(partners, sibling)
        for channel in channels:
            channel.send_mesh(0, partners)

    def after_mesh(channels, step):
        for channel in channels:
            channel.after_mesh(step, partners, cubes)

    def after_cube(channels, total):
        for channel in channels:
            channel.after_cube(sibling, total)

    after_core(early)
    loop(2, attend_back)
    after_core(late)
    loop(4, lambda pair: attend_back(pair + 2))
    after_mesh(early, 0)

    loop(8, lambda c: qkv_payload(c, slots, core, a1t, d_qkv_t, qbuf))
    rest_payload(slots, core, a1t, d_qkv_t, rbuf)
    for channel in qkv_channels:
        channel.core_copy(sibling).start()
    after_mesh(late, 0)
    after_mesh(early, 1)

    for step in range(3):
        lines = slice(256 * step, 256 * step + 256)
        piece = dot(w_qkv[lines, :], d_qkv_t[...]).T
        d_norm_own[:, lines] = piece[OWN:LOW_CORNERS]
        for target, first, count in (
            (0, TOP, 96),
            (96, BOTTOM, 96),
            (192, LEFT, 96),
            (288, TOP_CORNERS, 48),
            (336, LOW_CORNERS, 48),
            (384, RIGHT, 96),
            (480, TOP_CORNERS + 48, 48),
            (528, LOW_CORNERS + 48, 48),
        ):
            d_far[target : target + count, lines] = piece[first : first + count].astype(
                jnp.bfloat16
            )
    side_copies = copies(
        (
            (part(d_far, 192, 192), part(d_side_in, 192, 192), to_left),
            (part(d_far, 384, 192), part(d_side_in, 0, 192), to_right),
        ),
        0,
        back_send,
        back_recv,
    )
    band_copies = copies(
        (
            (part(d_band, 0, 96), part(d_band_in, 96, 96), above),
            (part(d_band, 96, 96), part(d_band_in, 0, 96), below),
        ),
        2,
        back_send,
        back_recv,
    )
    for copy in side_copies:
        copy.start()

    after_core(qkv_channels)
    after_mesh(late, 1)
    after_mesh(early, 2)

    after_mesh(qkv_channels, 0)
    after_mesh(late, 2)

    for copy in side_copies:
        copy.wait_recv()
    own = jnp.concatenate([d_side_in[0:96], d_side_in[192:288]], axis=0)
    far = jnp.concatenate([d_side_in[96:192], d_side_in[288:384]], axis=0)
    for copy in near_copies + corner_copies:
        copy.wait_send()
    d_band[0:192] = (d_far[0:192].astype(jnp.float32) + dot(corners_t[...], far)).astype(
        jnp.bfloat16
    )
    for copy in band_copies:
        copy.start()
    d_norm_own[...] = d_norm_own[...] + dot(sides_t[...], own)

    after_mesh(qkv_channels, 1)
    after_cube(early, total_up)
    after_mesh(qkv_channels, 2)
    after_cube(late, total_up)
    up_last = exchange(total_up, other_up, last_sems[0:2], sibling)
    up_last.start()

    after_cube(qkv_channels, qkv_sums)

    for copy in band_copies:
        copy.wait_recv()
    band = d_band_in[...].astype(jnp.float32)
    summed = d_norm_own[...]
    d_normed = jnp.concatenate(
        [summed[:96] + band[:96], summed[96:160], summed[160:] + band[96:]], axis=0
    )
    wide = tokens[...].astype(jnp.float32)
    d_tokens[...] = (
        d_tokens[...].astype(jnp.float32)
        + norm_back(wide, inverse_rms(wide), gain_row(gain_attn), d_normed)
    ).astype(jnp.bfloat16)

    first = core == 0
    up_last.wait_recv()
    up_sums[0] = jnp.where(first, total_up[...], other_up[...])
    up_sums[1] = jnp.where(first, other_up[...], total_up[...])

    for channel in up_channels + qkv_channels:
        channel.finish(partners, sibling)
    for copy in side_copies + band_copies + [up_last]:
        copy.wait_send()


def on_device(
    tokens,
    cotangent,
    gain_attn,
    gain_mlp,
    weight_qkv,
    weight_out,
    weight_up,
    weight_down,
    *stats,
):
    scaling = float(TOKENS * lax.axis_size("rows") * lax.axis_size("cols")) ** (-0.5)
    sides, corners = halo_tables()
    bf16, f32 = jnp.bfloat16, jnp.float32

    def vmem(kind, *shape):
        return pltpu.VMEM(shape, kind)

    def boxes(count, size):
        return [vmem(bf16, 2, count, CHIPS, size, 128), vmem(bf16, count, CHIPS, size, 128)]

    def sems_of(count):
        return [
            pltpu.SemaphoreType.DMA((count,)),
            pltpu.SemaphoreType.DMA((count,)),
            pltpu.SemaphoreType.DMA((count, 4)),
            pltpu.SemaphoreType.DMA((count, 4)),
            pltpu.SemaphoreType.REGULAR((count, 3)),
        ]

    in_vmem = pl.BlockSpec(memory_space=pltpu.VMEM)
    tile = jax.ShapeDtypeStruct((TOKENS, MODEL), bf16)
    mixed, d_tokens, up_sums, qkv_sums = pl.pallas_call(
        whole_kernel,
        out_shape=[
            tile,
            tile,
            jax.ShapeDtypeStruct((2, 288, 128), f32),
            jax.ShapeDtypeStruct((112, 128), f32),
        ],
        in_specs=[in_vmem] * 8 + [pl.BlockSpec(memory_space=pl.ANY)] * 4,
        out_specs=[in_vmem] * 4,
        scratch_shapes=[
            vmem(bf16, MODEL, 3 * MODEL),
            vmem(bf16, MODEL, MODEL),
            vmem(bf16, MODEL, HIDDEN),
            vmem(bf16, HIDDEN, MODEL),
            vmem(bf16, KEYS, MODEL),
            vmem(bf16, 384, MODEL),
            vmem(bf16, KEYS, 2 * MODEL),
            vmem(bf16, TOKENS, MODEL),
            vmem(bf16, MODEL, TOKENS),
            vmem(bf16, PAIRS, 2, SPAN, 256),
            vmem(bf16, 2, SPAN, 128),
            vmem(bf16, MODEL, TOKENS),
            vmem(bf16, TOKENS, MODEL),
            vmem(bf16, MODEL, TOKENS),
            vmem(f32, TOKENS, MODEL),
            vmem(bf16, 384, MODEL),
            vmem(bf16, 192, MODEL),
            vmem(bf16, MODEL, KEYS),
            vmem(bf16, MODEL, TOKENS),
            vmem(bf16, MODEL, TOKENS),
            vmem(bf16, TOKENS, HIDDEN),
            vmem(bf16, TOKENS, HIDDEN),
            vmem(bf16, 3 * MODEL, KEYS),
        ]
        + boxes(6, 48)
        + [vmem(bf16, 6, 8, 48, 128)]
        + boxes(6, 16)
        + [vmem(bf16, 6, CHIPS, 16, 128)]
        + boxes(1, 16)
        + [vmem(bf16, 1, CHIPS, 16, 128)]
        + [vmem(f32, 288, 128), vmem(f32, 288, 128)]
        + [
            pltpu.SemaphoreType.DMA((4,)),
            pltpu.SemaphoreType.DMA((8,)),
            pltpu.SemaphoreType.DMA((8,)),
            pltpu.SemaphoreType.DMA((4,)),
            pltpu.SemaphoreType.DMA((4,)),
        ]
        + sems_of(6)
        + sems_of(6)
        + sems_of(1)
        + [pltpu.SemaphoreType.DMA] * 2,
        compiler_params=pltpu.CompilerParams(
            collective_id=0, has_side_effects=True, vmem_limit_bytes=63 * 2**20 + 2**19
        ),
    )(
        tokens.reshape(TOKENS, MODEL),
        cotangent.reshape(TOKENS, MODEL),
        gain_attn,
        gain_mlp,
        jnp.asarray(sides, bf16),
        jnp.asarray(corners, bf16),
        jnp.asarray(sides.T, bf16),
        jnp.asarray(corners.T, bf16),
        weight_qkv,
        weight_out,
        weight_up,
        weight_down,
    )
    mixed, d_tokens, *new_stats = pl.pallas_call(
        functools.partial(stats_kernel, scaling),
        out_shape=[tile, tile] + [jax.ShapeDtypeStruct(stat.shape, f32) for stat in stats],
        in_specs=[in_vmem] * 10,
        out_specs=[in_vmem] * 8,
        compiler_params=pltpu.CompilerParams(vmem_limit_bytes=62 * 2**20 + 2**19),
    )(mixed, d_tokens, up_sums, qkv_sums, *stats)
    return (
        mixed.reshape(TILE, TILE, MODEL),
        d_tokens.reshape(TILE, TILE, MODEL),
        *new_stats,
    )


def solution(mesh):
    in_specs = (
        P("rows", "cols", None),
        P("rows", "cols", None),
        P(),
        P(),
        P(),
        P(),
        P(),
        P(),
        P(("rows", "cols"), None, None),
        P(("rows", "cols"), None, None),
        P(("rows", "cols"), None, None),
        P(("rows", "cols"), None, None),
        P(("rows", "cols"), None, None),
        P(("rows", "cols"), None, None),
    )
    out_specs = (
        P("rows", "cols", None),
        P("rows", "cols", None),
        P(("rows", "cols"), None, None),
        P(("rows", "cols"), None, None),
        P(("rows", "cols"), None, None),
        P(("rows", "cols"), None, None),
        P(("rows", "cols"), None, None),
        P(("rows", "cols"), None, None),
    )
    return jax.shard_map(
        on_device, mesh=mesh, in_specs=in_specs, out_specs=out_specs, check_vma=False
    )
```
